32 devices in a mesh: dp: 8 (over z, x), seq: 4 (over y, core).
Axes of the slice: x: 2, y: 2, z: 4, core: 2. Of those that a mesh axis runs over, the one named last changes fastest.
Arguments:
- block_input: bfloat16 [8, 1024, 1024], P('dp', 'seq'), may hold values from -6 to 6
- output_grad: bfloat16 [8, 1024, 1024], P('dp', 'seq'), may hold values from -9 to 9
- row_lengths: int32 [8], P('dp'), may hold values from 341 to 1024, as said below
- qkv_weight: float32 [2, 1024, 3, 1024], P(None, 'dp', None, 'seq'), may hold values from -0.1875 to 0.1875
- proj_weight: float32 [2, 1024, 1024], P(None, 'seq', 'dp'), may hold values from -0.5 to 0.5
- up_weight: float32 [2, 1024, 4096], P(None, 'dp', 'seq'), may hold values from -0.1875 to 0.1875
- down_weight: float32 [2, 4096, 1024], P(None, 'seq', 'dp'), may hold values from -0.125 to 0.125
- norm_params: float32 [2, 4, 1024], P(None, None, ('dp', 'seq')), may hold values from -2 to 2
- qkv_first: float32 [2, 1024, 3, 1024], P(None, 'dp', None, 'seq'), may hold values from -0.00012207031 to 0.00012207031
- proj_first: float32 [2, 1024, 1024], P(None, 'seq', 'dp'), may hold values from -0.00012207031 to 0.00012207031
- up_first: float32 [2, 1024, 4096], P(None, 'dp', 'seq'), may hold values from -0.00012207031 to 0.00012207031
- down_first: float32 [2, 4096, 1024], P(None, 'seq', 'dp'), may hold values from -0.00012207031 to 0.00012207031
- norm_first: float32 [2, 4, 1024], P(None, None, ('dp', 'seq')), may hold values from -0.00012207031 to 0.00012207031
- qkv_second: float32 [2, 1024, 3, 1024], P(None, 'dp', None, 'seq'), may hold values from 1.3113022e-10 to 5.1657356e-10
- proj_second: float32 [2, 1024, 1024], P(None, 'seq', 'dp'), may hold values from 1.3113022e-10 to 5.1657356e-10
- up_second: float32 [2, 1024, 4096], P(None, 'dp', 'seq'), may hold values from 1.3113022e-10 to 5.1657356e-10
- down_second: float32 [2, 4096, 1024], P(None, 'seq', 'dp'), may hold values from 1.3113022e-10 to 5.1657356e-10
- norm_second: float32 [2, 4, 1024], P(None, None, ('dp', 'seq')), may hold values from 1.3113022e-10 to 5.1657356e-10
Outputs:
- block_output: float32 [8, 1024, 1024], P('dp', 'seq')
- input_grad: float32 [8, 1024, 1024], P('dp', 'seq')
- grad_norm: float32 [], replicated
- qkv_grad: float32 [2, 1024, 3, 1024], P(None, 'dp', None, 'seq')
- proj_grad: float32 [2, 1024, 1024], P(None, 'seq', 'dp')
- up_grad: float32 [2, 1024, 4096], P(None, 'dp', 'seq')
- down_grad: float32 [2, 4096, 1024], P(None, 'seq', 'dp')
- norm_grad: float32 [2, 4, 1024], P(None, None, ('dp', 'seq'))
- qkv_momentum: float32 [2, 1024, 3, 1024], P(None, 'dp', None, 'seq')
- proj_momentum: float32 [2, 1024, 1024], P(None, 'seq', 'dp')
- up_momentum: float32 [2, 1024, 4096], P(None, 'dp', 'seq')
- down_momentum: float32 [2, 4096, 1024], P(None, 'seq', 'dp')
- norm_momentum: float32 [2, 4, 1024], P(None, None, ('dp', 'seq'))
- qkv_variance: float32 [2, 1024, 3, 1024], P(None, 'dp', None, 'seq')
- proj_variance: float32 [2, 1024, 1024], P(None, 'seq', 'dp')
- up_variance: float32 [2, 1024, 4096], P(None, 'dp', 'seq')
- down_variance: float32 [2, 4096, 1024], P(None, 'seq', 'dp')
- norm_variance: float32 [2, 4, 1024], P(None, None, ('dp', 'seq'))
- qkv_new: float32 [2, 1024, 3, 1024], P(None, 'dp', None, 'seq')
- proj_new: float32 [2, 1024, 1024], P(None, 'seq', 'dp')
- up_new: float32 [2, 1024, 4096], P(None, 'dp', 'seq')
- down_new: float32 [2, 4096, 1024], P(None, 'seq', 'dp')
- norm_new: float32 [2, 4, 1024], P(None, None, ('dp', 'seq'))
- qkv_copy: bfloat16 [2, 1024, 3, 1024], P(None, 'dp', None, 'seq')
- proj_copy: bfloat16 [2, 1024, 1024], P(None, 'seq', 'dp')
- up_copy: bfloat16 [2, 1024, 4096], P(None, 'dp', 'seq')
- down_copy: bfloat16 [2, 4096, 1024], P(None, 'seq', 'dp')
- norm_copy: bfloat16 [2, 4, 1024], P(None, None, ('dp', 'seq'))
The draws below stay inside these ranges and needn't reach their ends.
Inputs may be any that keep to these rules, and one draw needn't show every extreme that they name: Slots of row r below row_lengths[r] hold real tokens, the others padding. In every draw one row is 1024 long and one row is 341 long.
All inputs are finite; a program needn't handle non-finite values.
Results may differ from the reference program's by a relative error of at most 0.025.
Values may be sent and summed in bfloat16 or wider, within the bound.
A program may use at most 320 MiB of HBM per device.

```python
import math
import jax
import jax.numpy as jnp
import numpy as np
from jax import lax

D = 1024
H = 8
HD = 128
FF = 4096
LAYERS = 2
STEP = 5
ROWS = 8
SLOTS = 1024


def draw_row_lengths(key, part):
    key_length, key_pick = jax.random.split(key)
    length_draw = jax.random.randint(key_length, (ROWS,), SLOTS // 3, SLOTS + 1, dtype=jnp.int32)
    row_order = jax.random.permutation(key_pick, ROWS)
    length_draw = length_draw.at[row_order[0]].set(SLOTS)
    return length_draw.at[row_order[1]].set(SLOTS // 3)


def draw_norm_params(key, part):
    key_gain, key_bias = jax.random.split(jax.random.fold_in(key, 7))
    gain_rows = (jnp.arange(4) % 2 == 0)[None, :, None]
    column_place = jnp.arange(D, dtype=jnp.float32) / (D - 1.0)
    gain_base = 0.5 * jnp.exp(jnp.log(3.2) * column_place)
    gain_values = gain_base[None, None, :] * jax.random.uniform(key_gain, (LAYERS, 4, D), jnp.float32, 0.8, 1.2)
    bias_values = jnp.clip(0.5 * jax.random.normal(key_bias, (LAYERS, 4, D), jnp.float32), -2.0, 2.0)
    return jnp.where(gain_rows, gain_values, bias_values)


def draw_output_grad(key, part):
    key_values = jax.random.fold_in(key, 11)
    column_place = jnp.arange(D, dtype=jnp.float32) / (D - 1.0)
    column_scale = jnp.exp(jnp.log(8.0) * column_place) / 3.9
    values = jnp.clip(jax.random.normal(key_values, (ROWS, SLOTS, D), jnp.float32), -4.0, 4.0)
    return (values * column_scale[None, None, :]).astype(jnp.bfloat16)


def level_of(key, shape, cuts, smallest, largest):
    loudness = 1.0
    for axis_at, shards_of in cuts:
        heights = jax.random.uniform(jax.random.fold_in(jax.random.fold_in(key, 6), axis_at), (shards_of,), jnp.float32, smallest / len(cuts), largest / len(cuts))
        loudness = loudness * jnp.repeat(jnp.exp(heights), shape[axis_at] // shards_of).reshape((-1,) + (1,) * (len(shape) - 1 - axis_at))
    return loudness


def normal_values(key, extent, spread, reach, cuts=(), kind=jnp.bfloat16):
    array = spread * jax.random.normal(key, extent, jnp.float32)
    if cuts:
        array = array * level_of(key, extent, cuts, -0.22, 0.18)
    return jnp.clip(array, -reach, reach).astype(kind)


def setup_inputs(seed: int = 0) -> dict:
    streams_of = jax.random.split(jax.random.key(seed), 19)
    block_input = normal_values(streams_of[0], (ROWS, SLOTS, D), 1.0, 6.0, ((0, 8), (1, 4)))
    output_grad = draw_output_grad(jax.random.fold_in(streams_of[18], 71), 0)
    row_lengths = draw_row_lengths(jax.random.fold_in(streams_of[18], 71), 0)
    qkv_weight = normal_values(streams_of[3], (LAYERS, D, 3, D), D ** -0.5, 0.1875, ((1, 8), (3, 4)), jnp.float32)
    proj_weight = normal_values(streams_of[4], (LAYERS, D, D), (D // 8) ** -0.5, 0.5, ((1, 4), (2, 8)), jnp.float32)
    up_weight = normal_values(streams_of[5], (LAYERS, D, FF), D ** -0.5, 0.1875, ((1, 8), (2, 4)), jnp.float32)
    down_weight = normal_values(streams_of[6], (LAYERS, FF, D), (FF // 2) ** -0.5, 0.125, ((1, 4), (2, 8)), jnp.float32)
    norm_params = draw_norm_params(jax.random.fold_in(streams_of[18], 71), 0)
    qkv_first = normal_values(streams_of[8], (LAYERS, D, 3, D), (0.1 / (LAYERS * D * (4 * D + 2 * FF)) ** 0.5), 0.00012207031, ((1, 8), (3, 4)), jnp.float32)
    proj_first = normal_values(streams_of[9], (LAYERS, D, D), (0.1 / (LAYERS * D * (4 * D + 2 * FF)) ** 0.5), 0.00012207031, ((1, 4), (2, 8)), jnp.float32)
    up_first = normal_values(streams_of[10], (LAYERS, D, FF), (0.1 / (LAYERS * D * (4 * D + 2 * FF)) ** 0.5), 0.00012207031, ((1, 8), (2, 4)), jnp.float32)
    down_first = normal_values(streams_of[11], (LAYERS, FF, D), (0.1 / (LAYERS * D * (4 * D + 2 * FF)) ** 0.5), 0.00012207031, ((1, 4), (2, 8)), jnp.float32)
    norm_first = normal_values(streams_of[12], (LAYERS, 4, D), (0.1 / (LAYERS * D * (4 * D + 2 * FF)) ** 0.5), 0.00012207031, ((2, 32),), jnp.float32)
    qkv_second = jnp.clip(jnp.exp(math.log(5.165735617040923e-10) - 1.37102684 * jax.random.uniform(streams_of[13], (LAYERS, D, 3, D), jnp.float32) ** level_of(streams_of[13], (LAYERS, D, 3, D), ((1, 8), (3, 4)), -0.2, 0.2)), 1.3113021779531664e-10, 5.165735617040923e-10)
    proj_second = jnp.clip(jnp.exp(math.log(5.165735617040923e-10) - 1.37102684 * jax.random.uniform(streams_of[14], (LAYERS, D, D), jnp.float32) ** level_of(streams_of[14], (LAYERS, D, D), ((1, 4), (2, 8)), -0.2, 0.2)), 1.3113021779531664e-10, 5.165735617040923e-10)
    up_second = jnp.clip(jnp.exp(math.log(5.165735617040923e-10) - 1.37102684 * jax.random.uniform(streams_of[15], (LAYERS, D, FF), jnp.float32) ** level_of(streams_of[15], (LAYERS, D, FF), ((1, 8), (2, 4)), -0.2, 0.2)), 1.3113021779531664e-10, 5.165735617040923e-10)
    down_second = jnp.clip(jnp.exp(math.log(5.165735617040923e-10) - 1.37102684 * jax.random.uniform(streams_of[16], (LAYERS, FF, D), jnp.float32) ** level_of(streams_of[16], (LAYERS, FF, D), ((1, 4), (2, 8)), -0.2, 0.2)), 1.3113021779531664e-10, 5.165735617040923e-10)
    norm_second = jnp.clip(jnp.exp(math.log(5.165735617040923e-10) - 1.37102684 * jax.random.uniform(streams_of[17], (LAYERS, 4, D), jnp.float32) ** level_of(streams_of[17], (LAYERS, 4, D), ((2, 32),), -0.2, 0.2)), 1.3113021779531664e-10, 5.165735617040923e-10)
    return dict(block_input=block_input, output_grad=output_grad, row_lengths=row_lengths, qkv_weight=qkv_weight, proj_weight=proj_weight, up_weight=up_weight, down_weight=down_weight, norm_params=norm_params, qkv_first=qkv_first, proj_first=proj_first, up_first=up_first, down_first=down_first, norm_first=norm_first, qkv_second=qkv_second, proj_second=proj_second, up_second=up_second, down_second=down_second, norm_second=norm_second)


EPS_NORM = 1e-05
BETA_ONE = 0.5
BETA_TWO = 0.75
LEARN_RATE = 0.03
NORM_RATE = 0.3
WEIGHT_DECAY = 0.1
CLIP_NORM = 0.1
ADAM_EPS = 1e-08

@jax.custom_vjp
def low(v):
    return lax.optimization_barrier(v.astype(jnp.bfloat16)).astype(jnp.float32)

@jax.custom_vjp
def low_back(v):
    return v

def low_keep(v):
    return (low(v), None)

def low_pass(kept, grad):
    return (grad,)

def back_keep(v):
    return (v, None)

def back_low(kept, grad):
    return (low(grad),)
low.defvjp(low_keep, low_pass)
low_back.defvjp(back_keep, back_low)

def slope_table(head_count):
    return np.power(2.0, -8.0 * (np.arange(head_count) + 1.0) / head_count)

def matmul(left, right):
    return jnp.dot(left, right, precision=lax.Precision.HIGHEST, preferred_element_type=jnp.float32)

def layer_norm(hidden, gain, bias):
    centre = lax.optimization_barrier(jnp.mean(hidden, axis=-1, keepdims=True))
    centered = hidden - centre
    variance = lax.optimization_barrier(jnp.mean(centered * centered, axis=-1, keepdims=True))
    scaled = centered * lax.rsqrt(variance + EPS_NORM)
    return (scaled, scaled * gain + bias)

def attend(queries, key_rows, values, slope, length):
    block_rows = min(512, SLOTS)
    key_pos = jnp.arange(SLOTS, dtype=jnp.int32)

    def one_block(block_index):
        first_row = block_index * block_rows
        query_block = lax.dynamic_slice_in_dim(queries, first_row, block_rows, 0)
        query_pos = first_row + jnp.arange(block_rows, dtype=jnp.int32)
        distance = (key_pos[None, :] - query_pos[:, None]).astype(jnp.float32)
        raw = matmul(query_block, key_rows.T) * HD ** (-0.5) + slope * distance
        allowed = (key_pos[None, :] <= query_pos[:, None]) & (key_pos[None, :] < length)
        scores = jnp.where(allowed, low_back(raw), -jnp.inf)
        attention = low(jnp.exp(scores - jax.nn.logsumexp(scores, axis=1, keepdims=True)))
        return low_back(low(matmul(attention, values)))
    blocks = lax.map(jax.checkpoint(one_block), jnp.arange(SLOTS // block_rows, dtype=jnp.int32))
    return blocks.reshape(SLOTS, -1)

def row_forward(hidden, length, weights):
    w_qkv, w_proj, w_up, w_down, norm_rows = weights
    slopes = jnp.asarray(slope_table(H), jnp.float32)
    for layer_index in range(LAYERS):
        unused, normed = layer_norm(hidden, norm_rows[layer_index, 0], norm_rows[layer_index, 1])
        qkv_matrix = w_qkv[layer_index].reshape(D, 3 * D)
        projected = low_back(low(matmul(low(normed), qkv_matrix))).reshape(SLOTS, 3, H, HD)
        context = jax.vmap(attend, in_axes=(1, 1, 1, 0, None), out_axes=1)(projected[:, 0], projected[:, 1], projected[:, 2], slopes, length)
        middle = hidden + low_back(matmul(context.reshape(SLOTS, D), w_proj[layer_index]))
        unused, normed_two = layer_norm(middle, norm_rows[layer_index, 2], norm_rows[layer_index, 3])
        upper = low_back(matmul(low(normed_two), w_up[layer_index]))
        hidden = middle + low_back(matmul(low(jax.nn.gelu(upper, approximate=True)), w_down[layer_index]))
    return hidden

def forward(inputs, params, lengths):
    weights = (low(params[0]), low(params[1]), low(params[2]), low(params[3]), low(params[4]))

    def one_row(pair):
        return row_forward(pair[0], pair[1], weights)
    return lax.map(jax.checkpoint(one_row), (inputs, lengths))

def adam_update(master, grad, first, second, factor, fix_one, fix_two, decay, rate):
    clipped = grad * factor
    momentum = BETA_ONE * first + (1.0 - BETA_ONE) * clipped
    variance = BETA_TWO * second + (1.0 - BETA_TWO) * clipped * clipped
    step_size = momentum / fix_one / (jnp.sqrt(variance / fix_two) + ADAM_EPS) + decay * master
    fresh = master - rate * step_size
    return (momentum, variance, fresh, fresh.astype(jnp.bfloat16))

def reference(block_input, output_grad, row_lengths, qkv_weight, proj_weight, up_weight, down_weight, norm_params, qkv_first, proj_first, up_first, down_first, norm_first, qkv_second, proj_second, up_second, down_second, norm_second):
    params = (qkv_weight, proj_weight, up_weight, down_weight, norm_params)

    def run(inputs, values):
        return forward(inputs, values, row_lengths)
    block_output, pullback = jax.vjp(run, block_input.astype(jnp.float32), params)
    token_mask = (jnp.arange(SLOTS, dtype=jnp.int32)[None, :] < row_lengths[:, None]).astype(jnp.float32)
    input_grad, grads = pullback(output_grad.astype(jnp.float32) * token_mask[:, :, None])
    qkv_grad, proj_grad, up_grad, down_grad, norm_grad = grads
    total = jnp.sum(qkv_grad * qkv_grad) + jnp.sum(proj_grad * proj_grad) + jnp.sum(up_grad * up_grad) + jnp.sum(down_grad * down_grad) + jnp.sum(norm_grad * norm_grad)
    grad_norm = jnp.sqrt(total)
    factor = CLIP_NORM / jnp.maximum(grad_norm, CLIP_NORM)
    fix_one = 1.0 - BETA_ONE ** STEP
    fix_two = 1.0 - BETA_TWO ** STEP
    qkv_out = adam_update(qkv_weight, qkv_grad, qkv_first, qkv_second, factor, fix_one, fix_two, WEIGHT_DECAY, LEARN_RATE)
    proj_out = adam_update(proj_weight, proj_grad, proj_first, proj_second, factor, fix_one, fix_two, WEIGHT_DECAY, LEARN_RATE)
    up_out = adam_update(up_weight, up_grad, up_first, up_second, factor, fix_one, fix_two, WEIGHT_DECAY, LEARN_RATE)
    down_out = adam_update(down_weight, down_grad, down_first, down_second, factor, fix_one, fix_two, WEIGHT_DECAY, LEARN_RATE)
    norm_out = adam_update(norm_params, norm_grad, norm_first, norm_second, factor, fix_one, fix_two, 0.0, NORM_RATE)
    return (block_output, input_grad, grad_norm, qkv_grad, proj_grad, up_grad, down_grad, norm_grad, qkv_out[0], proj_out[0], up_out[0], down_out[0], norm_out[0], qkv_out[1], proj_out[1], up_out[1], down_out[1], norm_out[1], qkv_out[2], proj_out[2], up_out[2], down_out[2], norm_out[2], qkv_out[3], proj_out[3], up_out[3], down_out[3], norm_out[3])
```

```python
import jax
import jax.numpy as jnp
import numpy as np
from jax import lax
from jax.sharding import PartitionSpec as P

H = 8
HD = 128
STEP = 5


EPS_NORM = 1e-05
BETA_ONE = 0.5
BETA_TWO = 0.75
LEARN_RATE = 0.03
NORM_RATE = 0.3
WEIGHT_DECAY = 0.1
CLIP_NORM = 0.1
ADAM_EPS = 1e-08


def slope_table(head_count):
    return np.power(2.0, -8.0 * (np.arange(head_count) + 1.0) / head_count)


def smooth_act(values):
    return jax.nn.gelu(values, approximate=True)


def smooth_back(upper, grad_act):
    unused, pullback = jax.vjp(smooth_act, upper)
    return pullback(grad_act)[0]


def layer_norm(hidden, gain, bias):
    centre = jnp.mean(hidden, axis=-1, keepdims=True)
    centered = hidden - centre
    variance = jnp.mean(centered * centered, axis=-1, keepdims=True)
    scaled = centered * lax.rsqrt(variance + EPS_NORM)
    return (scaled, scaled * gain + bias)


def norm_back(hidden, gain, grad_out):
    centered = hidden - jnp.mean(hidden, axis=-1, keepdims=True)
    inverse = lax.rsqrt(jnp.mean(centered * centered, axis=-1, keepdims=True) + EPS_NORM)
    scaled = centered * inverse
    grad_scaled = grad_out * gain
    grad_hidden = inverse * (
        grad_scaled
        - jnp.mean(grad_scaled, axis=-1, keepdims=True)
        - scaled * jnp.mean(grad_scaled * scaled, axis=-1, keepdims=True)
    )
    return (grad_hidden, jnp.sum(grad_out * scaled, axis=0), jnp.sum(grad_out, axis=0))


def pack_layer(masters, layer_index):
    qkv, proj, up, down = (masters[i][layer_index].astype(jnp.bfloat16) for i in range(4))
    return qkv.reshape(qkv.shape[0], -1), proj, up, down


def gather_layer(masters, layer_index):
    qkv, proj, up, down = pack_layer(masters, layer_index)
    return (
        lax.all_gather(qkv, "dp", axis=0, tiled=True),
        lax.all_gather(proj, "dp", axis=1, tiled=True),
        lax.all_gather(up, "dp", axis=0, tiled=True),
        lax.all_gather(down, "dp", axis=1, tiled=True),
    )


def scatter_sum(part, axis_name, dimension):
    return lax.psum_scatter(
        part.astype(jnp.bfloat16), axis_name, scatter_dimension=dimension, tiled=True
    ).astype(jnp.float32)


def block_scores(query_block, key_rows, first_row, slopes, lengths):
    block_rows = query_block.shape[1]
    slot_count = key_rows.shape[1]
    raw = jnp.einsum(
        "rqhd,rkhd->rhqk", query_block, key_rows, preferred_element_type=jnp.float32
    ) * HD ** (-0.5)
    query_pos = first_row + jnp.arange(block_rows, dtype=jnp.int32)
    key_pos = jnp.arange(slot_count, dtype=jnp.int32)
    distance = (key_pos[None, :] - query_pos[:, None]).astype(jnp.float32)
    raw = raw + slopes[None, :, None, None] * distance[None, None]
    causal = key_pos[None, :] <= query_pos[:, None]
    filled = key_pos[None, :] < lengths[:, None]
    allowed = causal[None, None] & filled[:, None, None, :]
    return jnp.where(allowed, raw, -jnp.inf)


def attend_forward(queries, key_rows, values, slopes, lengths):
    row_count, slot_count, head_local, head_size = queries.shape
    block_rows = min(512, slot_count)

    def one_block(block_index, carry):
        context, log_total = carry
        first_row = block_index * block_rows
        query_block = lax.dynamic_slice_in_dim(queries, first_row, block_rows, 1)
        scores = block_scores(query_block, key_rows, first_row, slopes, lengths)
        block_total = jax.nn.logsumexp(scores, axis=3, keepdims=True)
        attention = jnp.exp(scores - block_total).astype(jnp.bfloat16)
        block_context = jnp.einsum(
            "rhqk,rkhd->rqhd", attention, values, preferred_element_type=jnp.float32
        ).astype(jnp.bfloat16)
        context = lax.dynamic_update_slice_in_dim(context, block_context, first_row, 1)
        log_total = lax.dynamic_update_slice_in_dim(log_total, block_total[..., 0], first_row, 2)
        return (context, log_total)

    initial = (
        jnp.zeros(queries.shape, jnp.bfloat16),
        jnp.zeros((row_count, head_local, slot_count), jnp.float32),
    )
    return lax.fori_loop(0, slot_count // block_rows, one_block, initial)


def attend_backward(queries, key_rows, values, grad_context, log_total, slopes, lengths):
    row_count, slot_count, head_local, head_size = queries.shape
    block_rows = min(512, slot_count)
    score_scale = HD ** (-0.5)

    def one_block(block_index, carry):
        grad_queries, grad_keys, grad_values = carry
        first_row = block_index * block_rows
        query_block = lax.dynamic_slice_in_dim(queries, first_row, block_rows, 1)
        grad_block = lax.dynamic_slice_in_dim(grad_context, first_row, block_rows, 1)
        scores = block_scores(query_block, key_rows, first_row, slopes, lengths)
        block_total = lax.dynamic_slice_in_dim(log_total, first_row, block_rows, 2)
        attention = jnp.exp(scores - block_total[..., None])
        grad_attention = jnp.einsum(
            "rqhd,rkhd->rhqk", grad_block, values, preferred_element_type=jnp.float32
        )
        inner_sum = jnp.sum(attention * grad_attention, axis=3, keepdims=True)
        grad_scores = (attention * (grad_attention - inner_sum)).astype(jnp.bfloat16)
        block_grad = (
            jnp.einsum("rhqk,rkhd->rqhd", grad_scores, key_rows, preferred_element_type=jnp.float32)
            * score_scale
        ).astype(jnp.bfloat16)
        grad_queries = lax.dynamic_update_slice_in_dim(grad_queries, block_grad, first_row, 1)
        grad_keys = (
            grad_keys
            + jnp.einsum(
                "rhqk,rqhd->rkhd", grad_scores, query_block, preferred_element_type=jnp.float32
            )
            * score_scale
        )
        grad_values = grad_values + jnp.einsum(
            "rhqk,rqhd->rkhd",
            attention.astype(jnp.bfloat16),
            grad_block,
            preferred_element_type=jnp.float32,
        )
        return (grad_queries, grad_keys, grad_values)

    initial = (
        jnp.zeros(queries.shape, jnp.bfloat16),
        jnp.zeros(queries.shape, jnp.float32),
        jnp.zeros(queries.shape, jnp.float32),
    )
    return lax.fori_loop(0, slot_count // block_rows, one_block, initial)


def adam_update(master, grad, first, second, factor, fix_one, fix_two, decay, rate):
    clipped = grad * factor
    momentum = BETA_ONE * first + (1.0 - BETA_ONE) * clipped
    variance = BETA_TWO * second + (1.0 - BETA_TWO) * clipped * clipped
    step_size = momentum / fix_one / (jnp.sqrt(variance / fix_two) + ADAM_EPS) + decay * master
    fresh = master - rate * step_size
    return (momentum, variance, fresh, fresh.astype(jnp.bfloat16))


def body(
    block_input,
    output_grad,
    row_lengths,
    qkv_weight,
    proj_weight,
    up_weight,
    down_weight,
    norm_params,
    qkv_first,
    proj_first,
    up_first,
    down_first,
    norm_first,
    qkv_second,
    proj_second,
    up_second,
    down_second,
    norm_second,
):
    masters = (qkv_weight, proj_weight, up_weight, down_weight, norm_params)
    row_count, local_slots, model_width = block_input.shape
    seq_count = lax.axis_size("seq")
    head_local = H // seq_count
    token_count = row_count * local_slots
    layer_count = qkv_weight.shape[0]
    table = jnp.asarray(slope_table(H), jnp.float32)
    head_ids = lax.axis_index("seq") * head_local + jnp.arange(head_local, dtype=jnp.int32)
    slopes = jnp.sum(
        jnp.where(
            jnp.arange(H, dtype=jnp.int32)[None, :] == head_ids[:, None], table[None, :], 0.0
        ),
        axis=1,
    )
    hidden = block_input.astype(jnp.float32).reshape(token_count, model_width)
    local_width = head_local * HD
    group_count = lax.axis_size("dp")
    norm_piece = norm_params.shape[2]
    norm_all = lax.all_gather(
        norm_params.astype(jnp.bfloat16), ("dp", "seq"), axis=2, tiled=True
    ).astype(jnp.float32)
    saved = []
    for layer_index in range(layer_count):
        w_qkv, w_proj, w_up, w_down = gather_layer(masters, layer_index)
        norm_rows = norm_all[layer_index]
        unused, normed = layer_norm(hidden, norm_rows[0], norm_rows[1])
        normed_one = lax.all_gather(normed.astype(jnp.bfloat16), "seq", axis=0, tiled=True)
        projected = jnp.dot(normed_one, w_qkv, preferred_element_type=jnp.float32).astype(
            jnp.bfloat16
        )
        spread = projected.reshape(row_count, local_slots * seq_count, 3, head_local, HD)
        context, log_total = attend_forward(
            spread[:, :, 0], spread[:, :, 1], spread[:, :, 2], slopes, row_lengths
        )
        context_rows = context.reshape(-1, local_width)
        middle = hidden + scatter_sum(
            jnp.dot(context_rows, w_proj, preferred_element_type=jnp.float32), "seq", 0
        )
        unused, normed_two = layer_norm(middle, norm_rows[2], norm_rows[3])
        normed_two = lax.all_gather(normed_two.astype(jnp.bfloat16), "seq", axis=0, tiled=True)
        upper = jnp.dot(normed_two, w_up, preferred_element_type=jnp.float32)
        act_low = smooth_act(upper).astype(jnp.bfloat16)
        following = middle + scatter_sum(
            jnp.dot(act_low, w_down, preferred_element_type=jnp.float32), "seq", 0
        )
        saved.append(
            (hidden, middle, spread, log_total, context_rows, act_low, upper, normed_one,
             normed_two, (w_qkv, w_proj, w_up, w_down, norm_rows))
        )
        hidden = following
    block_output = hidden.reshape(row_count, local_slots, model_width)
    positions = lax.axis_index("seq") * local_slots + jnp.arange(local_slots, dtype=jnp.int32)
    token_mask = (positions[None, :] < row_lengths[:, None]).astype(jnp.float32)
    grad_hidden = (output_grad.astype(jnp.float32) * token_mask[:, :, None]).reshape(
        token_count, model_width
    )
    reduced_all = [None] * layer_count
    norm_parts = [None] * layer_count
    for layer_index in reversed(range(layer_count)):
        (hidden_in, middle, spread, log_total, context_rows, act_low, upper, normed_one,
         normed_two, weights) = saved[layer_index]
        w_qkv, w_proj, w_up, w_down, norm_rows = weights
        grad_ffn = lax.all_gather(grad_hidden.astype(jnp.bfloat16), "seq", axis=0, tiled=True)
        down_grad = scatter_sum(
            jnp.einsum("tf,td->fd", act_low, grad_ffn, preferred_element_type=jnp.float32), "dp", 1
        )
        grad_act = jnp.einsum("td,fd->tf", grad_ffn, w_down, preferred_element_type=jnp.float32)
        grad_upper = smooth_back(upper, grad_act).astype(jnp.bfloat16)
        up_grad = scatter_sum(
            jnp.einsum("td,tf->df", normed_two, grad_upper, preferred_element_type=jnp.float32),
            "dp", 0,
        )
        grad_normed_two = scatter_sum(
            jnp.einsum("tf,df->td", grad_upper, w_up, preferred_element_type=jnp.float32), "seq", 0
        )
        grad_middle_norm, gain_two, bias_two = norm_back(middle, norm_rows[2], grad_normed_two)
        grad_middle = grad_hidden + grad_middle_norm
        grad_branch = lax.all_gather(grad_middle.astype(jnp.bfloat16), "seq", axis=0, tiled=True)
        proj_grad = scatter_sum(
            jnp.einsum("td,te->de", context_rows, grad_branch, preferred_element_type=jnp.float32),
            "dp", 1,
        )
        grad_context = jnp.einsum(
            "te,de->td", grad_branch, w_proj, preferred_element_type=jnp.float32
        ).astype(jnp.bfloat16)
        grad_context = grad_context.reshape(row_count, -1, head_local, HD)
        grad_queries, grad_keys, grad_values = attend_backward(
            spread[:, :, 0], spread[:, :, 1], spread[:, :, 2], grad_context, log_total, slopes,
            row_lengths,
        )
        grad_projected = jnp.stack(
            (grad_queries, grad_keys.astype(jnp.bfloat16), grad_values.astype(jnp.bfloat16)), axis=2
        ).reshape(-1, 3 * local_width)
        qkv_grad = scatter_sum(
            jnp.einsum("td,te->de", normed_one, grad_projected, preferred_element_type=jnp.float32),
            "dp", 0,
        ).reshape(-1, 3, local_width)
        grad_normed = scatter_sum(
            jnp.einsum("te,de->td", grad_projected, w_qkv, preferred_element_type=jnp.float32),
            "seq", 0,
        )
        grad_input_norm, gain_one, bias_one = norm_back(hidden_in, norm_rows[0], grad_normed)
        grad_hidden = grad_middle + grad_input_norm
        norm_parts[layer_index] = jnp.stack((gain_one, bias_one, gain_two, bias_two), axis=0)
        reduced_all[layer_index] = (qkv_grad, proj_grad, up_grad, down_grad)
    input_grad = grad_hidden.reshape(row_count, local_slots, model_width)
    norm_grad = lax.psum_scatter(
        jnp.stack(norm_parts, axis=0), ("dp", "seq"), scatter_dimension=2, tiled=True
    )
    stacked = [
        jnp.stack([layer_grads[position] for layer_grads in reduced_all], axis=0)
        for position in range(4)
    ] + [norm_grad]
    square_sum = (
        jnp.sum(stacked[0] * stacked[0])
        + jnp.sum(stacked[1] * stacked[1])
        + jnp.sum(stacked[2] * stacked[2])
        + jnp.sum(stacked[3] * stacked[3])
        + jnp.sum(stacked[4] * stacked[4])
    )
    grad_norm = jnp.sqrt(lax.psum(square_sum, ("dp", "seq")))
    factor = CLIP_NORM / jnp.maximum(grad_norm, CLIP_NORM)
    fix_one = 1.0 - BETA_ONE**STEP
    fix_two = 1.0 - BETA_TWO**STEP
    qkv_out = adam_update(
        qkv_weight,
        stacked[0],
        qkv_first,
        qkv_second,
        factor,
        fix_one,
        fix_two,
        WEIGHT_DECAY,
        LEARN_RATE,
    )
    proj_out = adam_update(
        proj_weight,
        stacked[1],
        proj_first,
        proj_second,
        factor,
        fix_one,
        fix_two,
        WEIGHT_DECAY,
        LEARN_RATE,
    )
    up_out = adam_update(
        up_weight,
        stacked[2],
        up_first,
        up_second,
        factor,
        fix_one,
        fix_two,
        WEIGHT_DECAY,
        LEARN_RATE,
    )
    down_out = adam_update(
        down_weight,
        stacked[3],
        down_first,
        down_second,
        factor,
        fix_one,
        fix_two,
        WEIGHT_DECAY,
        LEARN_RATE,
    )
    norm_out = adam_update(
        norm_params, stacked[4], norm_first, norm_second, factor, fix_one, fix_two, 0.0, NORM_RATE
    )
    return (
        block_output,
        input_grad,
        grad_norm,
        stacked[0],
        stacked[1],
        stacked[2],
        stacked[3],
        stacked[4],
        qkv_out[0],
        proj_out[0],
        up_out[0],
        down_out[0],
        norm_out[0],
        qkv_out[1],
        proj_out[1],
        up_out[1],
        down_out[1],
        norm_out[1],
        qkv_out[2],
        proj_out[2],
        up_out[2],
        down_out[2],
        norm_out[2],
        qkv_out[3],
        proj_out[3],
        up_out[3],
        down_out[3],
        norm_out[3],
    )


def solution(mesh):
    return jax.shard_map(
        body,
        mesh=mesh,
        in_specs=(
            P("dp", "seq", None),
            P("dp", "seq", None),
            P("dp"),
            P(None, "dp", None, "seq"),
            P(None, "seq", "dp"),
            P(None, "dp", "seq"),
            P(None, "seq", "dp"),
            P(None, None, ("dp", "seq")),
            P(None, "dp", None, "seq"),
            P(None, "seq", "dp"),
            P(None, "dp", "seq"),
            P(None, "seq", "dp"),
            P(None, None, ("dp", "seq")),
            P(None, "dp", None, "seq"),
            P(None, "seq", "dp"),
            P(None, "dp", "seq"),
            P(None, "seq", "dp"),
            P(None, None, ("dp", "seq")),
        ),
        out_specs=(
            P("dp", "seq", None),
            P("dp", "seq", None),
            P(),
            P(None, "dp", None, "seq"),
            P(None, "seq", "dp"),
            P(None, "dp", "seq"),
            P(None, "seq", "dp"),
            P(None, None, ("dp", "seq")),
            P(None, "dp", None, "seq"),
            P(None, "seq", "dp"),
            P(None, "dp", "seq"),
            P(None, "seq", "dp"),
            P(None, None, ("dp", "seq")),
            P(None, "dp", None, "seq"),
            P(None, "seq", "dp"),
            P(None, "dp", "seq"),
            P(None, "seq", "dp"),
            P(None, None, ("dp", "seq")),
            P(None, "dp", None, "seq"),
            P(None, "seq", "dp"),
            P(None, "dp", "seq"),
            P(None, "seq", "dp"),
            P(None, None, ("dp", "seq")),
            P(None, "dp", None, "seq"),
            P(None, "seq", "dp"),
            P(None, "dp", "seq"),
            P(None, "seq", "dp"),
            P(None, None, ("dp", "seq")),
        ),
        check_vma=False,
    )
```

```python
import functools

import jax
import jax.numpy as jnp
import numpy as np
from jax import lax
from jax.experimental import pallas as pl
from jax.experimental.pallas import tpu as pltpu
from jax.sharding import PartitionSpec as P

H = 8
HD = 128
STEP = 5
CORES = 2
ZSIZE = 4

EPS_NORM = 1e-05
BETA_ONE = 0.5
BETA_TWO = 0.75
LEARN_RATE = 0.03
NORM_RATE = 0.3
WEIGHT_DECAY = 0.1
CLIP_NORM = 0.1
ADAM_EPS = 1e-08

F32 = jnp.float32
BF16 = jnp.bfloat16
MESH = pl.DeviceIdType.MESH
SCORE_SCALE = HD ** (-0.5)
GELU_A = (2.0 / np.pi) ** 0.5
GELU_B = 0.044715


def slope_table(head_count):
    return np.power(2.0, -8.0 * (np.arange(head_count) + 1.0) / head_count)


def mm_nn(a, b):
    return lax.dot_general(a, b, (((1,), (0,)), ((), ())), preferred_element_type=F32)


def mm_nt(a, b):
    return lax.dot_general(a, b, (((1,), (1,)), ((), ())), preferred_element_type=F32)


def mm_tn(a, b):
    return lax.dot_general(a, b, (((0,), (0,)), ((), ())), preferred_element_type=F32)


def normalise(v):
    centered = v - jnp.mean(v, axis=-1, keepdims=True)
    inverse = lax.rsqrt(jnp.mean(centered * centered, axis=-1, keepdims=True) + EPS_NORM)
    return centered * inverse, inverse


def rows_of(index, size):
    return pl.ds(pl.multiple_of(index * size, size), size)


class Place:
    def __init__(self, zn, xn, yn):
        self.zn, self.xn, self.yn = zn, xn, yn
        self.dp = lax.axis_index("dp")
        self.seq = lax.axis_index("seq")
        self.z, self.x = self.dp // xn, lax.rem(self.dp, xn)
        self.y, self.c = self.seq // CORES, lax.rem(self.seq, CORES)

    def zo(self, k):
        return lax.rem(self.z + k + self.zn, self.zn)

    def xo(self, k):
        return lax.rem(self.x + k + self.xn, self.xn)

    def yo(self, k):
        return lax.rem(self.y + k + self.yn, self.yn)

    def dev(self, dz=0, dx=0, dy=0, dc=0):
        core = (1 - self.c) if dc else self.c
        return (self.zo(dz) * self.xn + self.xo(dx), self.yo(dy) * CORES + core)

    def dp_at(self, dz, dx):
        return self.zo(dz) * self.xn + self.xo(dx)

    def seq_at(self, dy, dc):
        core = (1 - self.c) if dc else self.c
        return self.yo(dy) * CORES + core

    def peers(self):
        out = [self.dev(dc=1)]
        out += [self.dev(dy=k) for k in range(1, self.yn)]
        out += [self.dev(dx=k) for k in range(1, self.xn)]
        out += [self.dev(dz=k) for k in range(1, self.zn)]
        return out

    def barrier(self):
        sem = pltpu.get_barrier_semaphore()
        peers = self.peers()
        for peer in peers:
            pl.semaphore_signal(sem, inc=1, device_id=peer, device_id_type=MESH)
        pl.semaphore_wait(sem, len(peers))


def near_first(count):
    order = []
    for k in range(1, count):
        order.append((min(k, count - k), k))
    return [k for unused, k in sorted(order)]


def remote(src, dst, send, recv, dev):
    return pltpu.make_async_remote_copy(
        src_ref=src, dst_ref=dst, send_sem=send, recv_sem=recv, device_id=dev, device_id_type=MESH
    )


def all_sum(place, value, slots, send, recv):
    stages = (
        (CORES, place.c, lambda k: place.dev(dc=1), lambda k: 1 - place.c),
        (place.yn, place.y, lambda k: place.dev(dy=k), lambda k: place.yo(-k)),
        (place.xn, place.x, lambda k: place.dev(dx=k), lambda k: place.xo(-k)),
        (place.zn, place.z, lambda k: place.dev(dz=k), lambda k: place.zo(-k)),
    )
    base = 0
    at = 0
    for size, mine, target, origin in stages:
        slots[base + mine] = value
        own = slots.at[base + mine]
        for k in range(1, size):
            remote(own, own, send.at[at + k - 1], recv.at[at + k - 1], target(k)).start()
        for k in range(1, size):
            came = slots.at[base + origin(k)]
            remote(came, came, send.at[at + k - 1], recv.at[at + k - 1], target(k)).wait_recv()
        for k in range(1, size):
            remote(own, own, send.at[at + k - 1], recv.at[at + k - 1], target(k)).wait_send()
        value = slots[base]
        for k in range(1, size):
            value = value + slots[base + k]
        base += size
        at += size - 1
    return value


def sum_slots(zn, xn, yn):
    return CORES + yn + xn + zn, 1 + (yn - 1) + (xn - 1) + (zn - 1)


class Gather:
    def __init__(self, place, buf, block, send, recv):
        self.p, self.buf, self.block, self.send, self.recv = place, buf, block, send, recv

    def at(self, dy, dc):
        return self.buf.at[rows_of(self.p.seq_at(dy, dc), self.block)]

    def start(self):
        p, own = self.p, self.at(0, 0)
        for k in range(1, p.yn):
            remote(own, own, self.send.at[k], self.recv.at[k], p.dev(dy=k)).start()
        remote(own, own, self.send.at[0], self.recv.at[0], p.dev(dc=1)).start()

    def wait_chip(self):
        came = self.at(0, 1)
        remote(came, came, self.send.at[0], self.recv.at[0], self.p.dev(dc=1)).wait_recv()

    def forward(self):
        p = self.p
        for k in range(1, p.yn):
            came = self.at(-k, 0)
            remote(came, came, self.send.at[k], self.recv.at[k], p.dev(dy=k)).wait_recv()
            f = p.yn - 1 + k
            remote(came, came, self.send.at[f], self.recv.at[f], p.dev(dc=1)).start()

    def wait_rest(self):
        p = self.p
        for k in range(1, p.yn):
            f = p.yn - 1 + k
            came = self.at(-k, 1)
            remote(came, came, self.send.at[f], self.recv.at[f], p.dev(dc=1)).wait_recv()
        own = self.at(0, 0)
        for k in range(1, p.yn):
            remote(own, own, self.send.at[k], self.recv.at[k], p.dev(dy=k)).wait_send()
            f = p.yn - 1 + k
            sent = self.at(-k, 0)
            remote(sent, sent, self.send.at[f], self.recv.at[f], p.dev(dc=1)).wait_send()
        remote(own, own, self.send.at[0], self.recv.at[0], p.dev(dc=1)).wait_send()


class Scatter:
    def __init__(self, place, sbuf, rbuf, ysend, yrecv, acc, send, recv):
        self.p = place
        self.sbuf, self.rbuf, self.ysend, self.yrecv, self.acc = sbuf, rbuf, ysend, yrecv, acc
        self.send, self.recv = send, recv

    def core(self, k):
        return remote(
            self.sbuf.at[k], self.rbuf.at[k], self.send.at[k], self.recv.at[k], self.p.dev(dc=1)
        )

    def cross(self, k):
        s = self.p.yn + k - 1
        return remote(
            self.ysend.at[k - 1],
            self.yrecv.at[k - 1],
            self.send.at[s],
            self.recv.at[s],
            self.p.dev(dy=k),
        )

    def start(self, part):
        p = self.p
        for k in list(range(1, p.yn)) + [0]:
            self.sbuf[k] = part(p.seq_at(k, 1)).astype(BF16)
            self.core(k).start()
            mine = part(p.seq_at(k, 0))
            self.core(k).wait_recv()
            mine = mine + self.rbuf[k].astype(F32)
            if k:
                self.ysend[k - 1] = mine.astype(BF16)
                self.cross(k).start()
            else:
                self.acc[...] = mine

    def wait(self):
        p = self.p
        for k in range(1, p.yn):
            self.cross(k).wait_recv()
        for k in range(1, p.yn):
            self.cross(k).wait_send()
        for k in range(p.yn):
            self.core(k).wait_send()

    def rows(self, at):
        value = self.acc[at, :]
        for k in range(1, self.p.yn):
            value = value + self.yrecv[k - 1, at, :].astype(F32)
        return value


def row_loop(total, step, fn):
    def one(i, unused):
        fn(rows_of(i, step))
        return unused

    lax.fori_loop(0, total // step, one, 0)


def forward_kernel(dims, *refs):
    (layers, slots, width, block, local_width, local_ff, groups, zn, xn, yn) = dims
    heads = local_width // HD
    shard = width // groups
    refs = list(refs)

    def take(count):
        out = refs[:count]
        del refs[:count]
        return out

    lengths, slopes, x_in, norm_in = take(4)
    ws = take(4)
    out, norm_out = take(2)
    w_save = take(4)
    xn1_save, xn2_save, qkv_save, ctx_save, lse_save, act_save, dact_save, hid_save, mid_save = take(9)
    w = take(4)
    xn1, xn2, qkv, ctx, lse, act, dact, hid, mid, upper = take(10)
    sbuf, rbuf, ysend, yrecv, acc, nslots = take(6)
    zsend, zrecv, xsend, xrecv, own_sem, wsave_sem = take(6)
    ag_send, ag_recv, rs_send, rs_recv, ns_send, ns_recv, save_sem = take(7)

    p = Place(zn, xn, yn)
    z_order = near_first(zn)
    length = lengths[0]

    def shard_rows(index):
        return rows_of(index, shard)

    def z_copy(l, k, dz):
        at = shard_rows(p.dp)
        return remote(
            ws[k].at[l], w[k].at[l, at], zsend.at[l, k, dz - 1], zrecv.at[l, k, dz - 1], p.dev(dz=dz)
        )

    def z_came(l, k, dz):
        at = shard_rows(p.dp_at(-dz, 0))
        return remote(
            ws[k].at[l], w[k].at[l, at], zsend.at[l, k, dz - 1], zrecv.at[l, k, dz - 1], p.dev(dz=dz)
        )

    def x_copy(l, k, dx, dz):
        at = shard_rows(p.dp_at(-dz, 0))
        src = w[k].at[l, at] if dz else ws[k].at[l]
        return remote(
            src, w[k].at[l, at], xsend.at[l, k, dx - 1, dz], xrecv.at[l, k, dx - 1, dz], p.dev(dx=dx)
        )

    def x_came(l, k, dx, dz):
        at = shard_rows(p.dp_at(-dz, -dx))
        return remote(
            ws[k].at[l],
            w[k].at[l, at],
            xsend.at[l, k, dx - 1, dz],
            xrecv.at[l, k, dx - 1, dz],
            p.dev(dx=dx),
        )

    def own_copy(l, k):
        return pltpu.make_async_copy(ws[k].at[l], w[k].at[l, shard_rows(p.dp)], own_sem.at[l, k])

    def start_own(l, k):
        for dz in z_order:
            z_copy(l, k, dz).start()
        for dx in range(1, xn):
            x_copy(l, k, dx, 0).start()
        own_copy(l, k).start()

    def pump(l, k):
        for dz in z_order:
            z_came(l, k, dz).wait_recv()
            for dx in range(1, xn):
                x_copy(l, k, dx, dz).start()

    def save_weight(l, k):
        return pltpu.make_async_copy(w[k].at[l], w_save[k].at[l], wsave_sem.at[l, k])

    def need(l, k):
        own_copy(l, k).wait()
        for dz in [0] + z_order:
            for dx in range(1, xn):
                x_came(l, k, dx, dz).wait_recv()
        save_weight(l, k).start()

    def finish_weight(l, k):
        for dz in z_order:
            z_copy(l, k, dz).wait_send()
        for dz in range(zn):
            for dx in range(1, xn):
                x_copy(l, k, dx, dz).wait_send()
        save_weight(l, k).wait()

    def save(l, which, src, dst):
        return pltpu.make_async_copy(src, dst, save_sem.at[l, which])

    def saves(l):
        return (
            save(l, 0, xn1.at[l], xn1_save.at[l]),
            save(l, 1, xn2.at[l], xn2_save.at[l]),
            save(l, 2, qkv.at[l], qkv_save.at[l]),
            save(l, 3, ctx.at[l], ctx_save.at[l]),
            save(l, 4, lse.at[l], lse_save.at[l]),
            save(l, 5, act.at[l], act_save.at[l]),
            save(l, 6, dact.at[l], dact_save.at[l]),
            save(l, 7, hid.at[l], hid_save.at[l]),
            save(l, 8, mid.at[l], mid_save.at[l]),
        )

    p.barrier()
    start_own(0, 0)
    start_own(0, 1)
    norm_out[...] = all_sum(p, norm_in[...], nslots, ns_send, ns_recv)

    def load_in(at):
        hid[0, at, :] = x_in[at, :].astype(F32)

    row_loop(block, 64, load_in)
    first = p.seq * block

    def norm_row(index):
        return norm_out[pl.ds(index, 1), :]

    def norm_into(l, source, target, row):
        gain, bias = norm_row(4 * l + row), norm_row(4 * l + row + 1)

        def one(i, unused):
            scaled, inverse = normalise(source[l, rows_of(i, 32), :])
            at = pl.ds(pl.multiple_of(first + i * 32, 32), 32)
            target[l, at, :] = (scaled * gain + bias).astype(BF16)
            return unused

        lax.fori_loop(0, block // 32, one, 0)

    def attention(l):
        key_at = lax.broadcasted_iota(jnp.int32, (1, slots), 1)
        step = 256
        causal = lax.broadcasted_iota(jnp.int32, (step, step), 1) <= lax.broadcasted_iota(
            jnp.int32, (step, step), 0
        )
        for h in range(heads):
            bias = jnp.where(key_at < length, slopes[h] * key_at.astype(F32), -jnp.inf)
            cols = pl.ds(h * HD, HD)
            for b in range(slots // step):
                here = pl.ds(b * step, step)
                before = pl.ds(0, b * step)
                k_cols = pl.ds(local_width + h * HD, HD)
                v_cols = pl.ds(2 * local_width + h * HD, HD)
                q = qkv[l, here, cols]
                raw = mm_nt(q, qkv[l, here, k_cols]) * SCORE_SCALE + bias[:, b * step : (b + 1) * step]
                raw = jnp.where(causal, raw, -jnp.inf)
                top = jnp.max(raw, axis=1, keepdims=True)
                if b:
                    past = mm_nt(q, qkv[l, before, k_cols]) * SCORE_SCALE + bias[:, : b * step]
                    top = jnp.maximum(top, jnp.max(past, axis=1, keepdims=True))
                e_here = jnp.exp(raw - top)
                total = jnp.sum(e_here, axis=1, keepdims=True)
                value = mm_nn(e_here.astype(BF16), qkv[l, here, v_cols])
                if b:
                    e_past = jnp.exp(past - top)
                    total = total + jnp.sum(e_past, axis=1, keepdims=True)
                    value = value + mm_nn(e_past.astype(BF16), qkv[l, before, v_cols])
                ctx[l, here, cols] = (value / total).astype(BF16)
                lse[l, here, pl.ds(h, 1)] = top + jnp.log(total)

    def layer(l, unused):
        last = layers - 1
        g_one = Gather(p, xn1.at[l], block, ag_send.at[2 * l], ag_recv.at[2 * l])
        g_two = Gather(p, xn2.at[l], block, ag_send.at[2 * l + 1], ag_recv.at[2 * l + 1])
        rs = [
            Scatter(
                p, sbuf, rbuf, ysend, yrecv, acc,
                rs_send.at[2 * l + i], rs_recv.at[2 * l + i],
            )
            for i in range(2)
        ]
        save_at = saves(l)
        save_at[7].start()
        norm_into(l, hid, xn1, 0)
        g_one.start()

        @pl.when(l == 0)
        def _():
            pump(0, 0)
            start_own(0, 2)

        def project(index):
            at = rows_of(index, block)
            qkv[l, at, :] = mm_nn(xn1[l, at, :], w[0][l]).astype(BF16)

        g_one.wait_chip()
        g_one.forward()
        need(l, 0)
        project(p.seq_at(0, 0))
        project(p.seq_at(0, 1))
        g_one.wait_rest()
        save_at[0].start()
        for k in range(1, yn):
            project(p.seq_at(-k, 0))
            project(p.seq_at(-k, 1))
        save_at[2].start()
        attention(l)
        save_at[3].start()
        save_at[4].start()
        pump(l, 1)
        start_own(l, 3)
        need(l, 1)
        rs[0].start(lambda b: mm_nt(ctx[l, rows_of(b, block), :], w[1][l]))
        pump(l, 2)

        @pl.when(l < last)
        def _():
            start_own(l + 1, 0)

        rs[0].wait()

        def add_middle(at):
            mid[l, at, :] = hid[l, at, :] + rs[0].rows(at)

        row_loop(block, 32, add_middle)
        save_at[8].start()
        norm_into(l, mid, xn2, 2)
        g_two.start()
        need(l, 2)

        def expand(index):
            base = pl.multiple_of(index * block, block)
            upper[...] = mm_nn(xn2[l, pl.ds(base, block), :], w[2][l])

            def one(i, unused):
                u = upper[rows_of(i, 16), :]
                at = pl.ds(pl.multiple_of(base + i * 16, 16), 16)
                square = u * u
                t = jnp.tanh(GELU_A * u * (1.0 + GELU_B * square))
                half = 0.5 * (1.0 + t)
                act[l, at, :] = (u * half).astype(BF16)
                slope = (0.5 * GELU_A) * u * (1.0 - t * t) * (1.0 + (3.0 * GELU_B) * square)
                dact[l, at, :] = (half + slope).astype(BF16)
                return unused

            lax.fori_loop(0, block // 16, one, 0)

        expand(p.seq_at(0, 0))
        g_two.wait_chip()
        expand(p.seq_at(0, 1))
        g_two.forward()
        pump(l, 3)

        @pl.when(l < last)
        def _():
            start_own(l + 1, 1)

        g_two.wait_rest()
        save_at[1].start()
        for k in range(1, yn):
            expand(p.seq_at(-k, 0))
            expand(p.seq_at(-k, 1))
        save_at[5].start()
        save_at[6].start()
        need(l, 3)
        rs[1].start(lambda b: mm_nt(act[l, rows_of(b, block), :], w[3][l]))

        @pl.when(l < last)
        def _():
            pump(l + 1, 0)
            start_own(l + 1, 2)

        rs[1].wait()

        @pl.when(l < last)
        def _():
            def add_next(at):
                hid[l + 1, at, :] = mid[l, at, :] + rs[1].rows(at)

            row_loop(block, 32, add_next)

        @pl.when(l == last)
        def _():
            def add_out(at):
                out[at, :] = mid[l, at, :] + rs[1].rows(at)

            row_loop(block, 32, add_out)

        return unused

    lax.fori_loop(0, layers, layer, 0)

    def finish(l, unused):
        for k in range(4):
            finish_weight(l, k)
        for item in saves(l):
            item.wait()
        return unused

    lax.fori_loop(0, layers, finish, 0)


def run_forward(dims, lengths, slopes, x_in, norm_in, shards):
    (layers, slots, width, block, local_width, local_ff, groups, zn, xn, yn) = dims
    cols = (3 * local_width, local_width, local_ff, local_ff)
    slot_count, sem_count = sum_slots(zn, xn, yn)

    def saved(*shape, dtype=BF16):
        return jax.ShapeDtypeStruct((layers,) + shape, dtype)

    vmem = pl.BlockSpec(memory_space=pltpu.VMEM)
    smem = pl.BlockSpec(memory_space=pltpu.SMEM)
    hbm = pl.BlockSpec(memory_space=pl.ANY)
    kept = [saved(width, c) for c in cols] + [
        saved(slots, width),
        saved(slots, width),
        saved(slots, 3 * local_width),
        saved(slots, local_width),
        saved(slots, 128, dtype=F32),
        saved(slots, local_ff),
        saved(slots, local_ff),
        saved(block, width, dtype=F32),
        saved(block, width, dtype=F32),
    ]
    dma = pltpu.SemaphoreType.DMA
    return pl.pallas_call(
        functools.partial(forward_kernel, dims),
        out_shape=[
            jax.ShapeDtypeStruct((block, width), F32),
            jax.ShapeDtypeStruct((4 * layers, width), F32),
        ]
        + kept,
        in_specs=[smem, smem] + [vmem] * 6,
        out_specs=[vmem, vmem] + [hbm] * len(kept),
        scratch_shapes=[pltpu.VMEM(k.shape, k.dtype) for k in kept]
        + [
            pltpu.VMEM((block, local_ff), F32),
            pltpu.VMEM((yn, block, width), BF16),
            pltpu.VMEM((yn, block, width), BF16),
            pltpu.VMEM((yn - 1, block, width), BF16),
            pltpu.VMEM((yn - 1, block, width), BF16),
            pltpu.VMEM((block, width), F32),
            pltpu.VMEM((slot_count, 4 * layers, width), F32),
            dma((layers, 4, zn - 1)),
            dma((layers, 4, zn - 1)),
            dma((layers, 4, xn - 1, zn)),
            dma((layers, 4, xn - 1, zn)),
            dma((layers, 4)),
            dma((layers, 4)),
            dma((2 * layers, 2 * yn - 1)),
            dma((2 * layers, 2 * yn - 1)),
            dma((2 * layers, 2 * yn - 1)),
            dma((2 * layers, 2 * yn - 1)),
            dma((sem_count,)),
            dma((sem_count,)),
            dma((layers, 9)),
        ],
        compiler_params=pltpu.CompilerParams(
            collective_id=0, has_side_effects=True, vmem_limit_bytes=60 * 2**20
        ),
        name="forward_layers",
    )(lengths, slopes, x_in, norm_in, *shards)


def norm_back(hidden, gain, grad_out):
    centered = hidden - jnp.mean(hidden, axis=-1, keepdims=True)
    inverse = lax.rsqrt(jnp.mean(centered * centered, axis=-1, keepdims=True) + EPS_NORM)
    scaled = centered * inverse
    grad_scaled = grad_out * gain
    grad_hidden = inverse * (
        grad_scaled
        - jnp.mean(grad_scaled, axis=-1, keepdims=True)
        - scaled * jnp.mean(grad_scaled * scaled, axis=-1, keepdims=True)
    )
    return (grad_hidden, jnp.sum(grad_out * scaled, axis=0), jnp.sum(grad_out, axis=0))


def scatter_sum(part, axis_name, dimension):
    return lax.psum_scatter(
        part.astype(jnp.bfloat16), axis_name, scatter_dimension=dimension, tiled=True
    ).astype(jnp.float32)


def block_scores(query_block, key_rows, first_row, slopes, lengths):
    block_rows = query_block.shape[1]
    slot_count = key_rows.shape[1]
    raw = jnp.einsum(
        "rqhd,rkhd->rhqk", query_block, key_rows, preferred_element_type=jnp.float32
    ) * HD ** (-0.5)
    query_pos = first_row + jnp.arange(block_rows, dtype=jnp.int32)
    key_pos = jnp.arange(slot_count, dtype=jnp.int32)
    distance = jnp.broadcast_to(key_pos[None, :], (block_rows, slot_count)).astype(jnp.float32)
    raw = raw + slopes[None, :, None, None] * distance[None, None]
    causal = key_pos[None, :] <= query_pos[:, None]
    filled = key_pos[None, :] < lengths[:, None]
    allowed = causal[None, None] & filled[:, None, None, :]
    return jnp.where(allowed, raw, -jnp.inf)


def attend_backward(queries, key_rows, values, grad_context, log_total, slopes, lengths):
    row_count, slot_count, head_local, head_size = queries.shape
    block_rows = min(512, slot_count)
    score_scale = HD ** (-0.5)

    def one_block(block_index, carry):
        grad_queries, grad_keys, grad_values = carry
        first_row = block_index * block_rows
        query_block = lax.dynamic_slice_in_dim(queries, first_row, block_rows, 1)
        grad_block = lax.dynamic_slice_in_dim(grad_context, first_row, block_rows, 1)
        scores = block_scores(query_block, key_rows, first_row, slopes, lengths)
        block_total = lax.dynamic_slice_in_dim(log_total, first_row, block_rows, 2)
        attention = jnp.exp(scores - block_total[..., None])
        grad_attention = jnp.einsum(
            "rqhd,rkhd->rhqk", grad_block, values, preferred_element_type=jnp.float32
        )
        inner_sum = jnp.sum(attention * grad_attention, axis=3, keepdims=True)
        grad_scores = (attention * (grad_attention - inner_sum)).astype(jnp.bfloat16)
        block_grad = (
            jnp.einsum("rhqk,rkhd->rqhd", grad_scores, key_rows, preferred_element_type=jnp.float32)
            * score_scale
        ).astype(jnp.bfloat16)
        grad_queries = lax.dynamic_update_slice_in_dim(grad_queries, block_grad, first_row, 1)
        grad_keys = (
            grad_keys
            + jnp.einsum(
                "rhqk,rqhd->rkhd", grad_scores, query_block, preferred_element_type=jnp.float32
            )
            * score_scale
        )
        grad_values = grad_values + jnp.einsum(
            "rhqk,rqhd->rkhd",
            attention.astype(jnp.bfloat16),
            grad_block,
            preferred_element_type=jnp.float32,
        )
        return (grad_queries, grad_keys, grad_values)

    initial = (
        jnp.zeros(queries.shape, jnp.bfloat16),
        jnp.zeros(queries.shape, jnp.float32),
        jnp.zeros(queries.shape, jnp.float32),
    )
    return lax.fori_loop(0, slot_count // block_rows, one_block, initial)


def adam_update(master, grad, first, second, factor, fix_one, fix_two, decay, rate):
    clipped = grad * factor
    momentum = BETA_ONE * first + (1.0 - BETA_ONE) * clipped
    variance = BETA_TWO * second + (1.0 - BETA_TWO) * clipped * clipped
    step_size = momentum / fix_one / (jnp.sqrt(variance / fix_two) + ADAM_EPS) + decay * master
    fresh = master - rate * step_size
    return (momentum, variance, fresh, fresh.astype(jnp.bfloat16))


def body(
    block_input,
    output_grad,
    row_lengths,
    qkv_weight,
    proj_weight,
    up_weight,
    down_weight,
    norm_params,
    qkv_first,
    proj_first,
    up_first,
    down_first,
    norm_first,
    qkv_second,
    proj_second,
    up_second,
    down_second,
    norm_second,
):
    row_count, local_slots, width = block_input.shape
    seq_count = lax.axis_size("seq")
    groups = lax.axis_size("dp")
    layer_count = qkv_weight.shape[0]
    slots = local_slots * seq_count
    local_width = qkv_weight.shape[3]
    local_ff = up_weight.shape[2]
    head_local = local_width // HD
    dims = (
        layer_count, slots, width, local_slots, local_width, local_ff, groups,
        ZSIZE, groups // ZSIZE, seq_count // CORES,
    )
    head_ids = lax.axis_index("seq") * head_local + jnp.arange(head_local, dtype=jnp.int32)
    slopes = jnp.asarray(slope_table(H), F32)[head_ids]
    shards = (
        qkv_weight.astype(BF16).reshape(layer_count, -1, 3 * local_width),
        jnp.swapaxes(proj_weight.astype(BF16), 1, 2),
        up_weight.astype(BF16),
        jnp.swapaxes(down_weight.astype(BF16), 1, 2),
    )
    piece = norm_params.shape[2]
    device_at = lax.axis_index("dp") * seq_count + lax.axis_index("seq")
    norm_local = norm_params.astype(BF16).astype(F32).reshape(4 * layer_count, piece)
    norm_in = lax.dynamic_update_slice(
        jnp.zeros((4 * layer_count, width), F32), norm_local, (0, device_at * piece)
    )
    kept = run_forward(
        dims, row_lengths, slopes, block_input.reshape(local_slots, width), norm_in, shards
    )
    block_output = kept[0].reshape(row_count, local_slots, width)
    norm_all = kept[1].reshape(layer_count, 4, width)
    positions = lax.axis_index("seq") * local_slots + jnp.arange(local_slots, dtype=jnp.int32)
    token_mask = (positions[None, :] < row_lengths[:, None]).astype(jnp.float32)
    grad_hidden = (output_grad.astype(jnp.float32) * token_mask[:, :, None]).reshape(
        local_slots * row_count, width
    )
    reduced_all = [None] * layer_count
    norm_parts = [None] * layer_count
    for layer_index in reversed(range(layer_count)):
        (w_qkv, w_proj_t, w_up, w_down_t, normed_one, normed_two, qkv_rows, context_rows, log_all,
         act_low, act_slope, hidden_in, middle) = (item[layer_index] for item in kept[2:])
        norm_rows = norm_all[layer_index]
        spread = qkv_rows.reshape(row_count, slots, 3, head_local, HD)
        log_total = log_all[:, :head_local].T[None]
        grad_ffn = lax.all_gather(grad_hidden.astype(jnp.bfloat16), "seq", axis=0, tiled=True)
        down_grad = scatter_sum(
            jnp.einsum("tf,td->fd", act_low, grad_ffn, preferred_element_type=jnp.float32), "dp", 1
        )
        grad_act = jnp.einsum("td,df->tf", grad_ffn, w_down_t, preferred_element_type=jnp.float32)
        grad_upper = (grad_act * act_slope.astype(F32)).astype(jnp.bfloat16)
        up_grad = scatter_sum(
            jnp.einsum("td,tf->df", normed_two, grad_upper, preferred_element_type=jnp.float32),
            "dp", 0,
        )
        grad_normed_two = scatter_sum(
            jnp.einsum("tf,df->td", grad_upper, w_up, preferred_element_type=jnp.float32), "seq", 0
        )
        grad_middle_norm, gain_two, bias_two = norm_back(middle, norm_rows[2], grad_normed_two)
        grad_middle = grad_hidden + grad_middle_norm
        grad_branch = lax.all_gather(grad_middle.astype(jnp.bfloat16), "seq", axis=0, tiled=True)
        proj_grad = scatter_sum(
            jnp.einsum("td,te->de", context_rows, grad_branch, preferred_element_type=jnp.float32),
            "dp", 1,
        )
        grad_context = jnp.einsum(
            "te,ed->td", grad_branch, w_proj_t, preferred_element_type=jnp.float32
        ).astype(jnp.bfloat16)
        grad_context = grad_context.reshape(row_count, -1, head_local, HD)
        grad_queries, grad_keys, grad_values = attend_backward(
            spread[:, :, 0], spread[:, :, 1], spread[:, :, 2], grad_context, log_total, slopes,
            row_lengths,
        )
        grad_projected = jnp.stack(
            (grad_queries, grad_keys.astype(jnp.bfloat16), grad_values.astype(jnp.bfloat16)), axis=2
        ).reshape(-1, 3 * local_width)
        qkv_grad = scatter_sum(
            jnp.einsum("td,te->de", normed_one, grad_projected, preferred_element_type=jnp.float32),
            "dp", 0,
        ).reshape(-1, 3, local_width)
        grad_normed = scatter_sum(
            jnp.einsum("te,de->td", grad_projected, w_qkv, preferred_element_type=jnp.float32),
            "seq", 0,
        )
        grad_input_norm, gain_one, bias_one = norm_back(hidden_in, norm_rows[0], grad_normed)
        grad_hidden = grad_middle + grad_input_norm
        norm_parts[layer_index] = jnp.stack((gain_one, bias_one, gain_two, bias_two), axis=0)
        reduced_all[layer_index] = (qkv_grad, proj_grad, up_grad, down_grad)
    input_grad = grad_hidden.reshape(row_count, local_slots, width)
    norm_grad = lax.psum_scatter(
        jnp.stack(norm_parts, axis=0), ("dp", "seq"), scatter_dimension=2, tiled=True
    )
    stacked = [
        jnp.stack([layer_grads[position] for layer_grads in reduced_all], axis=0)
        for position in range(4)
    ] + [norm_grad]
    square_sum = (
        jnp.sum(stacked[0] * stacked[0])
        + jnp.sum(stacked[1] * stacked[1])
        + jnp.sum(stacked[2] * stacked[2])
        + jnp.sum(stacked[3] * stacked[3])
        + jnp.sum(stacked[4] * stacked[4])
    )
    grad_norm = jnp.sqrt(lax.psum(square_sum, ("dp", "seq")))
    factor = CLIP_NORM / jnp.maximum(grad_norm, CLIP_NORM)
    fix_one = 1.0 - BETA_ONE**STEP
    fix_two = 1.0 - BETA_TWO**STEP
    qkv_out = adam_update(
        qkv_weight,
        stacked[0],
        qkv_first,
        qkv_second,
        factor,
        fix_one,
        fix_two,
        WEIGHT_DECAY,
        LEARN_RATE,
    )
    proj_out = adam_update(
        proj_weight,
        stacked[1],
        proj_first,
        proj_second,
        factor,
        fix_one,
        fix_two,
        WEIGHT_DECAY,
        LEARN_RATE,
    )
    up_out = adam_update(
        up_weight,
        stacked[2],
        up_first,
        up_second,
        factor,
        fix_one,
        fix_two,
        WEIGHT_DECAY,
        LEARN_RATE,
    )
    down_out = adam_update(
        down_weight,
        stacked[3],
        down_first,
        down_second,
        factor,
        fix_one,
        fix_two,
        WEIGHT_DECAY,
        LEARN_RATE,
    )
    norm_out = adam_update(
        norm_params, stacked[4], norm_first, norm_second, factor, fix_one, fix_two, 0.0, NORM_RATE
    )
    return (
        block_output,
        input_grad,
        grad_norm,
        stacked[0],
        stacked[1],
        stacked[2],
        stacked[3],
        stacked[4],
        qkv_out[0],
        proj_out[0],
        up_out[0],
        down_out[0],
        norm_out[0],
        qkv_out[1],
        proj_out[1],
        up_out[1],
        down_out[1],
        norm_out[1],
        qkv_out[2],
        proj_out[2],
        up_out[2],
        down_out[2],
        norm_out[2],
        qkv_out[3],
        proj_out[3],
        up_out[3],
        down_out[3],
        norm_out[3],
    )


def solution(mesh):
    return jax.shard_map(
        body,
        mesh=mesh,
        in_specs=(
            P("dp", "seq", None),
            P("dp", "seq", None),
            P("dp"),
            P(None, "dp", None, "seq"),
            P(None, "seq", "dp"),
            P(None, "dp", "seq"),
            P(None, "seq", "dp"),
            P(None, None, ("dp", "seq")),
            P(None, "dp", None, "seq"),
            P(None, "seq", "dp"),
            P(None, "dp", "seq"),
            P(None, "seq", "dp"),
            P(None, None, ("dp", "seq")),
            P(None, "dp", None, "seq"),
            P(None, "seq", "dp"),
            P(None, "dp", "seq"),
            P(None, "seq", "dp"),
            P(None, None, ("dp", "seq")),
        ),
        out_specs=(
            P("dp", "seq", None),
            P("dp", "seq", None),
            P(),
            P(None, "dp", None, "seq"),
            P(None, "seq", "dp"),
            P(None, "dp", "seq"),
            P(None, "seq", "dp"),
            P(None, None, ("dp", "seq")),
            P(None, "dp", None, "seq"),
            P(None, "seq", "dp"),
            P(None, "dp", "seq"),
            P(None, "seq", "dp"),
            P(None, None, ("dp", "seq")),
            P(None, "dp", None, "seq"),
            P(None, "seq", "dp"),
            P(None, "dp", "seq"),
            P(None, "seq", "dp"),
            P(None, None, ("dp", "seq")),
            P(None, "dp", None, "seq"),
            P(None, "seq", "dp"),
            P(None, "dp", "seq"),
            P(None, "seq", "dp"),
            P(None, None, ("dp", "seq")),
            P(None, "dp", None, "seq"),
            P(None, "seq", "dp"),
            P(None, "dp", "seq"),
            P(None, "seq", "dp"),
            P(None, None, ("dp", "seq")),
        ),
        check_vma=False,
    )
```

```python
import functools

import jax
import jax.numpy as jnp
import numpy as np
from jax import lax
from jax.experimental import pallas as pl
from jax.experimental.pallas import tpu as pltpu
from jax.sharding import PartitionSpec as P

H = 8
HD = 128
STEP = 5
CORES = 2
ZSIZE = 4

EPS_NORM = 1e-05
BETA_ONE = 0.5
BETA_TWO = 0.75
LEARN_RATE = 0.03
NORM_RATE = 0.3
WEIGHT_DECAY = 0.1
CLIP_NORM = 0.1
ADAM_EPS = 1e-08

F32 = jnp.float32
BF16 = jnp.bfloat16
MESH = pl.DeviceIdType.MESH
SCORE_SCALE = HD ** (-0.5)
GELU_A = (2.0 / np.pi) ** 0.5
GELU_B = 0.044715


def slope_table(head_count):
    return np.power(2.0, -8.0 * (np.arange(head_count) + 1.0) / head_count)


def mm_nn(a, b):
    return lax.dot_general(a, b, (((1,), (0,)), ((), ())), preferred_element_type=F32)


def mm_nt(a, b):
    return lax.dot_general(a, b, (((1,), (1,)), ((), ())), preferred_element_type=F32)


def mm_tn(a, b):
    return lax.dot_general(a, b, (((0,), (0,)), ((), ())), preferred_element_type=F32)


def normalise(v):
    centered = v - jnp.mean(v, axis=-1, keepdims=True)
    inverse = lax.rsqrt(jnp.mean(centered * centered, axis=-1, keepdims=True) + EPS_NORM)
    return centered * inverse, inverse


def rows_of(index, size):
    return pl.ds(pl.multiple_of(index * size, size), size)


class Place:
    def __init__(self, zn, xn, yn):
        self.zn, self.xn, self.yn = zn, xn, yn
        self.dp = lax.axis_index("dp")
        self.seq = lax.axis_index("seq")
        self.z, self.x = self.dp // xn, lax.rem(self.dp, xn)
        self.y, self.c = self.seq // CORES, lax.rem(self.seq, CORES)

    def zo(self, k):
        return lax.rem(self.z + k + self.zn, self.zn)

    def xo(self, k):
        return lax.rem(self.x + k + self.xn, self.xn)

    def yo(self, k):
        return lax.rem(self.y + k + self.yn, self.yn)

    def dev(self, dz=0, dx=0, dy=0, dc=0):
        core = (1 - self.c) if dc else self.c
        return (self.zo(dz) * self.xn + self.xo(dx), self.yo(dy) * CORES + core)

    def dp_at(self, dz, dx):
        return self.zo(dz) * self.xn + self.xo(dx)

    def seq_at(self, dy, dc):
        core = (1 - self.c) if dc else self.c
        return self.yo(dy) * CORES + core

    def peers(self):
        out = [self.dev(dc=1)]
        out += [self.dev(dy=k) for k in range(1, self.yn)]
        out += [self.dev(dx=k) for k in range(1, self.xn)]
        out += [self.dev(dz=k) for k in range(1, self.zn)]
        return out

    def barrier(self):
        sem = pltpu.get_barrier_semaphore()
        peers = self.peers()
        for peer in peers:
            pl.semaphore_signal(sem, inc=1, device_id=peer, device_id_type=MESH)
        pl.semaphore_wait(sem, len(peers))


def near_first(count):
    order = []
    for k in range(1, count):
        order.append((min(k, count - k), k))
    return [k for unused, k in sorted(order)]


def remote(src, dst, send, recv, dev):
    return pltpu.make_async_remote_copy(
        src_ref=src, dst_ref=dst, send_sem=send, recv_sem=recv, device_id=dev, device_id_type=MESH
    )


def all_sum(place, value, slots, send, recv):
    stages = (
        (CORES, place.c, lambda k: place.dev(dc=1), lambda k: 1 - place.c),
        (place.yn, place.y, lambda k: place.dev(dy=k), lambda k: place.yo(-k)),
        (place.xn, place.x, lambda k: place.dev(dx=k), lambda k: place.xo(-k)),
        (place.zn, place.z, lambda k: place.dev(dz=k), lambda k: place.zo(-k)),
    )
    base = 0
    at = 0
    for size, mine, target, origin in stages:
        slots[base + mine] = value
        own = slots.at[base + mine]
        for k in range(1, size):
            remote(own, own, send.at[at + k - 1], recv.at[at + k - 1], target(k)).start()
        for k in range(1, size):
            came = slots.at[base + origin(k)]
            remote(came, came, send.at[at + k - 1], recv.at[at + k - 1], target(k)).wait_recv()
        for k in range(1, size):
            remote(own, own, send.at[at + k - 1], recv.at[at + k - 1], target(k)).wait_send()
        value = slots[base]
        for k in range(1, size):
            value = value + slots[base + k]
        base += size
        at += size - 1
    return value


def sum_slots(zn, xn, yn):
    return CORES + yn + xn + zn, 1 + (yn - 1) + (xn - 1) + (zn - 1)


class Gather:
    def __init__(self, place, buf, block, send, recv):
        self.p, self.buf, self.block, self.send, self.recv = place, buf, block, send, recv

    def at(self, dy, dc):
        return self.buf.at[rows_of(self.p.seq_at(dy, dc), self.block)]

    def start(self):
        p, own = self.p, self.at(0, 0)
        for k in range(1, p.yn):
            remote(own, own, self.send.at[k], self.recv.at[k], p.dev(dy=k)).start()
        remote(own, own, self.send.at[0], self.recv.at[0], p.dev(dc=1)).start()

    def wait_chip(self):
        came = self.at(0, 1)
        remote(came, came, self.send.at[0], self.recv.at[0], self.p.dev(dc=1)).wait_recv()

    def forward(self):
        p = self.p
        for k in range(1, p.yn):
            came = self.at(-k, 0)
            remote(came, came, self.send.at[k], self.recv.at[k], p.dev(dy=k)).wait_recv()
            f = p.yn - 1 + k
            remote(came, came, self.send.at[f], self.recv.at[f], p.dev(dc=1)).start()

    def wait_rest(self):
        p = self.p
        for k in range(1, p.yn):
            f = p.yn - 1 + k
            came = self.at(-k, 1)
            remote(came, came, self.send.at[f], self.recv.at[f], p.dev(dc=1)).wait_recv()
        own = self.at(0, 0)
        for k in range(1, p.yn):
            remote(own, own, self.send.at[k], self.recv.at[k], p.dev(dy=k)).wait_send()
            f = p.yn - 1 + k
            sent = self.at(-k, 0)
            remote(sent, sent, self.send.at[f], self.recv.at[f], p.dev(dc=1)).wait_send()
        remote(own, own, self.send.at[0], self.recv.at[0], p.dev(dc=1)).wait_send()


class Scatter:
    def __init__(self, place, sbuf, rbuf, ysend, yrecv, acc, send, recv):
        self.p = place
        self.sbuf, self.rbuf, self.ysend, self.yrecv, self.acc = sbuf, rbuf, ysend, yrecv, acc
        self.send, self.recv = send, recv

    def core(self, k):
        return remote(
            self.sbuf.at[k], self.rbuf.at[k], self.send.at[k], self.recv.at[k], self.p.dev(dc=1)
        )

    def cross(self, k):
        s = self.p.yn + k - 1
        return remote(
            self.ysend.at[k - 1],
            self.yrecv.at[k - 1],
            self.send.at[s],
            self.recv.at[s],
            self.p.dev(dy=k),
        )

    def start(self, part):
        p = self.p
        for k in list(range(1, p.yn)) + [0]:
            self.sbuf[k] = part(p.seq_at(k, 1)).astype(BF16)
            self.core(k).start()
            mine = part(p.seq_at(k, 0))
            self.core(k).wait_recv()
            mine = mine + self.rbuf[k].astype(F32)
            if k:
                self.ysend[k - 1] = mine.astype(BF16)
                self.cross(k).start()
            else:
                self.acc[...] = mine

    def wait(self):
        p = self.p
        for k in range(1, p.yn):
            self.cross(k).wait_recv()
        for k in range(1, p.yn):
            self.cross(k).wait_send()
        for k in range(p.yn):
            self.core(k).wait_send()

    def rows(self, at):
        value = self.acc[at, :]
        for k in range(1, self.p.yn):
            value = value + self.yrecv[k - 1, at, :].astype(F32)
        return value


def row_loop(total, step, fn):
    def one(i, unused):
        fn(rows_of(i, step))
        return unused

    lax.fori_loop(0, total // step, one, 0)


def forward_kernel(dims, *refs):
    (layers, slots, width, block, local_width, local_ff, groups, zn, xn, yn) = dims
    heads = local_width // HD
    shard = width // groups
    refs = list(refs)

    def take(count):
        out = refs[:count]
        del refs[:count]
        return out

    lengths, slopes, x_in, norm_in = take(4)
    ws = take(4)
    out, norm_out = take(2)
    w_save = take(4)
    xn1_save, xn2_save, qkv_save, ctx_save, lse_save, act_save, dact_save, hid_save, mid_save = take(9)
    w = take(4)
    xn1, xn2, qkv, ctx, lse, act, dact, hid, mid, upper = take(10)
    sbuf, rbuf, ysend, yrecv, acc, nslots = take(6)
    zsend, zrecv, xsend, xrecv, own_sem, wsave_sem = take(6)
    ag_send, ag_recv, rs_send, rs_recv, ns_send, ns_recv, save_sem = take(7)

    p = Place(zn, xn, yn)
    z_order = near_first(zn)
    length = lengths[0]

    def shard_rows(index):
        return rows_of(index, shard)

    def z_copy(l, k, dz):
        at = shard_rows(p.dp)
        return remote(
            ws[k].at[l], w[k].at[l, at], zsend.at[l, k, dz - 1], zrecv.at[l, k, dz - 1], p.dev(dz=dz)
        )

    def z_came(l, k, dz):
        at = shard_rows(p.dp_at(-dz, 0))
        return remote(
            ws[k].at[l], w[k].at[l, at], zsend.at[l, k, dz - 1], zrecv.at[l, k, dz - 1], p.dev(dz=dz)
        )

    def x_copy(l, k, dx, dz):
        at = shard_rows(p.dp_at(-dz, 0))
        src = w[k].at[l, at] if dz else ws[k].at[l]
        return remote(
            src, w[k].at[l, at], xsend.at[l, k, dx - 1, dz], xrecv.at[l, k, dx - 1, dz], p.dev(dx=dx)
        )

    def x_came(l, k, dx, dz):
        at = shard_rows(p.dp_at(-dz, -dx))
        return remote(
            ws[k].at[l],
            w[k].at[l, at],
            xsend.at[l, k, dx - 1, dz],
            xrecv.at[l, k, dx - 1, dz],
            p.dev(dx=dx),
        )

    def own_copy(l, k):
        return pltpu.make_async_copy(ws[k].at[l], w[k].at[l, shard_rows(p.dp)], own_sem.at[l, k])

    def start_own(l, k):
        for dz in z_order:
            z_copy(l, k, dz).start()
        for dx in range(1, xn):
            x_copy(l, k, dx, 0).start()
        own_copy(l, k).start()

    def pump(l, k):
        for dz in z_order:
            z_came(l, k, dz).wait_recv()
            for dx in range(1, xn):
                x_copy(l, k, dx, dz).start()

    def save_weight(l, k):
        return pltpu.make_async_copy(w[k].at[l], w_save[k].at[l], wsave_sem.at[l, k])

    def need(l, k):
        own_copy(l, k).wait()
        for dz in [0] + z_order:
            for dx in range(1, xn):
                x_came(l, k, dx, dz).wait_recv()
        save_weight(l, k).start()

    def finish_weight(l, k):
        for dz in z_order:
            z_copy(l, k, dz).wait_send()
        for dz in range(zn):
            for dx in range(1, xn):
                x_copy(l, k, dx, dz).wait_send()
        save_weight(l, k).wait()

    def save(l, which, src, dst):
        return pltpu.make_async_copy(src, dst, save_sem.at[l, which])

    def saves(l):
        return (
            save(l, 0, xn1.at[l], xn1_save.at[l]),
            save(l, 1, xn2.at[l], xn2_save.at[l]),
            save(l, 2, qkv.at[l], qkv_save.at[l]),
            save(l, 3, ctx.at[l], ctx_save.at[l]),
            save(l, 4, lse.at[l], lse_save.at[l]),
            save(l, 5, act.at[l], act_save.at[l]),
            save(l, 6, dact.at[l], dact_save.at[l]),
            save(l, 7, hid.at[l], hid_save.at[l]),
            save(l, 8, mid.at[l], mid_save.at[l]),
        )

    p.barrier()
    start_own(0, 0)
    start_own(0, 1)
    norm_out[...] = all_sum(p, norm_in[...], nslots, ns_send, ns_recv)

    def load_in(at):
        hid[0, at, :] = x_in[at, :].astype(F32)

    row_loop(block, 64, load_in)
    first = p.seq * block

    def norm_row(index):
        return norm_out[pl.ds(index, 1), :]

    def norm_into(l, source, target, row):
        gain, bias = norm_row(4 * l + row), norm_row(4 * l + row + 1)

        def one(i, unused):
            scaled, inverse = normalise(source[l, rows_of(i, 32), :])
            at = pl.ds(pl.multiple_of(first + i * 32, 32), 32)
            target[l, at, :] = (scaled * gain + bias).astype(BF16)
            return unused

        lax.fori_loop(0, block // 32, one, 0)

    def attention(l):
        key_at = lax.broadcasted_iota(jnp.int32, (1, slots), 1)
        step = 256
        causal = lax.broadcasted_iota(jnp.int32, (step, step), 1) <= lax.broadcasted_iota(
            jnp.int32, (step, step), 0
        )
        for h in range(heads):
            bias = jnp.where(key_at < length, slopes[h] * key_at.astype(F32), -jnp.inf)
            cols = pl.ds(h * HD, HD)
            for b in range(slots // step):
                here = pl.ds(b * step, step)
                before = pl.ds(0, b * step)
                k_cols = pl.ds(local_width + h * HD, HD)
                v_cols = pl.ds(2 * local_width + h * HD, HD)
                q = qkv[l, here, cols]
                raw = mm_nt(q, qkv[l, here, k_cols]) * SCORE_SCALE + bias[:, b * step : (b + 1) * step]
                raw = jnp.where(causal, raw, -jnp.inf)
                top = jnp.max(raw, axis=1, keepdims=True)
                if b:
                    past = mm_nt(q, qkv[l, before, k_cols]) * SCORE_SCALE + bias[:, : b * step]
                    top = jnp.maximum(top, jnp.max(past, axis=1, keepdims=True))
                e_here = jnp.exp(raw - top)
                total = jnp.sum(e_here, axis=1, keepdims=True)
                value = mm_nn(e_here.astype(BF16), qkv[l, here, v_cols])
                if b:
                    e_past = jnp.exp(past - top)
                    total = total + jnp.sum(e_past, axis=1, keepdims=True)
                    value = value + mm_nn(e_past.astype(BF16), qkv[l, before, v_cols])
                ctx[l, here, cols] = (value / total).astype(BF16)
                lse[l, here, pl.ds(h, 1)] = top + jnp.log(total)

    def layer(l, unused):
        last = layers - 1
        g_one = Gather(p, xn1.at[l], block, ag_send.at[2 * l], ag_recv.at[2 * l])
        g_two = Gather(p, xn2.at[l], block, ag_send.at[2 * l + 1], ag_recv.at[2 * l + 1])
        rs = [
            Scatter(
                p, sbuf, rbuf, ysend, yrecv, acc,
                rs_send.at[2 * l + i], rs_recv.at[2 * l + i],
            )
            for i in range(2)
        ]
        save_at = saves(l)
        save_at[7].start()
        norm_into(l, hid, xn1, 0)
        g_one.start()

        @pl.when(l == 0)
        def _():
            pump(0, 0)
            start_own(0, 2)

        def project(index):
            at = rows_of(index, block)
            qkv[l, at, :] = mm_nn(xn1[l, at, :], w[0][l]).astype(BF16)

        g_one.wait_chip()
        g_one.forward()
        need(l, 0)
        project(p.seq_at(0, 0))
        project(p.seq_at(0, 1))
        g_one.wait_rest()
        save_at[0].start()
        for k in range(1, yn):
            project(p.seq_at(-k, 0))
            project(p.seq_at(-k, 1))
        save_at[2].start()
        attention(l)
        save_at[3].start()
        save_at[4].start()
        pump(l, 1)
        start_own(l, 3)
        need(l, 1)
        rs[0].start(lambda b: mm_nt(ctx[l, rows_of(b, block), :], w[1][l]))
        pump(l, 2)

        @pl.when(l < last)
        def _():
            start_own(l + 1, 0)

        rs[0].wait()

        def add_middle(at):
            mid[l, at, :] = hid[l, at, :] + rs[0].rows(at)

        row_loop(block, 32, add_middle)
        save_at[8].start()
        norm_into(l, mid, xn2, 2)
        g_two.start()
        need(l, 2)

        def expand(index):
            base = pl.multiple_of(index * block, block)
            upper[...] = mm_nn(xn2[l, pl.ds(base, block), :], w[2][l])

            def one(i, unused):
                u = upper[rows_of(i, 16), :]
                at = pl.ds(pl.multiple_of(base + i * 16, 16), 16)
                square = u * u
                t = jnp.tanh(GELU_A * u * (1.0 + GELU_B * square))
                half = 0.5 * (1.0 + t)
                act[l, at, :] = (u * half).astype(BF16)
                slope = (0.5 * GELU_A) * u * (1.0 - t * t) * (1.0 + (3.0 * GELU_B) * square)
                dact[l, at, :] = (half + slope).astype(BF16)
                return unused

            lax.fori_loop(0, block // 16, one, 0)

        expand(p.seq_at(0, 0))
        g_two.wait_chip()
        expand(p.seq_at(0, 1))
        g_two.forward()
        pump(l, 3)

        @pl.when(l < last)
        def _():
            start_own(l + 1, 1)

        g_two.wait_rest()
        save_at[1].start()
        for k in range(1, yn):
            expand(p.seq_at(-k, 0))
            expand(p.seq_at(-k, 1))
        save_at[5].start()
        save_at[6].start()
        need(l, 3)
        rs[1].start(lambda b: mm_nt(act[l, rows_of(b, block), :], w[3][l]))

        @pl.when(l < last)
        def _():
            pump(l + 1, 0)
            start_own(l + 1, 2)

        rs[1].wait()

        @pl.when(l < last)
        def _():
            def add_next(at):
                hid[l + 1, at, :] = mid[l, at, :] + rs[1].rows(at)

            row_loop(block, 32, add_next)

        @pl.when(l == last)
        def _():
            def add_out(at):
                out[at, :] = mid[l, at, :] + rs[1].rows(at)

            row_loop(block, 32, add_out)

        return unused

    lax.fori_loop(0, layers, layer, 0)

    def finish(l, unused):
        for k in range(4):
            finish_weight(l, k)
        for item in saves(l):
            item.wait()
        return unused

    lax.fori_loop(0, layers, finish, 0)


def run_forward(dims, lengths, slopes, x_in, norm_in, shards):
    (layers, slots, width, block, local_width, local_ff, groups, zn, xn, yn) = dims
    cols = (3 * local_width, local_width, local_ff, local_ff)
    slot_count, sem_count = sum_slots(zn, xn, yn)

    def saved(*shape, dtype=BF16):
        return jax.ShapeDtypeStruct((layers,) + shape, dtype)

    vmem = pl.BlockSpec(memory_space=pltpu.VMEM)
    smem = pl.BlockSpec(memory_space=pltpu.SMEM)
    hbm = pl.BlockSpec(memory_space=pl.ANY)
    kept = [saved(width, c) for c in cols] + [
        saved(slots, width),
        saved(slots, width),
        saved(slots, 3 * local_width),
        saved(slots, local_width),
        saved(slots, 128, dtype=F32),
        saved(slots, local_ff),
        saved(slots, local_ff),
        saved(block, width, dtype=F32),
        saved(block, width, dtype=F32),
    ]
    dma = pltpu.SemaphoreType.DMA
    return pl.pallas_call(
        functools.partial(forward_kernel, dims),
        out_shape=[
            jax.ShapeDtypeStruct((block, width), F32),
            jax.ShapeDtypeStruct((4 * layers, width), F32),
        ]
        + kept,
        in_specs=[smem, smem] + [vmem] * 6,
        out_specs=[vmem, vmem] + [hbm] * len(kept),
        scratch_shapes=[pltpu.VMEM(k.shape, k.dtype) for k in kept]
        + [
            pltpu.VMEM((block, local_ff), F32),
            pltpu.VMEM((yn, block, width), BF16),
            pltpu.VMEM((yn, block, width), BF16),
            pltpu.VMEM((yn - 1, block, width), BF16),
            pltpu.VMEM((yn - 1, block, width), BF16),
            pltpu.VMEM((block, width), F32),
            pltpu.VMEM((slot_count, 4 * layers, width), F32),
            dma((layers, 4, zn - 1)),
            dma((layers, 4, zn - 1)),
            dma((layers, 4, xn - 1, zn)),
            dma((layers, 4, xn - 1, zn)),
            dma((layers, 4)),
            dma((layers, 4)),
            dma((2 * layers, 2 * yn - 1)),
            dma((2 * layers, 2 * yn - 1)),
            dma((2 * layers, 2 * yn - 1)),
            dma((2 * layers, 2 * yn - 1)),
            dma((sem_count,)),
            dma((sem_count,)),
            dma((layers, 9)),
        ],
        compiler_params=pltpu.CompilerParams(
            collective_id=0, has_side_effects=True, vmem_limit_bytes=60 * 2**20
        ),
        name="forward_layers",
    )(lengths, slopes, x_in, norm_in, *shards)


def backward_kernel(dims, *refs):
    (layers, slots, width, block, local_width, local_ff, groups, zn, xn, yn) = dims
    heads = local_width // HD
    shard = width // groups
    slab = shard * xn
    refs = list(refs)

    def take(count):
        out = refs[:count]
        del refs[:count]
        return out

    lengths, slopes, g_in, norms = take(4)
    kept = take(13)
    g_out, norm_grad, total_out = take(3)
    shards = take(4)
    held = take(13)
    w = held[:4]
    xn1, xn2, qkv, ctx, lse, act, dact, hid, mid = held[4:]
    gfull, gbfull, gctx, dqkv, dk, dv, g, gm, npart = take(9)
    dw = take(4)
    xland = take(4)
    zland = take(4)
    sbuf, rbuf, ysend, yrecv, acc, nslots, tslots = take(7)
    zsend, zrecv, xsend, xrecv = take(4)
    ag_send, ag_recv, rs_send, rs_recv, ns_send, ns_recv, ts_send, ts_recv, load_sem = take(9)

    p = Place(zn, xn, yn)
    length = lengths[0]
    first = p.seq * block
    gu = dact

    def load(l, which):
        return pltpu.make_async_copy(kept[which].at[l], held[which], load_sem.at[which])

    def rows_at(dz, dx):
        return rows_of(p.dp_at(dz, dx), shard)

    def x_copy(l, k, zi, dx):
        return remote(
            dw[k].at[rows_at(zi, dx)],
            xland[k].at[l, dx - 1, zi],
            xsend.at[l, k, dx - 1, zi],
            xrecv.at[l, k, dx - 1, zi],
            p.dev(dx=dx),
        )

    def z_copy(l, k, zi):
        return remote(
            dw[k].at[rows_at(zi, 0)],
            zland[k].at[l, zi - 1],
            zsend.at[l, k, zi - 1],
            zrecv.at[l, k, zi - 1],
            p.dev(dz=zi),
        )

    z_order = near_first(zn)

    def weight_grad(l, k, left, right):
        for zi in z_order[::-1] + [0]:
            at = rows_of(p.zo(zi), slab)
            dw[k][at, :] = mm_tn(left[:, at], right[...]).astype(BF16)
            for dx in range(1, xn):
                x_copy(l, k, zi, dx).start()

    def reduce_x(l, k):
        for zi in z_order[::-1] + [0]:
            for dx in range(1, xn):
                x_copy(l, k, zi, dx).wait_recv()
            base = pl.multiple_of(p.dp_at(zi, 0) * shard, shard)

            def one(i, unused):
                here = rows_of(i, 16)
                at = pl.ds(pl.multiple_of(base + i * 16, 16), 16)
                value = dw[k][at, :].astype(F32)
                for dx in range(1, xn):
                    value = value + xland[k][l, dx - 1, zi, here, :].astype(F32)
                if zi:
                    dw[k][at, :] = value.astype(BF16)
                else:
                    shards[k][l, here, :] = value
                return unused

            lax.fori_loop(0, shard // 16, one, 0)
            if zi:
                z_copy(l, k, zi).start()

    def reduce_z(l, k):
        for zi in z_order:
            z_copy(l, k, zi).wait_recv()

        def one(at):
            value = shards[k][l, at, :]
            for zi in range(1, zn):
                value = value + zland[k][l, zi - 1, at, :].astype(F32)
            shards[k][l, at, :] = value

        row_loop(shard, 16, one)
        for zi in z_order:
            z_copy(l, k, zi).wait_send()
        for zi in range(zn):
            for dx in range(1, xn):
                x_copy(l, k, zi, dx).wait_send()

    def norm_back(l, source, rs, base, row, target, low):
        gain = norms[pl.ds(4 * l + row, 1), :]
        zero = jnp.zeros((8, width), F32)

        def one(i, carry):
            at = rows_of(i, 32)
            scaled, inverse = normalise(source[at, :])
            e = rs.rows(at)
            eg = e * gain
            part = inverse * (
                eg
                - jnp.mean(eg, axis=-1, keepdims=True)
                - scaled * jnp.mean(eg * scaled, axis=-1, keepdims=True)
            )
            value = base[at, :] + part
            target[at, :] = value
            if low is not None:
                low[pl.ds(pl.multiple_of(first + i * 32, 32), 32), :] = value.astype(BF16)
            es = e * scaled
            gains, biases = carry
            for r in range(4):
                gains = gains + es[r * 8 : r * 8 + 8]
                biases = biases + e[r * 8 : r * 8 + 8]
            return gains, biases

        gains, biases = lax.fori_loop(0, block // 32, one, (zero, zero))
        npart[pl.ds(4 * l + row, 1), :] = jnp.sum(gains, axis=0, keepdims=True)
        npart[pl.ds(4 * l + row + 1, 1), :] = jnp.sum(biases, axis=0, keepdims=True)

    def attention():
        key_at = lax.broadcasted_iota(jnp.int32, (1, slots), 1)
        step = 256
        causal = lax.broadcasted_iota(jnp.int32, (step, step), 1) <= lax.broadcasted_iota(
            jnp.int32, (step, step), 0
        )
        for h in range(heads):
            bias = jnp.where(key_at < length, slopes[h] * key_at.astype(F32), -jnp.inf)
            cols = pl.ds(h * HD, HD)
            k_cols = pl.ds(local_width + h * HD, HD)
            v_cols = pl.ds(2 * local_width + h * HD, HD)
            for b in range(slots // step):
                here = pl.ds(b * step, step)
                before = pl.ds(0, b * step)
                q = qkv[here, cols]
                gc = gctx[here, cols]
                shift = lse[here, pl.ds(h, 1)]
                raw = mm_nt(q, qkv[here, k_cols]) * SCORE_SCALE + bias[:, b * step : (b + 1) * step]
                p_here = jnp.exp(jnp.where(causal, raw, -jnp.inf) - shift)
                dp_here = mm_nt(gc, qkv[here, v_cols])
                delta = jnp.sum(p_here * dp_here, axis=1, keepdims=True)
                dv[here, :] = mm_tn(p_here.astype(BF16), gc)
                if b:
                    past = mm_nt(q, qkv[before, k_cols]) * SCORE_SCALE + bias[:, : b * step]
                    p_past = jnp.exp(past - shift)
                    dp_past = mm_nt(gc, qkv[before, v_cols])
                    delta = delta + jnp.sum(p_past * dp_past, axis=1, keepdims=True)
                    dv[before, :] += mm_tn(p_past.astype(BF16), gc)
                ds_here = (p_here * (dp_here - delta)).astype(BF16)
                dq = mm_nn(ds_here, qkv[here, k_cols])
                dk[here, :] = mm_tn(ds_here, q)
                if b:
                    ds_past = (p_past * (dp_past - delta)).astype(BF16)
                    dq = dq + mm_nn(ds_past, qkv[before, k_cols])
                    dk[before, :] += mm_tn(ds_past, q)
                dqkv[here, cols] = (dq * SCORE_SCALE).astype(BF16)

            def store(at):
                dqkv[at, k_cols] = (dk[at, :] * SCORE_SCALE).astype(BF16)
                dqkv[at, v_cols] = dv[at, :].astype(BF16)

            row_loop(slots, 64, store)

    p.barrier()

    def mask_in(i, unused):
        at = rows_of(i, 32)
        slot = first + i * 32 + lax.broadcasted_iota(jnp.int32, (32, 1), 0)
        g[at, :] = jnp.where(slot < length, g_in[at, :].astype(F32), 0.0)
        return unused

    lax.fori_loop(0, block // 32, mask_in, 0)
    load_order = (3, 10, 2, 9, 5, 12, 1, 7, 6, 8, 0, 4, 11)

    def layer(step, unused):
        l = layers - 1 - step
        later = l + 1
        for which in load_order:
            load(l, which).start()
        g_one = Gather(p, gfull, block, ag_send.at[2 * l], ag_recv.at[2 * l])
        g_two = Gather(p, gbfull, block, ag_send.at[2 * l + 1], ag_recv.at[2 * l + 1])
        rs = [
            Scatter(
                p, sbuf, rbuf, ysend, yrecv, acc, rs_send.at[2 * l + i], rs_recv.at[2 * l + i]
            )
            for i in range(2)
        ]

        def low_in(i, unused):
            at = pl.ds(pl.multiple_of(first + i * 32, 32), 32)
            gfull[at, :] = g[rows_of(i, 32), :].astype(BF16)
            return unused

        lax.fori_loop(0, block // 32, low_in, 0)
        g_one.start()

        @pl.when(step > 0)
        def _():
            reduce_x(later, 0)
            reduce_z(later, 2)

        load(l, 3).wait()
        load(l, 10).wait()

        def upper_grad(index):
            at = rows_of(index, block)
            value = mm_nn(gfull[at, :], w[3][...])
            gu[at, :] = (value * dact[at, :].astype(F32)).astype(BF16)

        upper_grad(p.seq_at(0, 0))
        g_one.wait_chip()
        upper_grad(p.seq_at(0, 1))
        g_one.forward()

        @pl.when(step > 0)
        def _():
            reduce_z(later, 1)

        g_one.wait_rest()
        for k in range(1, yn):
            upper_grad(p.seq_at(-k, 0))
            upper_grad(p.seq_at(-k, 1))
        load(l, 2).wait()
        rs[0].start(lambda b: mm_nt(gu[rows_of(b, block), :], w[2][...]))
        load(l, 9).wait()
        load(l, 5).wait()
        weight_grad(l, 3, gfull, act)
        weight_grad(l, 2, xn2, gu)
        load(l, 12).wait()
        rs[0].wait()
        norm_back(l, mid, rs[0], g, 2, gm, gbfull)
        g_two.start()
        reduce_x(l, 3)
        load(l, 1).wait()

        def context_grad(index):
            at = rows_of(index, block)
            gctx[at, :] = mm_nn(gbfull[at, :], w[1][...]).astype(BF16)

        context_grad(p.seq_at(0, 0))
        g_two.wait_chip()
        context_grad(p.seq_at(0, 1))
        g_two.forward()

        @pl.when(step > 0)
        def _():
            reduce_z(later, 0)

        g_two.wait_rest()
        for k in range(1, yn):
            context_grad(p.seq_at(-k, 0))
            context_grad(p.seq_at(-k, 1))
        load(l, 7).wait()
        weight_grad(l, 1, gbfull, ctx)
        load(l, 6).wait()
        load(l, 8).wait()
        attention()
        reduce_x(l, 2)
        load(l, 0).wait()
        rs[1].start(lambda b: mm_nt(dqkv[rows_of(b, block), :], w[0][...]))
        load(l, 4).wait()
        weight_grad(l, 0, xn1, dqkv)
        reduce_x(l, 1)
        reduce_z(l, 3)
        load(l, 11).wait()
        rs[1].wait()
        norm_back(l, hid, rs[1], gm, 0, g, None)
        return unused

    lax.fori_loop(0, layers, layer, 0)
    g_out[...] = g[...]
    norm_total = all_sum(p, npart[...], nslots, ns_send, ns_recv)
    norm_grad[...] = norm_total
    reduce_x(0, 0)
    reduce_z(0, 2)
    reduce_z(0, 1)
    reduce_z(0, 0)

    def squares(k, start):
        cols = shards[k].shape[2]

        def one(i, total):
            l, at = i // (shard // 8), rows_of(lax.rem(i, shard // 8), 8)
            value = shards[k][l, at, :]
            value = value * value
            for c in range(cols // 128):
                total = total + value[:, c * 128 : (c + 1) * 128]
            return total

        return lax.fori_loop(0, layers * shard // 8, one, start)

    tile = jnp.zeros((8, 128), F32)
    for k in range(4):
        tile = squares(k, tile)
    tile = all_sum(p, tile, tslots, ts_send, ts_recv)
    value = norm_grad[...]
    value = value * value
    for c in range(width // 128):
        piece = value[:, c * 128 : (c + 1) * 128]
        for r in range(4 * layers // 8):
            tile = tile + piece[r * 8 : r * 8 + 8]
    total = jnp.sum(jnp.sum(tile, axis=0, keepdims=True), axis=1, keepdims=True)
    total_out[...] = jnp.broadcast_to(jnp.sqrt(total), (8, 128))


def run_backward(dims, lengths, slopes, g_in, norms, kept):
    (layers, slots, width, block, local_width, local_ff, groups, zn, xn, yn) = dims
    cols = (3 * local_width, local_width, local_ff, local_ff)
    shard = width // groups
    slot_count, sem_count = sum_slots(zn, xn, yn)
    vmem = pl.BlockSpec(memory_space=pltpu.VMEM)
    smem = pl.BlockSpec(memory_space=pltpu.SMEM)
    hbm = pl.BlockSpec(memory_space=pl.ANY)
    dma = pltpu.SemaphoreType.DMA
    return pl.pallas_call(
        functools.partial(backward_kernel, dims),
        out_shape=[
            jax.ShapeDtypeStruct((block, width), F32),
            jax.ShapeDtypeStruct((4 * layers, width), F32),
            jax.ShapeDtypeStruct((8, 128), F32),
        ]
        + [jax.ShapeDtypeStruct((layers, shard, c), F32) for c in cols],
        in_specs=[smem, smem, vmem, vmem] + [hbm] * len(kept),
        out_specs=[vmem] * 7,
        scratch_shapes=[pltpu.VMEM(k.shape[1:], k.dtype) for k in kept]
        + [
            pltpu.VMEM((slots, width), BF16),
            pltpu.VMEM((slots, width), BF16),
            pltpu.VMEM((slots, local_width), BF16),
            pltpu.VMEM((slots, 3 * local_width), BF16),
            pltpu.VMEM((slots, HD), F32),
            pltpu.VMEM((slots, HD), F32),
            pltpu.VMEM((block, width), F32),
            pltpu.VMEM((block, width), F32),
            pltpu.VMEM((4 * layers, width), F32),
        ]
        + [pltpu.VMEM((width, c), BF16) for c in cols]
        + [pltpu.VMEM((layers, xn - 1, zn, shard, c), BF16) for c in cols]
        + [pltpu.VMEM((layers, zn - 1, shard, c), BF16) for c in cols]
        + [
            pltpu.VMEM((yn, block, width), BF16),
            pltpu.VMEM((yn, block, width), BF16),
            pltpu.VMEM((yn - 1, block, width), BF16),
            pltpu.VMEM((yn - 1, block, width), BF16),
            pltpu.VMEM((block, width), F32),
            pltpu.VMEM((slot_count, 4 * layers, width), F32),
            pltpu.VMEM((slot_count, 8, 128), F32),
            dma((layers, 4, zn - 1)),
            dma((layers, 4, zn - 1)),
            dma((layers, 4, xn - 1, zn)),
            dma((layers, 4, xn - 1, zn)),
            dma((2 * layers, 2 * yn - 1)),
            dma((2 * layers, 2 * yn - 1)),
            dma((2 * layers, 2 * yn - 1)),
            dma((2 * layers, 2 * yn - 1)),
            dma((sem_count,)),
            dma((sem_count,)),
            dma((sem_count,)),
            dma((sem_count,)),
            dma((len(kept),)),
        ],
        compiler_params=pltpu.CompilerParams(
            collective_id=1, has_side_effects=True, vmem_limit_bytes=62 * 2**20
        ),
        name="backward_layers",
    )(lengths, slopes, g_in, norms, *kept)


def adam_update(master, grad, first, second, factor, fix_one, fix_two, decay, rate):
    clipped = grad * factor
    momentum = BETA_ONE * first + (1.0 - BETA_ONE) * clipped
    variance = BETA_TWO * second + (1.0 - BETA_TWO) * clipped * clipped
    step_size = momentum / fix_one / (jnp.sqrt(variance / fix_two) + ADAM_EPS) + decay * master
    fresh = master - rate * step_size
    return (momentum, variance, fresh, fresh.astype(jnp.bfloat16))


def body(
    block_input,
    output_grad,
    row_lengths,
    qkv_weight,
    proj_weight,
    up_weight,
    down_weight,
    norm_params,
    qkv_first,
    proj_first,
    up_first,
    down_first,
    norm_first,
    qkv_second,
    proj_second,
    up_second,
    down_second,
    norm_second,
):
    row_count, local_slots, width = block_input.shape
    seq_count = lax.axis_size("seq")
    groups = lax.axis_size("dp")
    layer_count = qkv_weight.shape[0]
    slots = local_slots * seq_count
    local_width = qkv_weight.shape[3]
    local_ff = up_weight.shape[2]
    head_local = local_width // HD
    dims = (
        layer_count, slots, width, local_slots, local_width, local_ff, groups,
        ZSIZE, groups // ZSIZE, seq_count // CORES,
    )
    head_ids = lax.axis_index("seq") * head_local + jnp.arange(head_local, dtype=jnp.int32)
    slopes = jnp.asarray(slope_table(H), F32)[head_ids]
    shards = (
        qkv_weight.astype(BF16).reshape(layer_count, -1, 3 * local_width),
        jnp.swapaxes(proj_weight.astype(BF16), 1, 2),
        up_weight.astype(BF16),
        jnp.swapaxes(down_weight.astype(BF16), 1, 2),
    )
    piece = norm_params.shape[2]
    device_at = lax.axis_index("dp") * seq_count + lax.axis_index("seq")
    norm_local = norm_params.astype(BF16).astype(F32).reshape(4 * layer_count, piece)
    norm_in = lax.dynamic_update_slice(
        jnp.zeros((4 * layer_count, width), F32), norm_local, (0, device_at * piece)
    )
    kept = run_forward(
        dims, row_lengths, slopes, block_input.reshape(local_slots, width), norm_in, shards
    )
    block_output = kept[0].reshape(row_count, local_slots, width)
    back = run_backward(
        dims, row_lengths, slopes, output_grad.reshape(local_slots, width), kept[1], kept[2:]
    )
    input_grad = back[0].reshape(row_count, local_slots, width)
    norm_grad = lax.dynamic_slice(
        back[1], (0, device_at * piece), (4 * layer_count, piece)
    ).reshape(layer_count, 4, piece)
    grad_norm = back[2][0, 0]
    stacked = [
        back[3].reshape(qkv_weight.shape),
        jnp.swapaxes(back[4], 1, 2),
        back[5],
        jnp.swapaxes(back[6], 1, 2),
        norm_grad,
    ]
    factor = CLIP_NORM / jnp.maximum(grad_norm, CLIP_NORM)
    fix_one = 1.0 - BETA_ONE**STEP
    fix_two = 1.0 - BETA_TWO**STEP
    qkv_out = adam_update(
        qkv_weight,
        stacked[0],
        qkv_first,
        qkv_second,
        factor,
        fix_one,
        fix_two,
        WEIGHT_DECAY,
        LEARN_RATE,
    )
    proj_out = adam_update(
        proj_weight,
        stacked[1],
        proj_first,
        proj_second,
        factor,
        fix_one,
        fix_two,
        WEIGHT_DECAY,
        LEARN_RATE,
    )
    up_out = adam_update(
        up_weight,
        stacked[2],
        up_first,
        up_second,
        factor,
        fix_one,
        fix_two,
        WEIGHT_DECAY,
        LEARN_RATE,
    )
    down_out = adam_update(
        down_weight,
        stacked[3],
        down_first,
        down_second,
        factor,
        fix_one,
        fix_two,
        WEIGHT_DECAY,
        LEARN_RATE,
    )
    norm_out = adam_update(
        norm_params, stacked[4], norm_first, norm_second, factor, fix_one, fix_two, 0.0, NORM_RATE
    )
    return (
        block_output,
        input_grad,
        grad_norm,
        stacked[0],
        stacked[1],
        stacked[2],
        stacked[3],
        stacked[4],
        qkv_out[0],
        proj_out[0],
        up_out[0],
        down_out[0],
        norm_out[0],
        qkv_out[1],
        proj_out[1],
        up_out[1],
        down_out[1],
        norm_out[1],
        qkv_out[2],
        proj_out[2],
        up_out[2],
        down_out[2],
        norm_out[2],
        qkv_out[3],
        proj_out[3],
        up_out[3],
        down_out[3],
        norm_out[3],
    )


def solution(mesh):
    return jax.shard_map(
        body,
        mesh=mesh,
        in_specs=(
            P("dp", "seq", None),
            P("dp", "seq", None),
            P("dp"),
            P(None, "dp", None, "seq"),
            P(None, "seq", "dp"),
            P(None, "dp", "seq"),
            P(None, "seq", "dp"),
            P(None, None, ("dp", "seq")),
            P(None, "dp", None, "seq"),
            P(None, "seq", "dp"),
            P(None, "dp", "seq"),
            P(None, "seq", "dp"),
            P(None, None, ("dp", "seq")),
            P(None, "dp", None, "seq"),
            P(None, "seq", "dp"),
            P(None, "dp", "seq"),
            P(None, "seq", "dp"),
            P(None, None, ("dp", "seq")),
        ),
        out_specs=(
            P("dp", "seq", None),
            P("dp", "seq", None),
            P(),
            P(None, "dp", None, "seq"),
            P(None, "seq", "dp"),
            P(None, "dp", "seq"),
            P(None, "seq", "dp"),
            P(None, None, ("dp", "seq")),
            P(None, "dp", None, "seq"),
            P(None, "seq", "dp"),
            P(None, "dp", "seq"),
            P(None, "seq", "dp"),
            P(None, None, ("dp", "seq")),
            P(None, "dp", None, "seq"),
            P(None, "seq", "dp"),
            P(None, "dp", "seq"),
            P(None, "seq", "dp"),
            P(None, None, ("dp", "seq")),
            P(None, "dp", None, "seq"),
            P(None, "seq", "dp"),
            P(None, "dp", "seq"),
            P(None, "seq", "dp"),
            P(None, None, ("dp", "seq")),
            P(None, "dp", None, "seq"),
            P(None, "seq", "dp"),
            P(None, "dp", "seq"),
            P(None, "seq", "dp"),
            P(None, None, ("dp", "seq")),
        ),
        check_vma=False,
    )
```

```python
import functools

import jax
import jax.numpy as jnp
import numpy as np
from jax import lax
from jax.experimental import pallas as pl
from jax.experimental.pallas import tpu as pltpu
from jax.sharding import PartitionSpec as P

H = 8
HD = 128
STEP = 5
CORES = 2
ZSIZE = 4

EPS_NORM = 1e-05
BETA_ONE = 0.5
BETA_TWO = 0.75
LEARN_RATE = 0.03
NORM_RATE = 0.3
WEIGHT_DECAY = 0.1
CLIP_NORM = 0.1
ADAM_EPS = 1e-08

UNITS = 12
DEPTH = 2
PUMPS = (
    ((0, 1, 2), (15, 16)),
    ((3,), (17,)),
    ((4,), ()),
    ((5, 6), (18, 19)),
    ((7,), (20, 21)),
    ((8,), ()),
    ((9,), (22,)),
    ((10, 11), (23,)),
    ((12, 13, 14), ()),
)

F32 = jnp.float32
BF16 = jnp.bfloat16
MESH = pl.DeviceIdType.MESH
SCORE_SCALE = HD ** (-0.5)
GELU_A = (2.0 / np.pi) ** 0.5
GELU_B = 0.044715


def slope_table(head_count):
    return np.power(2.0, -8.0 * (np.arange(head_count) + 1.0) / head_count)


def slope_at(head):
    value = jnp.float32(0.0)
    for index, slope in enumerate(slope_table(H)):
        value = jnp.where(head == index, jnp.float32(slope), value)
    return value


def weight_cols(c):
    return pl.ds(0, 3 * c), pl.ds(3 * c, c), pl.ds(4 * c, 4 * c), pl.ds(8 * c, 4 * c)


def mm_nn(a, b):
    return lax.dot_general(a, b, (((1,), (0,)), ((), ())), preferred_element_type=F32)


def mm_nt(a, b):
    return lax.dot_general(a, b, (((1,), (1,)), ((), ())), preferred_element_type=F32)


def mm_tn(a, b):
    return lax.dot_general(a, b, (((0,), (0,)), ((), ())), preferred_element_type=F32)


def normalise(v):
    centered = v - jnp.mean(v, axis=-1, keepdims=True)
    inverse = lax.rsqrt(jnp.mean(centered * centered, axis=-1, keepdims=True) + EPS_NORM)
    return centered * inverse, inverse


def rows_of(index, size):
    return pl.ds(pl.multiple_of(index * size, size), size)


class Place:
    def __init__(self, zn, xn, yn):
        self.zn, self.xn, self.yn = zn, xn, yn
        self.dp = lax.axis_index("dp")
        self.seq = lax.axis_index("seq")
        self.z, self.x = self.dp // xn, lax.rem(self.dp, xn)
        self.y, self.c = self.seq // CORES, lax.rem(self.seq, CORES)

    def zo(self, k):
        return lax.rem(self.z + k + self.zn, self.zn)

    def xo(self, k):
        return lax.rem(self.x + k + self.xn, self.xn)

    def yo(self, k):
        return lax.rem(self.y + k + self.yn, self.yn)

    def dev(self, dz=0, dx=0, dy=0, dc=0):
        core = (1 - self.c) if dc else self.c
        return (self.zo(dz) * self.xn + self.xo(dx), self.yo(dy) * CORES + core)

    def dp_at(self, dz, dx):
        return self.zo(dz) * self.xn + self.xo(dx)

    def seq_at(self, dy, dc):
        core = (1 - self.c) if dc else self.c
        return self.yo(dy) * CORES + core

    def peers(self):
        out = [self.dev(dc=1)]
        out += [self.dev(dy=k) for k in range(1, self.yn)]
        out += [self.dev(dx=k) for k in range(1, self.xn)]
        out += [self.dev(dz=k) for k in range(1, self.zn)]
        return out

    def barrier(self):
        sem = pltpu.get_barrier_semaphore()
        peers = self.peers()
        for peer in peers:
            pl.semaphore_signal(sem, inc=1, device_id=peer, device_id_type=MESH)
        pl.semaphore_wait(sem, len(peers))


def near_first(count):
    order = []
    for k in range(1, count):
        order.append((min(k, count - k), k))
    return [k for unused, k in sorted(order)]


def remote(src, dst, send, recv, dev):
    return pltpu.make_async_remote_copy(
        src_ref=src, dst_ref=dst, send_sem=send, recv_sem=recv, device_id=dev, device_id_type=MESH
    )


def all_sum(place, value, slots, send, recv):
    stages = (
        (CORES, place.c, lambda k: place.dev(dc=1), lambda k: 1 - place.c),
        (place.yn, place.y, lambda k: place.dev(dy=k), lambda k: place.yo(-k)),
        (place.xn, place.x, lambda k: place.dev(dx=k), lambda k: place.xo(-k)),
        (place.zn, place.z, lambda k: place.dev(dz=k), lambda k: place.zo(-k)),
    )
    base = 0
    at = 0
    for size, mine, target, origin in stages:
        slots[base + mine] = value
        own = slots.at[base + mine]
        for k in range(1, size):
            remote(own, own, send.at[at + k - 1], recv.at[at + k - 1], target(k)).start()
        for k in range(1, size):
            came = slots.at[base + origin(k)]
            remote(came, came, send.at[at + k - 1], recv.at[at + k - 1], target(k)).wait_recv()
        for k in range(1, size):
            remote(own, own, send.at[at + k - 1], recv.at[at + k - 1], target(k)).wait_send()
        value = slots[base]
        for k in range(1, size):
            value = value + slots[base + k]
        base += size
        at += size - 1
    return value


def sum_slots(zn, xn, yn):
    return CORES + yn + xn + zn, 1 + (yn - 1) + (xn - 1) + (zn - 1)


class Gather:
    def __init__(self, place, buf, block, send, recv):
        self.p, self.buf, self.block, self.send, self.recv = place, buf, block, send, recv

    def at(self, dy, dc):
        return self.buf.at[rows_of(self.p.seq_at(dy, dc), self.block)]

    def start(self):
        p, own = self.p, self.at(0, 0)
        for k in range(1, p.yn):
            remote(own, own, self.send.at[k], self.recv.at[k], p.dev(dy=k)).start()
        remote(own, own, self.send.at[0], self.recv.at[0], p.dev(dc=1)).start()

    def wait_chip(self):
        came = self.at(0, 1)
        remote(came, came, self.send.at[0], self.recv.at[0], self.p.dev(dc=1)).wait_recv()

    def forward(self):
        p = self.p
        for k in range(1, p.yn):
            came = self.at(-k, 0)
            remote(came, came, self.send.at[k], self.recv.at[k], p.dev(dy=k)).wait_recv()
            f = p.yn - 1 + k
            remote(came, came, self.send.at[f], self.recv.at[f], p.dev(dc=1)).start()

    def wait_rest(self):
        p = self.p
        for k in range(1, p.yn):
            f = p.yn - 1 + k
            came = self.at(-k, 1)
            remote(came, came, self.send.at[f], self.recv.at[f], p.dev(dc=1)).wait_recv()
        own = self.at(0, 0)
        for k in range(1, p.yn):
            remote(own, own, self.send.at[k], self.recv.at[k], p.dev(dy=k)).wait_send()
            f = p.yn - 1 + k
            sent = self.at(-k, 0)
            remote(sent, sent, self.send.at[f], self.recv.at[f], p.dev(dc=1)).wait_send()
        remote(own, own, self.send.at[0], self.recv.at[0], p.dev(dc=1)).wait_send()


class Scatter:
    def __init__(self, place, sbuf, rbuf, ysend, yrecv, acc, send, recv):
        self.p = place
        self.sbuf, self.rbuf, self.ysend, self.yrecv, self.acc = sbuf, rbuf, ysend, yrecv, acc
        self.send, self.recv = send, recv

    def core(self, k):
        return remote(
            self.sbuf.at[k], self.rbuf.at[k], self.send.at[k], self.recv.at[k], self.p.dev(dc=1)
        )

    def cross(self, k):
        s = self.p.yn + k - 1
        return remote(
            self.ysend.at[k - 1],
            self.yrecv.at[k - 1],
            self.send.at[s],
            self.recv.at[s],
            self.p.dev(dy=k),
        )

    def start(self, part):
        p = self.p
        for k in list(range(1, p.yn)) + [0]:
            self.sbuf[k] = part(p.seq_at(k, 1)).astype(BF16)
            self.core(k).start()
            mine = part(p.seq_at(k, 0))
            self.core(k).wait_recv()
            mine = mine + self.rbuf[k].astype(F32)
            if k:
                self.ysend[k - 1] = mine.astype(BF16)
                self.cross(k).start()
            else:
                self.acc[...] = mine

    def wait(self):
        p = self.p
        for k in range(1, p.yn):
            self.cross(k).wait_recv()
        for k in range(1, p.yn):
            self.cross(k).wait_send()
        for k in range(p.yn):
            self.core(k).wait_send()

    def rows(self, at):
        value = self.acc[at, :]
        for k in range(1, self.p.yn):
            value = value + self.yrecv[k - 1, at, :].astype(F32)
        return value


def row_loop(total, step, fn):
    def one(i, unused):
        fn(rows_of(i, step))
        return unused

    lax.fori_loop(0, total // step, one, 0)


def forward_kernel(dims, *refs):
    (layers, slots, width, block, local_width, local_ff, groups, zn, xn, yn) = dims
    heads = local_width // HD
    shard = width // groups
    refs = list(refs)

    def take(count):
        out = refs[:count]
        del refs[:count]
        return out

    lengths, x_in, norm_in = take(3)
    masters = take(4)
    out, norm_out = take(2)
    w_save = take(1)[0]
    xn1_save, xn2_save, qkv_save, ctx_save, lse_save, act_save, dact_save, hid_save, mid_save = take(9)
    w = take(1)[0]
    xn1, xn2, qkv, ctx, lse, act, dact, hid, mid, upper, ws, norm_place = take(12)
    sbuf, rbuf, ysend, yrecv, acc, nslots = take(6)
    zsend, zrecv, xsend, xrecv, own_sem, wsave_sem = take(6)
    ag_send, ag_recv, rs_send, rs_recv, ns_send, ns_recv, save_sem = take(7)

    p = Place(zn, xn, yn)
    z_order = near_first(zn)
    length = lengths[0]
    cols_qkv, cols_o, cols_up, cols_down = weight_cols(local_width)

    unit_count = UNITS * layers
    slopes = [slope_at(p.seq * heads + h) for h in range(heads)]

    def shard_rows(index):
        return rows_of(index, shard)

    def unit_cols(u):
        return pl.ds((u % UNITS) * local_width, local_width)

    def z_copy(u, dz, origin):
        l, cols = u // UNITS, unit_cols(u)
        return remote(
            ws.at[l, :, cols],
            w.at[l, shard_rows(origin), cols],
            zsend.at[u, dz - 1],
            zrecv.at[u, dz - 1],
            p.dev(dz=dz),
        )

    def x_copy(u, dx, dz, origin):
        l, cols = u // UNITS, unit_cols(u)
        there = w.at[l, shard_rows(origin), cols]
        return remote(
            there if dz else ws.at[l, :, cols],
            there,
            xsend.at[u, dx - 1, dz],
            xrecv.at[u, dx - 1, dz],
            p.dev(dx=dx),
        )

    def own_copy(l):
        return pltpu.make_async_copy(ws.at[l], w.at[l, shard_rows(p.dp)], own_sem.at[l])

    def prepare(u):
        l, v = divmod(u, UNITS)
        cols = unit_cols(u)
        if v < 3:
            ws[l, :, cols] = masters[0][l, v].astype(BF16)
        elif 4 <= v < 8:
            ws[l, :, cols] = masters[2][l, :, pl.ds((v - 4) * local_width, local_width)].astype(BF16)
        else:
            source, base = (masters[1], 0) if v == 3 else (masters[3], (v - 8) * local_width)
            for c in range(local_width // 128):
                turned = source[l, pl.ds(base + c * 128, 128), :].T
                ws[l, :, pl.ds((v % UNITS) * local_width + c * 128, 128)] = turned.astype(BF16)

    def start_unit(u):
        for dz in z_order:
            z_copy(u, dz, p.dp).start()
        for dx in range(1, xn):
            x_copy(u, dx, 0, p.dp).start()

    def pump(u):
        for dz in z_order:
            z_copy(u, dz, p.dp_at(-dz, 0)).wait_recv()
            for dx in range(1, xn):
                x_copy(u, dx, dz, p.dp_at(-dz, 0)).start()
        if u + DEPTH < unit_count:
            start_unit(u + DEPTH)

    def pumps(l, *tables):
        for at, units in enumerate(tables):
            if units:

                @pl.when(l == at)
                def _(units=units):
                    for u in units:
                        pump(u)

    def save_weight(l):
        return pltpu.make_async_copy(w.at[l], w_save.at[l], wsave_sem.at[l])

    def need(l, low, high):
        def one(v, unused):
            u = UNITS * l + v
            for dz in range(zn):
                for dx in range(1, xn):
                    at = w.at[0, shard_rows(p.dp_at(-dz, -dx)), pl.ds(0, local_width)]
                    remote(
                        at, at, xsend.at[u, dx - 1, dz], xrecv.at[u, dx - 1, dz], p.dev(dx=dx)
                    ).wait_recv()
            return unused

        lax.fori_loop(low, high, one, 0)

    def finish_weight(l):
        def one(v, unused):
            u = UNITS * l + v
            at = ws.at[0, :, pl.ds(0, local_width)]
            for dz in z_order:
                remote(
                    at, at, zsend.at[u, dz - 1], zrecv.at[u, dz - 1], p.dev(dz=dz)
                ).wait_send()
            for dz in range(zn):
                for dx in range(1, xn):
                    remote(
                        at, at, xsend.at[u, dx - 1, dz], xrecv.at[u, dx - 1, dz], p.dev(dx=dx)
                    ).wait_send()
            return unused

        lax.fori_loop(0, UNITS, one, 0)
        save_weight(l).wait()

    def save(l, which, src, dst):
        return pltpu.make_async_copy(src, dst, save_sem.at[l, which])

    def saves(l):
        return (
            save(l, 0, xn1.at[l], xn1_save.at[l]),
            save(l, 1, xn2.at[l], xn2_save.at[l]),
            save(l, 2, qkv.at[l], qkv_save.at[l]),
            save(l, 3, ctx.at[l], ctx_save.at[l]),
            save(l, 4, lse.at[l], lse_save.at[l]),
            save(l, 5, act.at[l], act_save.at[l]),
            save(l, 6, dact.at[l], dact_save.at[l]),
            save(l, 7, hid.at[l], hid_save.at[l]),
            save(l, 8, mid.at[l], mid_save.at[l]),
        )

    p.barrier()
    for u in range(DEPTH):
        prepare(u)
        start_unit(u)
    piece = width // (groups * CORES * yn)
    at_lane = (p.dp * CORES * yn + p.seq) * piece
    norm_place[...] = jnp.zeros_like(norm_place)
    norm_place[:, rows_of(at_lane // 128, 128)] = pltpu.roll(norm_in[...], lax.rem(at_lane, 128), 1)
    norm_out[...] = all_sum(p, norm_place[...], nslots, ns_send, ns_recv)
    for u in range(DEPTH, UNITS):
        prepare(u)
    own_copy(0).start()

    def load_in(at):
        hid[0, at, :] = x_in[at, :].astype(F32)

    row_loop(block, 64, load_in)
    first = p.seq * block

    def norm_row(index):
        return norm_out[pl.ds(index, 1), :]

    def norm_into(l, source, target, row):
        gain, bias = norm_row(4 * l + row), norm_row(4 * l + row + 1)

        def one(i, unused):
            scaled, inverse = normalise(source[l, rows_of(i, 32), :])
            at = pl.ds(pl.multiple_of(first + i * 32, 32), 32)
            target[l, at, :] = (scaled * gain + bias).astype(BF16)
            return unused

        lax.fori_loop(0, block // 32, one, 0)

    def attention(l):
        key_at = lax.broadcasted_iota(jnp.int32, (1, slots), 1)
        step = 256
        causal = lax.broadcasted_iota(jnp.int32, (step, step), 1) <= lax.broadcasted_iota(
            jnp.int32, (step, step), 0
        )
        for h in range(heads):
            bias = jnp.where(key_at < length, slopes[h] * key_at.astype(F32), -jnp.inf)
            cols = pl.ds(h * HD, HD)
            for b in range(slots // step):
                here = pl.ds(b * step, step)
                before = pl.ds(0, b * step)
                k_cols = pl.ds(local_width + h * HD, HD)
                v_cols = pl.ds(2 * local_width + h * HD, HD)
                q = qkv[l, here, cols]
                raw = mm_nt(q, qkv[l, here, k_cols]) * SCORE_SCALE + bias[:, b * step : (b + 1) * step]
                raw = jnp.where(causal, raw, -jnp.inf)
                top = jnp.max(raw, axis=1, keepdims=True)
                if b:
                    past = mm_nt(q, qkv[l, before, k_cols]) * SCORE_SCALE + bias[:, : b * step]
                    top = jnp.maximum(top, jnp.max(past, axis=1, keepdims=True))
                e_here = jnp.exp(raw - top)
                total = jnp.sum(e_here, axis=1, keepdims=True)
                value = mm_nn(e_here.astype(BF16), qkv[l, here, v_cols])
                if b:
                    e_past = jnp.exp(past - top)
                    total = total + jnp.sum(e_past, axis=1, keepdims=True)
                    value = value + mm_nn(e_past.astype(BF16), qkv[l, before, v_cols])
                ctx[l, here, cols] = (value / total).astype(BF16)
                lse[l, here, pl.ds(h, 1)] = top + jnp.log(total)

    def layer(l, unused):
        last = layers - 1
        g_one = Gather(p, xn1.at[l], block, ag_send.at[2 * l], ag_recv.at[2 * l])
        g_two = Gather(p, xn2.at[l], block, ag_send.at[2 * l + 1], ag_recv.at[2 * l + 1])
        rs = [
            Scatter(
                p, sbuf, rbuf, ysend, yrecv, acc,
                rs_send.at[2 * l + i], rs_recv.at[2 * l + i],
            )
            for i in range(2)
        ]
        save_at = saves(l)
        save_at[7].start()
        norm_into(l, hid, xn1, 0)
        g_one.start()

        @pl.when(l == 0)
        def _():
            for u in range(UNITS, unit_count):
                prepare(u)

        @pl.when(l > 0)
        def _():
            own_copy(l).start()

        pumps(l, *PUMPS[0])
        own_copy(l).wait()

        def project(index):
            at = rows_of(index, block)
            qkv[l, at, :] = mm_nn(xn1[l, at, :], w[l, :, cols_qkv]).astype(BF16)

        g_one.wait_chip()
        g_one.forward()
        need(l, 0, 3)
        project(p.seq_at(0, 0))
        project(p.seq_at(0, 1))
        pumps(l, *PUMPS[1])
        g_one.wait_rest()
        save_at[0].start()
        for k in range(1, yn):
            project(p.seq_at(-k, 0))
            project(p.seq_at(-k, 1))
        save_at[2].start()
        attention(l)
        save_at[3].start()
        save_at[4].start()
        pumps(l, *PUMPS[2])
        need(l, 3, 4)
        rs[0].start(lambda b: mm_nt(ctx[l, rows_of(b, block), :], w[l, :, cols_o]))
        pumps(l, *PUMPS[3])
        rs[0].wait()

        def add_middle(at):
            mid[l, at, :] = hid[l, at, :] + rs[0].rows(at)

        row_loop(block, 32, add_middle)
        save_at[8].start()
        norm_into(l, mid, xn2, 2)
        g_two.start()
        pumps(l, *PUMPS[4])
        need(l, 4, 8)

        def expand(index):
            base = pl.multiple_of(index * block, block)
            upper[...] = mm_nn(xn2[l, pl.ds(base, block), :], w[l, :, cols_up])

            def one(i, unused):
                u = upper[rows_of(i, 16), :]
                at = pl.ds(pl.multiple_of(base + i * 16, 16), 16)
                square = u * u
                t = jnp.tanh(GELU_A * u * (1.0 + GELU_B * square))
                half = 0.5 * (1.0 + t)
                act[l, at, :] = (u * half).astype(BF16)
                slope = (0.5 * GELU_A) * u * (1.0 - t * t) * (1.0 + (3.0 * GELU_B) * square)
                dact[l, at, :] = (half + slope).astype(BF16)
                return unused

            lax.fori_loop(0, block // 16, one, 0)

        expand(p.seq_at(0, 0))
        g_two.wait_chip()
        expand(p.seq_at(0, 1))
        pumps(l, *PUMPS[5])
        g_two.forward()
        pumps(l, *PUMPS[6])
        g_two.wait_rest()
        save_at[1].start()
        for k in range(1, yn):
            expand(p.seq_at(-k, 0))
            expand(p.seq_at(-k, 1))
        save_at[5].start()
        save_at[6].start()
        pumps(l, *PUMPS[7])
        need(l, 8, 12)
        save_weight(l).start()
        rs[1].start(lambda b: mm_nt(act[l, rows_of(b, block), :], w[l, :, cols_down]))
        pumps(l, *PUMPS[8])
        rs[1].wait()

        @pl.when(l < last)
        def _():
            def add_next(at):
                hid[l + 1, at, :] = mid[l, at, :] + rs[1].rows(at)

            row_loop(block, 32, add_next)

        @pl.when(l == last)
        def _():
            def add_out(at):
                out[at, :] = mid[l, at, :] + rs[1].rows(at)

            row_loop(block, 32, add_out)

        return unused

    lax.fori_loop(0, layers, layer, 0)

    def finish(l, unused):
        finish_weight(l)
        for item in saves(l):
            item.wait()
        return unused

    lax.fori_loop(0, layers, finish, 0)


def run_forward(dims, lengths, x_in, norm_in, masters):
    (layers, slots, width, block, local_width, local_ff, groups, zn, xn, yn) = dims
    shard = width // groups
    slot_count, sem_count = sum_slots(zn, xn, yn)

    def saved(*shape, dtype=BF16):
        return jax.ShapeDtypeStruct((layers,) + shape, dtype)

    vmem = pl.BlockSpec(memory_space=pltpu.VMEM)
    smem = pl.BlockSpec(memory_space=pltpu.SMEM)
    hbm = pl.BlockSpec(memory_space=pl.ANY)
    kept = [
        saved(width, UNITS * local_width),
        saved(slots, width),
        saved(slots, width),
        saved(slots, 3 * local_width),
        saved(slots, local_width),
        saved(slots, 128, dtype=F32),
        saved(slots, local_ff),
        saved(slots, local_ff),
        saved(block, width, dtype=F32),
        saved(block, width, dtype=F32),
    ]
    dma = pltpu.SemaphoreType.DMA
    return pl.pallas_call(
        functools.partial(forward_kernel, dims),
        out_shape=[
            jax.ShapeDtypeStruct((block, width), F32),
            jax.ShapeDtypeStruct((4 * layers, width), F32),
        ]
        + kept,
        in_specs=[smem] + [vmem] * 6,
        out_specs=[vmem, vmem] + [hbm] * len(kept),
        scratch_shapes=[pltpu.VMEM(k.shape, k.dtype) for k in kept]
        + [
            pltpu.VMEM((block, local_ff), F32),
            pltpu.VMEM((layers, shard, UNITS * local_width), BF16),
            pltpu.VMEM((4 * layers, width), F32),
            pltpu.VMEM((yn, block, width), BF16),
            pltpu.VMEM((yn, block, width), BF16),
            pltpu.VMEM((yn - 1, block, width), BF16),
            pltpu.VMEM((yn - 1, block, width), BF16),
            pltpu.VMEM((block, width), F32),
            pltpu.VMEM((slot_count, 4 * layers, width), F32),
            dma((UNITS * layers, zn - 1)),
            dma((UNITS * layers, zn - 1)),
            dma((UNITS * layers, xn - 1, zn)),
            dma((UNITS * layers, xn - 1, zn)),
            dma((layers,)),
            dma((layers,)),
            dma((2 * layers, 2 * yn - 1)),
            dma((2 * layers, 2 * yn - 1)),
            dma((2 * layers, 2 * yn - 1)),
            dma((2 * layers, 2 * yn - 1)),
            dma((sem_count,)),
            dma((sem_count,)),
            dma((layers, 9)),
        ],
        compiler_params=pltpu.CompilerParams(
            collective_id=0, has_side_effects=True, vmem_limit_bytes=62 * 2**20
        ),
        name="forward_layers",
    )(lengths, x_in, norm_in, *masters)

def backward_kernel(dims, *refs):
    (layers, slots, width, block, local_width, local_ff, groups, zn, xn, yn) = dims
    heads = local_width // HD
    shard = width // groups
    refs = list(refs)

    def take(count):
        out = refs[:count]
        del refs[:count]
        return out

    lengths, g_in, norms = take(3)
    kept = take(10)
    g_out, norm_grad, total_out = take(3)
    shards = take(1)[0]
    held = take(10)
    w, xn1, xn2, qkv, ctx, lse, act, dact, hid, mid = held
    gfull, gbfull, gctx, dqkv, dk, dv, g, gm, npart = take(9)
    dw, xland, zland = take(3)
    sbuf, rbuf, ysend, yrecv, acc, nslots, tslots = take(7)
    zsend, zrecv, xsend, xrecv = take(4)
    ag_send, ag_recv, rs_send, rs_recv, ns_send, ns_recv, ts_send, ts_recv, load_sem = take(9)

    p = Place(zn, xn, yn)
    length = lengths[0]
    first = p.seq * block
    gu = dact
    w_all = kept[0]

    slopes = [slope_at(p.seq * heads + h) for h in range(heads)]
    weight_at = weight_cols(local_width)
    cols_qkv, cols_o, cols_up, cols_down = weight_at

    def load(l, which):
        if which < 4:
            cols = weight_at[which]
            return pltpu.make_async_copy(w_all.at[l, :, cols], w.at[:, cols], load_sem.at[which])
        return pltpu.make_async_copy(kept[which - 3].at[l], held[which - 3], load_sem.at[which])

    def rows_at(dz, dx):
        return rows_of(p.dp_at(dz, dx), shard)

    def unit_cols(v):
        return pl.ds(v * local_width, local_width)

    def x_copy(l, v, zi, dx):
        cols = unit_cols(v)
        return remote(
            dw.at[rows_at(zi, dx), cols],
            xland.at[l, dx - 1, zi, :, cols],
            xsend.at[l, v, dx - 1, zi],
            xrecv.at[l, v, dx - 1, zi],
            p.dev(dx=dx),
        )

    def z_copy(l, v, zi):
        cols = unit_cols(v)
        return remote(
            dw.at[rows_at(zi, 0), cols],
            zland.at[l, zi - 1, :, cols],
            zsend.at[l, v, zi - 1],
            zrecv.at[l, v, zi - 1],
            p.dev(dz=zi),
        )

    z_order = near_first(zn)
    zi_order = z_order[::-1] + [0]

    def weight_grad(left, right, low, count):
        def one(i, unused):
            at = rows_of(i, 256)
            dw[at, pl.ds(low * local_width, count * local_width)] = mm_tn(
                left[:, at], right[...]
            ).astype(BF16)
            return unused

        lax.fori_loop(0, width // 256, one, 0)

    def send_x(l, *units):
        for v in units:
            for zi in zi_order:
                for dx in range(1, xn):
                    x_copy(l, v, zi, dx).start()

    def reduce_x(l, *units):
        for v in units:
            cols = unit_cols(v)
            for zi in zi_order:
                for dx in range(1, xn):
                    x_copy(l, v, zi, dx).wait_recv()
                base = pl.multiple_of(p.dp_at(zi, 0) * shard, shard)

                def one(i, unused, zi=zi, cols=cols, base=base):
                    here = rows_of(i, 32)
                    at = pl.ds(pl.multiple_of(base + i * 32, 32), 32)
                    value = dw[at, cols].astype(F32)
                    for dx in range(1, xn):
                        value = value + xland[l, dx - 1, zi, here, cols].astype(F32)
                    if zi:
                        dw[at, cols] = value.astype(BF16)
                    else:
                        shards[l, here, cols] = value
                    return unused

                lax.fori_loop(0, shard // 32, one, 0)
                if zi:
                    z_copy(l, v, zi).start()

    def reduce_z(l, low, high):
        def unit(v, unused):
            cols = pl.ds(pl.multiple_of(v * local_width, local_width), local_width)
            here = dw.at[pl.ds(0, shard), pl.ds(0, local_width)]
            for zi in z_order:
                remote(
                    here, here, zsend.at[l, v, zi - 1], zrecv.at[l, v, zi - 1], p.dev(dz=zi)
                ).wait_recv()

            def one(at):
                value = shards[l, at, cols]
                for zi in range(1, zn):
                    value = value + zland[l, zi - 1, at, cols].astype(F32)
                shards[l, at, cols] = value

            row_loop(shard, 32, one)
            for zi in z_order:
                remote(
                    here, here, zsend.at[l, v, zi - 1], zrecv.at[l, v, zi - 1], p.dev(dz=zi)
                ).wait_send()
            for zi in range(zn):
                for dx in range(1, xn):
                    remote(
                        here,
                        here,
                        xsend.at[l, v, dx - 1, zi],
                        xrecv.at[l, v, dx - 1, zi],
                        p.dev(dx=dx),
                    ).wait_send()
            return unused

        lax.fori_loop(low, high, unit, 0)

    def norm_back(l, source, rs, base, row, target, low):
        gain = norms[pl.ds(4 * l + row, 1), :]
        zero = jnp.zeros((8, width), F32)

        def one(i, carry):
            at = rows_of(i, 32)
            scaled, inverse = normalise(source[at, :])
            e = rs.rows(at)
            eg = e * gain
            part = inverse * (
                eg
                - jnp.mean(eg, axis=-1, keepdims=True)
                - scaled * jnp.mean(eg * scaled, axis=-1, keepdims=True)
            )
            value = base[at, :] + part
            target[at, :] = value
            if low is not None:
                low[pl.ds(pl.multiple_of(first + i * 32, 32), 32), :] = value.astype(BF16)
            es = e * scaled
            gains, biases = carry
            for r in range(4):
                gains = gains + es[r * 8 : r * 8 + 8]
                biases = biases + e[r * 8 : r * 8 + 8]
            return gains, biases

        gains, biases = lax.fori_loop(0, block // 32, one, (zero, zero))
        npart[pl.ds(4 * l + row, 1), :] = jnp.sum(gains, axis=0, keepdims=True)
        npart[pl.ds(4 * l + row + 1, 1), :] = jnp.sum(biases, axis=0, keepdims=True)

    def attention(between):
        key_at = lax.broadcasted_iota(jnp.int32, (1, slots), 1)
        step = 256
        causal = lax.broadcasted_iota(jnp.int32, (step, step), 1) <= lax.broadcasted_iota(
            jnp.int32, (step, step), 0
        )
        for h in range(heads):
            bias = jnp.where(key_at < length, slopes[h] * key_at.astype(F32), -jnp.inf)
            cols = pl.ds(h * HD, HD)
            k_cols = pl.ds(local_width + h * HD, HD)
            v_cols = pl.ds(2 * local_width + h * HD, HD)
            for b in range(slots // step):
                here = pl.ds(b * step, step)
                before = pl.ds(0, b * step)
                q = qkv[here, cols]
                gc = gctx[here, cols]
                shift = lse[here, pl.ds(h, 1)]
                raw = mm_nt(q, qkv[here, k_cols]) * SCORE_SCALE + bias[:, b * step : (b + 1) * step]
                p_here = jnp.exp(jnp.where(causal, raw, -jnp.inf) - shift)
                dp_here = mm_nt(gc, qkv[here, v_cols])
                delta = jnp.sum(p_here * dp_here, axis=1, keepdims=True)
                dv[here, :] = mm_tn(p_here.astype(BF16), gc)
                if b:
                    past = mm_nt(q, qkv[before, k_cols]) * SCORE_SCALE + bias[:, : b * step]
                    p_past = jnp.exp(past - shift)
                    dp_past = mm_nt(gc, qkv[before, v_cols])
                    delta = delta + jnp.sum(p_past * dp_past, axis=1, keepdims=True)
                    dv[before, :] += mm_tn(p_past.astype(BF16), gc)
                ds_here = (p_here * (dp_here - delta)).astype(BF16)
                dq = mm_nn(ds_here, qkv[here, k_cols])
                dk[here, :] = mm_tn(ds_here, q)
                if b:
                    ds_past = (p_past * (dp_past - delta)).astype(BF16)
                    dq = dq + mm_nn(ds_past, qkv[before, k_cols])
                    dk[before, :] += mm_tn(ds_past, q)
                dqkv[here, cols] = (dq * SCORE_SCALE).astype(BF16)
                between(h * (slots // step) + b + 1, heads * (slots // step))

            def store(at):
                dqkv[at, k_cols] = (dk[at, :] * SCORE_SCALE).astype(BF16)
                dqkv[at, v_cols] = dv[at, :].astype(BF16)

            row_loop(slots, 64, store)

    p.barrier()

    def mask_in(i, unused):
        at = rows_of(i, 32)
        slot = first + i * 32 + lax.broadcasted_iota(jnp.int32, (32, 1), 0)
        g[at, :] = jnp.where(slot < length, g_in[at, :].astype(F32), 0.0)
        return unused

    lax.fori_loop(0, block // 32, mask_in, 0)
    load_order = (3, 10, 2, 9, 5, 12, 1, 7, 6, 8, 0, 4, 11)

    def layer(step, unused):
        l = layers - 1 - step
        later = l + 1
        for which in load_order:
            load(l, which).start()
        g_one = Gather(p, gfull, block, ag_send.at[2 * l], ag_recv.at[2 * l])
        g_two = Gather(p, gbfull, block, ag_send.at[2 * l + 1], ag_recv.at[2 * l + 1])
        rs = [
            Scatter(
                p, sbuf, rbuf, ysend, yrecv, acc, rs_send.at[2 * l + i], rs_recv.at[2 * l + i]
            )
            for i in range(2)
        ]

        def low_in(i, unused):
            at = pl.ds(pl.multiple_of(first + i * 32, 32), 32)
            gfull[at, :] = g[rows_of(i, 32), :].astype(BF16)
            return unused

        lax.fori_loop(0, block // 32, low_in, 0)
        g_one.start()

        load(l, 3).wait()
        load(l, 10).wait()

        def upper_grad(index):
            at = rows_of(index, block)
            value = mm_nn(gfull[at, :], w[:, cols_down])
            gu[at, :] = (value * dact[at, :].astype(F32)).astype(BF16)

        upper_grad(p.seq_at(0, 0))
        g_one.wait_chip()
        upper_grad(p.seq_at(0, 1))
        g_one.forward()

        @pl.when(step > 0)
        def _():
            reduce_x(later, 0)

        g_one.wait_rest()
        for k in range(1, yn):
            upper_grad(p.seq_at(-k, 0))
            upper_grad(p.seq_at(-k, 1))
        load(l, 2).wait()
        rs[0].start(lambda b: mm_nt(gu[rows_of(b, block), :], w[:, cols_up]))
        load(l, 9).wait()
        load(l, 5).wait()

        @pl.when(step > 0)
        def _():
            reduce_z(later, 3, 12)

        weight_grad(gfull, act, 8, 4)
        send_x(l, 8, 9, 10)
        weight_grad(xn2, gu, 4, 4)

        @pl.when(step > 0)
        def _():
            reduce_x(later, 1, 2)

        load(l, 12).wait()
        reduce_x(l, 8)
        send_x(l, 11)
        rs[0].wait()
        norm_back(l, mid, rs[0], g, 2, gm, gbfull)
        g_two.start()
        reduce_x(l, 9)
        send_x(l, 4)
        load(l, 1).wait()

        def context_grad(index):
            at = rows_of(index, block)
            gctx[at, :] = mm_nn(gbfull[at, :], w[:, cols_o]).astype(BF16)

        context_grad(p.seq_at(0, 0))
        g_two.wait_chip()
        context_grad(p.seq_at(0, 1))
        reduce_x(l, 10)
        send_x(l, 5)
        g_two.forward()

        @pl.when(step > 0)
        def _():
            reduce_z(later, 0, 3)

        g_two.wait_rest()
        for k in range(1, yn):
            context_grad(p.seq_at(-k, 0))
            context_grad(p.seq_at(-k, 1))
        reduce_x(l, 11)
        send_x(l, 6)
        load(l, 7).wait()
        weight_grad(gbfull, ctx, 3, 1)
        load(l, 6).wait()
        load(l, 8).wait()

        def between(done, count):
            if done == (count * 3) // 8:
                reduce_x(l, 4)
                send_x(l, 7)
            if done == (count * 6) // 8:
                reduce_x(l, 5)
                send_x(l, 3)

        attention(between)
        load(l, 0).wait()
        load(l, 4).wait()

        @pl.when(l == 0)
        def _():
            weight_grad(xn1, dqkv, 0, 3)
            send_x(l, 0)

        reduce_x(l, 6)
        rs[1].start(lambda b: mm_nt(dqkv[rows_of(b, block), :], w[:, cols_qkv]))

        @pl.when(l > 0)
        def _():
            weight_grad(xn1, dqkv, 0, 3)
            send_x(l, 0)

        reduce_x(l, 7)
        send_x(l, 1)
        reduce_x(l, 3)
        send_x(l, 2)
        load(l, 11).wait()
        rs[1].wait()
        norm_back(l, hid, rs[1], gm, 0, g, None)
        return unused

    lax.fori_loop(0, layers, layer, 0)
    reduce_x(0, 0, 1, 2)
    g_out[...] = g[...]
    norm_grad[...] = all_sum(p, npart[...], nslots, ns_send, ns_recv)
    reduce_z(0, 3, 12)
    reduce_z(0, 0, 3)

    def squares(i, total):
        l, at = i // (shard // 8), rows_of(lax.rem(i, shard // 8), 8)
        value = shards[l, at, :]
        value = value * value
        for c in range(UNITS * local_width // 128):
            total = total + value[:, c * 128 : (c + 1) * 128]
        return total

    tile = lax.fori_loop(0, layers * shard // 8, squares, jnp.zeros((8, 128), F32))
    tile = all_sum(p, tile, tslots, ts_send, ts_recv)
    value = norm_grad[...]
    value = value * value
    for c in range(width // 128):
        piece = value[:, c * 128 : (c + 1) * 128]
        for r in range(4 * layers // 8):
            tile = tile + piece[r * 8 : r * 8 + 8]
    total = jnp.sum(jnp.sum(tile, axis=0, keepdims=True), axis=1, keepdims=True)
    total_out[...] = jnp.broadcast_to(jnp.sqrt(total), (8, 128))


def run_backward(dims, lengths, g_in, norms, kept):
    (layers, slots, width, block, local_width, local_ff, groups, zn, xn, yn) = dims
    packed = UNITS * local_width
    shard = width // groups
    slot_count, sem_count = sum_slots(zn, xn, yn)
    vmem = pl.BlockSpec(memory_space=pltpu.VMEM)
    smem = pl.BlockSpec(memory_space=pltpu.SMEM)
    hbm = pl.BlockSpec(memory_space=pl.ANY)
    dma = pltpu.SemaphoreType.DMA
    return pl.pallas_call(
        functools.partial(backward_kernel, dims),
        out_shape=[
            jax.ShapeDtypeStruct((block, width), F32),
            jax.ShapeDtypeStruct((4 * layers, width), F32),
            jax.ShapeDtypeStruct((8, 128), F32),
            jax.ShapeDtypeStruct((layers, shard, packed), F32),
        ],
        in_specs=[smem, vmem, vmem] + [hbm] * len(kept),
        out_specs=[vmem] * 4,
        scratch_shapes=[pltpu.VMEM(k.shape[1:], k.dtype) for k in kept]
        + [
            pltpu.VMEM((slots, width), BF16),
            pltpu.VMEM((slots, width), BF16),
            pltpu.VMEM((slots, local_width), BF16),
            pltpu.VMEM((slots, 3 * local_width), BF16),
            pltpu.VMEM((slots, HD), F32),
            pltpu.VMEM((slots, HD), F32),
            pltpu.VMEM((block, width), F32),
            pltpu.VMEM((block, width), F32),
            pltpu.VMEM((4 * layers, width), F32),
            pltpu.VMEM((width, packed), BF16),
            pltpu.VMEM((layers, xn - 1, zn, shard, packed), BF16),
            pltpu.VMEM((layers, zn - 1, shard, packed), BF16),
            pltpu.VMEM((yn, block, width), BF16),
            pltpu.VMEM((yn, block, width), BF16),
            pltpu.VMEM((yn - 1, block, width), BF16),
            pltpu.VMEM((yn - 1, block, width), BF16),
            pltpu.VMEM((block, width), F32),
            pltpu.VMEM((slot_count, 4 * layers, width), F32),
            pltpu.VMEM((slot_count, 8, 128), F32),
            dma((layers, UNITS, zn - 1)),
            dma((layers, UNITS, zn - 1)),
            dma((layers, UNITS, xn - 1, zn)),
            dma((layers, UNITS, xn - 1, zn)),
            dma((2 * layers, 2 * yn - 1)),
            dma((2 * layers, 2 * yn - 1)),
            dma((2 * layers, 2 * yn - 1)),
            dma((2 * layers, 2 * yn - 1)),
            dma((sem_count,)),
            dma((sem_count,)),
            dma((sem_count,)),
            dma((sem_count,)),
            dma((len(kept) + 3,)),
        ],
        compiler_params=pltpu.CompilerParams(
            collective_id=1, has_side_effects=True, vmem_limit_bytes=62 * 2**20
        ),
        name="backward_layers",
    )(lengths, g_in, norms, *kept)


def adam_kernel(dims, *refs):
    (layers, slots, width, block, local_width, local_ff, groups, zn, xn, yn) = dims
    refs = list(refs)

    def take(count):
        out = refs[:count]
        del refs[:count]
        return out

    total, norm_grad, hidden_in, input_in = take(4)
    grads, masters, firsts, seconds = take(4), take(5), take(5), take(5)
    hidden_out, input_out = take(2)
    grad_out, moment_out, variance_out, new_out, copy_out = (take(5) for unused in range(5))
    factor = CLIP_NORM / jnp.maximum(total[0:1, 0:1], CLIP_NORM)
    fix_one = 1.0 / (1.0 - BETA_ONE**STEP)
    fix_two = 1.0 / (1.0 - BETA_TWO**STEP)

    def update(k, at, grad, decay, rate):
        clipped = grad * factor
        momentum = BETA_ONE * firsts[k][at] + (1.0 - BETA_ONE) * clipped
        variance = BETA_TWO * seconds[k][at] + (1.0 - BETA_TWO) * clipped * clipped
        master = masters[k][at]
        size = momentum * fix_one / (jnp.sqrt(variance * fix_two) + ADAM_EPS)
        if decay:
            size = size + decay * master
        fresh = master - rate * size
        grad_out[k][at] = grad
        moment_out[k][at] = momentum
        variance_out[k][at] = variance
        new_out[k][at] = fresh
        copy_out[k][at] = fresh.astype(BF16)

    def matrix(k, at, grad):
        update(k, at, grad, WEIGHT_DECAY, LEARN_RATE)

    hidden_out[...] = hidden_in[...]
    input_out[...] = input_in[...]
    every = slice(None)
    for part in range(3):
        grad = grads[0][0, :, part * local_width : (part + 1) * local_width]
        matrix(0, (0, part, every, every), grad)
    matrix(1, (0, every, every), grads[1][0].T)

    def up_rows(i, unused):
        at = rows_of(i, 16)
        matrix(2, (0, at, every), grads[2][0, at, :])
        return unused

    lax.fori_loop(0, grads[2].shape[1] // 16, up_rows, 0)
    for c in range(grads[3].shape[2] // 128):
        at = pl.ds(c * 128, 128)
        matrix(3, (0, at, every), grads[3][0, :, at].T)

    @pl.when((pl.program_id(0) == 0) & (pl.program_id(1) == 0))
    def _():
        seq_count = CORES * yn
        piece = width // (groups * seq_count)
        at = (lax.axis_index("dp") * seq_count + lax.axis_index("seq")) * piece
        tile = norm_grad[:, rows_of(at // 128, 128)]
        tile = pltpu.roll(tile, lax.rem(128 - lax.rem(at, 128), 128), 1)[:, :piece]
        for l in range(layers):
            update(4, (l,), tile[4 * l : 4 * l + 4], 0.0, NORM_RATE)


def run_adam(dims, total, norm_grad, hidden, input_grad, grad, masters, firsts, seconds):
    (layers, slots, width, block, local_width, local_ff, groups, zn, xn, yn) = dims
    parts = local_width // 128
    shard = width // groups
    piece = width // (groups * CORES * yn)
    rows = block // (layers * parts)

    def same(shape):
        return pl.BlockSpec(shape, lambda l, b: (0,) * len(shape))

    flat = pl.BlockSpec((rows, width), lambda l, b: (l * parts + b, 0))
    grad_specs = [
        pl.BlockSpec((1, shard // parts, 3 * local_width), lambda l, b: (l, b, 0)),
        pl.BlockSpec((1, shard, 128), lambda l, b: (l, 0, 3 * parts + b)),
        pl.BlockSpec((1, shard // parts, local_ff), lambda l, b: (l, b, 1)),
        pl.BlockSpec((1, shard, local_ff // parts), lambda l, b: (l, 0, 2 * parts + b)),
    ]
    own_specs = [
        pl.BlockSpec((1, 3, shard // parts, local_width), lambda l, b: (l, 0, b, 0)),
        pl.BlockSpec((1, 128, shard), lambda l, b: (l, b, 0)),
        pl.BlockSpec((1, shard // parts, local_ff), lambda l, b: (l, b, 0)),
        pl.BlockSpec((1, local_ff // parts, shard), lambda l, b: (l, b, 0)),
        same((layers, 4, piece)),
    ]

    def shapes(dtype):
        return [jax.ShapeDtypeStruct(m.shape, dtype) for m in masters]

    flat_shape = jax.ShapeDtypeStruct((block, width), F32)
    return pl.pallas_call(
        functools.partial(adam_kernel, dims),
        grid=(layers, parts),
        out_shape=[flat_shape, flat_shape] + shapes(F32) * 4 + shapes(BF16),
        in_specs=[same((8, 128)), same((4 * layers, width)), flat, flat]
        + grad_specs
        + own_specs * 3,
        out_specs=[flat, flat] + own_specs * 5,
        compiler_params=pltpu.CompilerParams(vmem_limit_bytes=60 * 2**20),
        name="adam_update",
    )(total, norm_grad, hidden, input_grad, *([grad] * 4), *masters, *firsts, *seconds)


def body(
    block_input,
    output_grad,
    row_lengths,
    qkv_weight,
    proj_weight,
    up_weight,
    down_weight,
    norm_params,
    qkv_first,
    proj_first,
    up_first,
    down_first,
    norm_first,
    qkv_second,
    proj_second,
    up_second,
    down_second,
    norm_second,
):
    row_count, local_slots, width = block_input.shape
    seq_count = lax.axis_size("seq")
    groups = lax.axis_size("dp")
    layer_count = qkv_weight.shape[0]
    local_width = qkv_weight.shape[3]
    dims = (
        layer_count, local_slots * seq_count, width, local_slots, local_width,
        up_weight.shape[2], groups, ZSIZE, groups // ZSIZE, seq_count // CORES,
    )

    def turned(qkv):
        return jnp.transpose(qkv, (0, 2, 1, 3))

    masters = (turned(qkv_weight), proj_weight, up_weight, down_weight, norm_params)
    firsts = (turned(qkv_first), proj_first, up_first, down_first, norm_first)
    seconds = (turned(qkv_second), proj_second, up_second, down_second, norm_second)
    piece = norm_params.shape[2]
    norm_in = norm_params.astype(BF16).astype(F32).reshape(4 * layer_count, piece)
    norm_in = jnp.pad(norm_in, ((0, 0), (0, 128 - piece)))
    flat = (local_slots, width)
    kept = run_forward(dims, row_lengths, block_input.reshape(flat), norm_in, masters[:4])
    back = run_backward(dims, row_lengths, output_grad.reshape(flat), kept[1], kept[2:])
    outs = run_adam(dims, back[2], back[1], kept[0], back[0], back[3], masters, firsts, seconds)
    whole = (row_count,) + flat
    final = [outs[0].reshape(whole), outs[1].reshape(whole), back[2][0, 0]]
    for group in range(5):
        mine = outs[2 + 5 * group : 7 + 5 * group]
        final += [turned(mine[0])] + list(mine[1:])
    return tuple(final)


def solution(mesh):
    return jax.shard_map(
        body,
        mesh=mesh,
        in_specs=(
            P("dp", "seq", None),
            P("dp", "seq", None),
            P("dp"),
            P(None, "dp", None, "seq"),
            P(None, "seq", "dp"),
            P(None, "dp", "seq"),
            P(None, "seq", "dp"),
            P(None, None, ("dp", "seq")),
            P(None, "dp", None, "seq"),
            P(None, "seq", "dp"),
            P(None, "dp", "seq"),
            P(None, "seq", "dp"),
            P(None, None, ("dp", "seq")),
            P(None, "dp", None, "seq"),
            P(None, "seq", "dp"),
            P(None, "dp", "seq"),
            P(None, "seq", "dp"),
            P(None, None, ("dp", "seq")),
        ),
        out_specs=(
            P("dp", "seq", None),
            P("dp", "seq", None),
            P(),
            P(None, "dp", None, "seq"),
            P(None, "seq", "dp"),
            P(None, "dp", "seq"),
            P(None, "seq", "dp"),
            P(None, None, ("dp", "seq")),
            P(None, "dp", None, "seq"),
            P(None, "seq", "dp"),
            P(None, "dp", "seq"),
            P(None, "seq", "dp"),
            P(None, None, ("dp", "seq")),
            P(None, "dp", None, "seq"),
            P(None, "seq", "dp"),
            P(None, "dp", "seq"),
            P(None, "seq", "dp"),
            P(None, None, ("dp", "seq")),
            P(None, "dp", None, "seq"),
            P(None, "seq", "dp"),
            P(None, "dp", "seq"),
            P(None, "seq", "dp"),
            P(None, None, ("dp", "seq")),
            P(None, "dp", None, "seq"),
            P(None, "seq", "dp"),
            P(None, "dp", "seq"),
            P(None, "seq", "dp"),
            P(None, None, ("dp", "seq")),
        ),
        check_vma=False,
    )
```

```python
import functools

import jax
import jax.numpy as jnp
import numpy as np
from jax import lax
from jax.experimental import pallas as pl
from jax.experimental.pallas import tpu as pltpu
from jax.sharding import PartitionSpec as P

H = 8
HD = 128
STEP = 5
CORES = 2
ZSIZE = 4

EPS_NORM = 1e-05
BETA_ONE = 0.5
BETA_TWO = 0.75
LEARN_RATE = 0.03
NORM_RATE = 0.3
WEIGHT_DECAY = 0.1
CLIP_NORM = 0.1
ADAM_EPS = 1e-08

UNITS = 12
DEPTH = 2
DEEPER = (4, 6)
PUMPS = (
    ((0, 1, 2), (16, 17)),
    ((3,), (18,)),
    ((4,), (19,)),
    ((5, 6), (20, 21)),
    ((7,), (22,)),
    ((8,), (23,)),
    ((9,), ()),
    ((10, 11), ()),
    ((12, 13, 14, 15), ()),
)

F32 = jnp.float32
BF16 = jnp.bfloat16
MESH = pl.DeviceIdType.MESH
SCORE_SCALE = HD ** (-0.5)
GELU_A = (2.0 / np.pi) ** 0.5
GELU_B = 0.044715


def slope_table(head_count):
    return np.power(2.0, -8.0 * (np.arange(head_count) + 1.0) / head_count)


def ahead(u):
    return u + 1 + DEPTH + sum(u >= step for step in DEEPER)


def slope_at(head):
    value = jnp.float32(0.0)
    for index, slope in enumerate(slope_table(H)):
        value = jnp.where(head == index, jnp.float32(slope), value)
    return value


def weight_cols(c):
    return pl.ds(0, 3 * c), pl.ds(3 * c, c), pl.ds(4 * c, 4 * c), pl.ds(8 * c, 4 * c)


def mm_nn(a, b):
    return lax.dot_general(a, b, (((1,), (0,)), ((), ())), preferred_element_type=F32)


def mm_nt(a, b):
    return lax.dot_general(a, b, (((1,), (1,)), ((), ())), preferred_element_type=F32)


def mm_tn(a, b):
    return lax.dot_general(a, b, (((0,), (0,)), ((), ())), preferred_element_type=F32)


def normalise(v):
    centered = v - jnp.mean(v, axis=-1, keepdims=True)
    inverse = lax.rsqrt(jnp.mean(centered * centered, axis=-1, keepdims=True) + EPS_NORM)
    return centered * inverse, inverse


def rows_of(index, size):
    return pl.ds(pl.multiple_of(index * size, size), size)


class Place:
    def __init__(self, zn, xn, yn):
        self.zn, self.xn, self.yn = zn, xn, yn
        self.dp = lax.axis_index("dp")
        self.seq = lax.axis_index("seq")
        self.z, self.x = self.dp // xn, lax.rem(self.dp, xn)
        self.y, self.c = self.seq // CORES, lax.rem(self.seq, CORES)

    def zo(self, k):
        return lax.rem(self.z + k + self.zn, self.zn)

    def xo(self, k):
        return lax.rem(self.x + k + self.xn, self.xn)

    def yo(self, k):
        return lax.rem(self.y + k + self.yn, self.yn)

    def dev(self, dz=0, dx=0, dy=0, dc=0):
        core = (1 - self.c) if dc else self.c
        return (self.zo(dz) * self.xn + self.xo(dx), self.yo(dy) * CORES + core)

    def dp_at(self, dz, dx):
        return self.zo(dz) * self.xn + self.xo(dx)

    def seq_at(self, dy, dc):
        core = (1 - self.c) if dc else self.c
        return self.yo(dy) * CORES + core

    def seq_others(self):
        return [(y, c) for c in range(CORES) for y in range(self.yn) if y or c]

    def dp_others(self):
        return [(z, x) for x in range(self.xn) for z in range(self.zn) if z or x]

    def peers(self, wide=False):
        if wide:
            out = [self.dev(dy=y, dc=c) for y, c in self.seq_others()]
            return out + [self.dev(dz=z, dx=x) for z, x in self.dp_others()]
        out = [self.dev(dc=1)]
        out += [self.dev(dy=k) for k in range(1, self.yn)]
        out += [self.dev(dx=k) for k in range(1, self.xn)]
        out += [self.dev(dz=k) for k in range(1, self.zn)]
        return out

    def barrier(self, wide=False):
        sem = pltpu.get_barrier_semaphore()
        peers = self.peers(wide)
        for peer in peers:
            pl.semaphore_signal(sem, inc=1, device_id=peer, device_id_type=MESH)
        pl.semaphore_wait(sem, len(peers))


def near_first(count):
    order = []
    for k in range(1, count):
        order.append((min(k, count - k), k))
    return [k for unused, k in sorted(order)]


def remote(src, dst, send, recv, dev):
    return pltpu.make_async_remote_copy(
        src_ref=src, dst_ref=dst, send_sem=send, recv_sem=recv, device_id=dev, device_id_type=MESH
    )


def all_sum(place, value, slots, send, recv):
    stages = (
        (CORES, place.c, lambda k: place.dev(dc=1), lambda k: 1 - place.c),
        (place.yn, place.y, lambda k: place.dev(dy=k), lambda k: place.yo(-k)),
        (place.xn, place.x, lambda k: place.dev(dx=k), lambda k: place.xo(-k)),
        (place.zn, place.z, lambda k: place.dev(dz=k), lambda k: place.zo(-k)),
    )
    base = 0
    at = 0
    for size, mine, target, origin in stages:
        slots[base + mine] = value
        own = slots.at[base + mine]
        for k in range(1, size):
            remote(own, own, send.at[at + k - 1], recv.at[at + k - 1], target(k)).start()
        for k in range(1, size):
            came = slots.at[base + origin(k)]
            remote(came, came, send.at[at + k - 1], recv.at[at + k - 1], target(k)).wait_recv()
        for k in range(1, size):
            remote(own, own, send.at[at + k - 1], recv.at[at + k - 1], target(k)).wait_send()
        value = slots[base]
        for k in range(1, size):
            value = value + slots[base + k]
        base += size
        at += size - 1
    return value


def sum_slots(zn, xn, yn):
    return CORES + yn + xn + zn, 1 + (yn - 1) + (xn - 1) + (zn - 1)


def all_sum_wide(place, value, slots, send, recv):
    p = place
    stages = (
        (p.seq, [(p.dev(dy=y, dc=c), p.seq_at(-y, c)) for y, c in p.seq_others()]),
        (p.dp, [(p.dev(dz=z, dx=x), p.dp_at(-z, -x)) for z, x in p.dp_others()]),
    )
    base = 0
    at = 0
    for mine, others in stages:
        slots[base + mine] = value
        own = slots.at[base + mine]
        for k, (target, origin) in enumerate(others):
            remote(own, own, send.at[at + k], recv.at[at + k], target).start()
        for k, (target, origin) in enumerate(others):
            came = slots.at[base + origin]
            remote(came, came, send.at[at + k], recv.at[at + k], target).wait_recv()
        for k, (target, origin) in enumerate(others):
            remote(own, own, send.at[at + k], recv.at[at + k], target).wait_send()
        value = slots[base]
        for k in range(len(others)):
            value = value + slots[base + k + 1]
        base += len(others) + 1
        at += len(others)
    return value


class Gather:
    def __init__(self, place, buf, block, send, recv):
        self.p, self.buf, self.block, self.send, self.recv = place, buf, block, send, recv

    def at(self, dy, dc):
        return self.buf.at[rows_of(self.p.seq_at(dy, dc), self.block)]

    def start(self):
        p, own = self.p, self.at(0, 0)
        for k in range(1, p.yn):
            remote(own, own, self.send.at[k], self.recv.at[k], p.dev(dy=k)).start()
        remote(own, own, self.send.at[0], self.recv.at[0], p.dev(dc=1)).start()

    def wait_chip(self):
        came = self.at(0, 1)
        remote(came, came, self.send.at[0], self.recv.at[0], self.p.dev(dc=1)).wait_recv()

    def forward(self):
        p = self.p
        for k in range(1, p.yn):
            came = self.at(-k, 0)
            remote(came, came, self.send.at[k], self.recv.at[k], p.dev(dy=k)).wait_recv()
            f = p.yn - 1 + k
            remote(came, came, self.send.at[f], self.recv.at[f], p.dev(dc=1)).start()

    def wait_rest(self):
        p = self.p
        for k in range(1, p.yn):
            f = p.yn - 1 + k
            came = self.at(-k, 1)
            remote(came, came, self.send.at[f], self.recv.at[f], p.dev(dc=1)).wait_recv()
        own = self.at(0, 0)
        for k in range(1, p.yn):
            remote(own, own, self.send.at[k], self.recv.at[k], p.dev(dy=k)).wait_send()
            f = p.yn - 1 + k
            sent = self.at(-k, 0)
            remote(sent, sent, self.send.at[f], self.recv.at[f], p.dev(dc=1)).wait_send()
        remote(own, own, self.send.at[0], self.recv.at[0], p.dev(dc=1)).wait_send()


class Scatter:
    def __init__(self, place, sbuf, rbuf, ysend, yrecv, acc, send, recv):
        self.p = place
        self.sbuf, self.rbuf, self.ysend, self.yrecv, self.acc = sbuf, rbuf, ysend, yrecv, acc
        self.send, self.recv = send, recv

    def core(self, k):
        return remote(
            self.sbuf.at[k], self.rbuf.at[k], self.send.at[k], self.recv.at[k], self.p.dev(dc=1)
        )

    def cross(self, k):
        s = self.p.yn + k - 1
        return remote(
            self.ysend.at[k - 1],
            self.yrecv.at[k - 1],
            self.send.at[s],
            self.recv.at[s],
            self.p.dev(dy=k),
        )

    def start(self, part):
        p = self.p
        for k in list(range(1, p.yn)) + [0]:
            self.sbuf[k] = part(p.seq_at(k, 1)).astype(BF16)
            self.core(k).start()
            mine = part(p.seq_at(k, 0))
            self.core(k).wait_recv()
            mine = mine + self.rbuf[k].astype(F32)
            if k:
                self.ysend[k - 1] = mine.astype(BF16)
                self.cross(k).start()
            else:
                self.acc[...] = mine

    def wait(self):
        p = self.p
        for k in range(1, p.yn):
            self.cross(k).wait_recv()
        for k in range(1, p.yn):
            self.cross(k).wait_send()
        for k in range(p.yn):
            self.core(k).wait_send()

    def rows(self, at):
        value = self.acc[at, :]
        for k in range(1, self.p.yn):
            value = value + self.yrecv[k - 1, at, :].astype(F32)
        return value


def row_loop(total, step, fn):
    def one(i, unused):
        fn(rows_of(i, step))
        return unused

    lax.fori_loop(0, total // step, one, 0)


def twice(v):
    return jnp.concatenate([v, v], axis=1)


def key_bias(bias, slots, length, slope):
    def one(i, unused):
        key = i * 64 + lax.broadcasted_iota(jnp.int32, (64, 128), 0)
        bias[rows_of(i, 64), :] = jnp.where(key < length, slope * key.astype(F32), -jnp.inf)
        return unused

    lax.fori_loop(0, slots // 64, one, 0)


def turn_rows(target, rows, slots):
    for c in range(slots // 256):
        at = pl.ds(c * 256, 256)
        target[:, at] = rows(at).astype(F32).T.astype(BF16)


def forward_kernel(dims, *refs):
    (layers, slots, width, block, local_width, local_ff, groups, zn, xn, yn) = dims
    heads = local_width // HD
    refs = list(refs)

    def take(count):
        out = refs[:count]
        del refs[:count]
        return out

    lengths, x_in, norm_in = take(3)
    masters = take(4)
    out, norm_out = take(2)
    w_save = take(1)[0]
    xn1_save, xn2_save, qkv_save, ctx_save, lse_save, act_save, dact_save, hid_save, mid_save = take(9)
    w = take(1)[0]
    xn1, xn2, qkv, ctx, lse, act, dact, hid, mid, upper, norm_place, bias, turned = take(13)
    sbuf, rbuf, ysend, yrecv, acc, nslots = take(6)
    zsend, zrecv, xsend, xrecv, wsave_sem = take(5)
    ag_send, ag_recv, rs_send, rs_recv, ns_send, ns_recv, save_sem = take(7)

    p = Place(zn, xn, yn)
    z_order = near_first(zn)
    length = lengths[0]
    cols_qkv, cols_o, cols_up, cols_down = weight_cols(local_width)

    unit_count = UNITS * layers
    slopes = [slope_at(p.seq * heads + h) for h in range(heads)]

    def unit_cols(u):
        return pl.ds((u % UNITS) * local_width, local_width)

    def z_copy(u, dz, zi):
        here = w.at[u // UNITS, zi, p.x, :, unit_cols(u)]
        return remote(here, here, zsend.at[u, dz - 1], zrecv.at[u, dz - 1], p.dev(dz=dz))

    def x_copy(u, dx, dz):
        here = w.at[u // UNITS, p.zo(-dz), p.x, :, unit_cols(u)]
        return remote(here, here, xsend.at[u, dx - 1, dz], xrecv.at[u, dx - 1, dz], p.dev(dx=dx))

    def prepare(u):
        l, v = divmod(u, UNITS)
        cols = unit_cols(u)
        if v < 3:
            w[l, p.z, p.x, :, cols] = masters[0][l, v].astype(BF16)
        elif 4 <= v < 8:
            source = pl.ds((v - 4) * local_width, local_width)
            w[l, p.z, p.x, :, cols] = masters[2][l, :, source].astype(BF16)
        else:
            source, base = (masters[1], 0) if v == 3 else (masters[3], (v - 8) * local_width)
            for c in range(local_width // 128):
                block_t = source[l, pl.ds(base + c * 128, 128), :].T
                w[l, p.z, p.x, :, pl.ds(v * local_width + c * 128, 128)] = block_t.astype(BF16)

    def start_unit(u):
        for dz in z_order:
            z_copy(u, dz, p.z).start()
        for dx in range(1, xn):
            x_copy(u, dx, 0).start()

    def pump(u):
        for dz in z_order:
            z_copy(u, dz, p.zo(-dz)).wait_recv()
            for dx in range(1, xn):
                x_copy(u, dx, dz).start()
        for later in range(ahead(u - 1), min(ahead(u), unit_count)):
            start_unit(later)

    def pumps(l, *tables):
        for at, units in enumerate(tables):
            if units:

                @pl.when(l == at)
                def _(units=units):
                    for u in units:
                        pump(u)

    def save_weight(l):
        return pltpu.make_async_copy(w.at[l], w_save.at[l], wsave_sem.at[l])

    def need(l, low, high):
        def one(v, unused):
            u = UNITS * l + v
            at = w.at[0, 0, 0, :, pl.ds(0, local_width)]
            for dz in range(zn):
                for dx in range(1, xn):
                    remote(
                        at, at, xsend.at[u, dx - 1, dz], xrecv.at[u, dx - 1, dz], p.dev(dx=dx)
                    ).wait_recv()
            return unused

        lax.fori_loop(low, high, one, 0)

    def finish_weight(l):
        def one(v, unused):
            u = UNITS * l + v
            at = w.at[0, 0, 0, :, pl.ds(0, local_width)]
            for dz in z_order:
                remote(
                    at, at, zsend.at[u, dz - 1], zrecv.at[u, dz - 1], p.dev(dz=dz)
                ).wait_send()
            for dz in range(zn):
                for dx in range(1, xn):
                    remote(
                        at, at, xsend.at[u, dx - 1, dz], xrecv.at[u, dx - 1, dz], p.dev(dx=dx)
                    ).wait_send()
            return unused

        lax.fori_loop(0, UNITS, one, 0)
        save_weight(l).wait()

    def weight(l, cols):
        return w[l, :, :, :, cols].reshape(width, cols.size)

    def save(l, which, src, dst):
        return pltpu.make_async_copy(src, dst, save_sem.at[l, which])

    def saves(l):
        return (
            save(l, 0, xn1.at[l], xn1_save.at[l]),
            save(l, 1, xn2.at[l], xn2_save.at[l]),
            save(l, 2, qkv.at[l], qkv_save.at[l]),
            save(l, 3, ctx.at[l], ctx_save.at[l]),
            save(l, 4, lse.at[l], lse_save.at[l]),
            save(l, 5, act.at[l], act_save.at[l]),
            save(l, 6, dact.at[l], dact_save.at[l]),
            save(l, 7, hid.at[l], hid_save.at[l]),
            save(l, 8, mid.at[l], mid_save.at[l]),
        )

    p.barrier()
    for u in range(ahead(-1)):
        prepare(u)
        start_unit(u)
    piece = width // (groups * CORES * yn)
    at_lane = (p.dp * CORES * yn + p.seq) * piece
    norm_place[...] = jnp.zeros_like(norm_place)
    norm_place[:, rows_of(at_lane // 128, 128)] = pltpu.roll(norm_in[...], lax.rem(at_lane, 128), 1)
    norm_out[...] = all_sum(p, norm_place[...], nslots, ns_send, ns_recv)
    for u in range(ahead(-1), UNITS):
        prepare(u)

    def load_in(at):
        hid[0, at, :] = x_in[at, :].astype(F32)

    row_loop(block, 64, load_in)
    first = p.seq * block

    def norm_row(index):
        return norm_out[pl.ds(index, 1), :]

    def norm_into(l, source, target, row):
        gain, bias = norm_row(4 * l + row), norm_row(4 * l + row + 1)

        def one(i, unused):
            scaled, inverse = normalise(source[l, rows_of(i, 32), :])
            at = pl.ds(pl.multiple_of(first + i * 32, 32), 32)
            target[l, at, :] = (scaled * gain + bias).astype(BF16)
            return unused

        lax.fori_loop(0, block // 32, one, 0)

    def attention(l):
        step = 256
        causal = lax.broadcasted_iota(jnp.int32, (step, step), 0) <= lax.broadcasted_iota(
            jnp.int32, (step, step), 1
        )
        for h in range(heads):
            cols = pl.ds(h * HD, HD)
            k_cols = pl.ds(local_width + h * HD, HD)
            v_cols = pl.ds(2 * local_width + h * HD, HD)
            key_bias(bias, slots, length, slopes[h])
            turn_rows(turned, lambda at: qkv[l, at, v_cols], slots)
            for b in range(slots // step):
                here = pl.ds(b * step, step)
                before = pl.ds(0, b * step)
                q = qkv[l, here, cols]
                raw = mm_nt(qkv[l, here, k_cols], q) * SCORE_SCALE + twice(bias[here, :])
                raw = jnp.where(causal, raw, -jnp.inf)
                top = jnp.max(raw, axis=0, keepdims=True)
                if b:
                    past = mm_nt(qkv[l, before, k_cols], q) * SCORE_SCALE + twice(bias[before, :])
                    top = jnp.maximum(top, jnp.max(past, axis=0, keepdims=True))
                e_here = jnp.exp(raw - top)
                total = jnp.sum(e_here, axis=0, keepdims=True)
                value = mm_nn(turned[:, here], e_here.astype(BF16))
                if b:
                    e_past = jnp.exp(past - top)
                    total = total + jnp.sum(e_past, axis=0, keepdims=True)
                    value = value + mm_nn(turned[:, before], e_past.astype(BF16))
                ctx[l, here, cols] = (value / total).T.astype(BF16)
                lse[l, pl.ds(h, 1), here] = top + jnp.log(total)

    def layer(l, unused):
        last = layers - 1
        g_one = Gather(p, xn1.at[l], block, ag_send.at[2 * l], ag_recv.at[2 * l])
        g_two = Gather(p, xn2.at[l], block, ag_send.at[2 * l + 1], ag_recv.at[2 * l + 1])
        rs = [
            Scatter(
                p, sbuf, rbuf, ysend, yrecv, acc,
                rs_send.at[2 * l + i], rs_recv.at[2 * l + i],
            )
            for i in range(2)
        ]
        save_at = saves(l)
        save_at[7].start()
        norm_into(l, hid, xn1, 0)
        g_one.start()

        @pl.when(l == 0)
        def _():
            for u in range(UNITS, unit_count):
                prepare(u)

        pumps(l, *PUMPS[0])

        def project(index):
            at = rows_of(index, block)
            qkv[l, at, :] = mm_nn(xn1[l, at, :], weight(l, cols_qkv)).astype(BF16)

        g_one.wait_chip()
        g_one.forward()
        need(l, 0, 3)
        project(p.seq_at(0, 0))
        project(p.seq_at(0, 1))
        pumps(l, *PUMPS[1])
        g_one.wait_rest()
        save_at[0].start()
        for k in range(1, yn):
            project(p.seq_at(-k, 0))
            project(p.seq_at(-k, 1))
        save_at[2].start()
        attention(l)
        save_at[3].start()
        save_at[4].start()
        pumps(l, *PUMPS[2])
        need(l, 3, 4)
        rs[0].start(lambda b: mm_nt(ctx[l, rows_of(b, block), :], weight(l, cols_o)))
        pumps(l, *PUMPS[3])
        rs[0].wait()

        def add_middle(at):
            mid[l, at, :] = hid[l, at, :] + rs[0].rows(at)

        row_loop(block, 32, add_middle)
        save_at[8].start()
        norm_into(l, mid, xn2, 2)
        g_two.start()
        pumps(l, *PUMPS[4])
        need(l, 4, 8)

        def expand(index):
            base = pl.multiple_of(index * block, block)
            upper[...] = mm_nn(xn2[l, pl.ds(base, block), :], weight(l, cols_up))

            def one(i, unused):
                u = upper[rows_of(i, 16), :]
                at = pl.ds(pl.multiple_of(base + i * 16, 16), 16)
                square = u * u
                t = jnp.tanh(GELU_A * u * (1.0 + GELU_B * square))
                half = 0.5 * (1.0 + t)
                act[l, at, :] = (u * half).astype(BF16)
                slope = (0.5 * GELU_A) * u * (1.0 - t * t) * (1.0 + (3.0 * GELU_B) * square)
                dact[l, at, :] = (half + slope).astype(BF16)
                return unused

            lax.fori_loop(0, block // 16, one, 0)

        expand(p.seq_at(0, 0))
        g_two.wait_chip()
        expand(p.seq_at(0, 1))
        pumps(l, *PUMPS[5])
        g_two.forward()
        pumps(l, *PUMPS[6])
        g_two.wait_rest()
        save_at[1].start()
        for k in range(1, yn):
            expand(p.seq_at(-k, 0))
            expand(p.seq_at(-k, 1))
        save_at[5].start()
        save_at[6].start()
        pumps(l, *PUMPS[7])
        need(l, 8, 12)
        save_weight(l).start()
        rs[1].start(lambda b: mm_nt(act[l, rows_of(b, block), :], weight(l, cols_down)))
        pumps(l, *PUMPS[8])
        rs[1].wait()

        @pl.when(l < last)
        def _():
            def add_next(at):
                hid[l + 1, at, :] = mid[l, at, :] + rs[1].rows(at)

            row_loop(block, 32, add_next)

        @pl.when(l == last)
        def _():
            def add_out(at):
                out[at, :] = mid[l, at, :] + rs[1].rows(at)

            row_loop(block, 32, add_out)

        return unused

    lax.fori_loop(0, layers, layer, 0)

    def finish(l, unused):
        finish_weight(l)
        for item in saves(l):
            item.wait()
        return unused

    lax.fori_loop(0, layers, finish, 0)


def run_forward(dims, lengths, x_in, norm_in, masters):
    (layers, slots, width, block, local_width, local_ff, groups, zn, xn, yn) = dims
    shard = width // groups
    slot_count, sem_count = sum_slots(zn, xn, yn)

    def saved(*shape, dtype=BF16):
        return jax.ShapeDtypeStruct((layers,) + shape, dtype)

    vmem = pl.BlockSpec(memory_space=pltpu.VMEM)
    smem = pl.BlockSpec(memory_space=pltpu.SMEM)
    hbm = pl.BlockSpec(memory_space=pl.ANY)
    kept = [
        saved(zn, xn, shard, UNITS * local_width),
        saved(slots, width),
        saved(slots, width),
        saved(slots, 3 * local_width),
        saved(slots, local_width),
        saved(8, slots, dtype=F32),
        saved(slots, local_ff),
        saved(slots, local_ff),
        saved(block, width, dtype=F32),
        saved(block, width, dtype=F32),
    ]
    dma = pltpu.SemaphoreType.DMA
    return pl.pallas_call(
        functools.partial(forward_kernel, dims),
        out_shape=[
            jax.ShapeDtypeStruct((block, width), F32),
            jax.ShapeDtypeStruct((4 * layers, width), F32),
        ]
        + kept,
        in_specs=[smem] + [vmem] * 6,
        out_specs=[vmem, vmem] + [hbm] * len(kept),
        scratch_shapes=[pltpu.VMEM(k.shape, k.dtype) for k in kept]
        + [
            pltpu.VMEM((block, local_ff), F32),
            pltpu.VMEM((4 * layers, width), F32),
            pltpu.VMEM((slots, 128), F32),
            pltpu.VMEM((HD, slots), BF16),
            pltpu.VMEM((yn, block, width), BF16),
            pltpu.VMEM((yn, block, width), BF16),
            pltpu.VMEM((yn - 1, block, width), BF16),
            pltpu.VMEM((yn - 1, block, width), BF16),
            pltpu.VMEM((block, width), F32),
            pltpu.VMEM((slot_count, 4 * layers, width), F32),
            dma((UNITS * layers, zn - 1)),
            dma((UNITS * layers, zn - 1)),
            dma((UNITS * layers, xn - 1, zn)),
            dma((UNITS * layers, xn - 1, zn)),
            dma((layers,)),
            dma((2 * layers, 2 * yn - 1)),
            dma((2 * layers, 2 * yn - 1)),
            dma((2 * layers, 2 * yn - 1)),
            dma((2 * layers, 2 * yn - 1)),
            dma((sem_count,)),
            dma((sem_count,)),
            dma((layers, 9)),
        ],
        compiler_params=pltpu.CompilerParams(
            collective_id=0, has_side_effects=True, vmem_limit_bytes=62 * 2**20
        ),
        name="forward_layers",
    )(lengths, x_in, norm_in, *masters)

def backward_kernel(dims, *refs):
    (layers, slots, width, block, local_width, local_ff, groups, zn, xn, yn) = dims
    heads = local_width // HD
    shard = width // groups
    slab = shard * xn
    refs = list(refs)

    def take(count):
        out = refs[:count]
        del refs[:count]
        return out

    lengths, g_in, norms = take(3)
    kept = take(10)
    g_out, norm_grad, total_out = take(3)
    shards = take(1)[0]
    held = take(10)
    w, xn1, xn2, qkv, ctx, lse, act, dact, hid, mid = held
    gfull, gbfull, gctx, dqkv, dk, dv, bias, turned, g, gm, npart = take(11)
    dw, xland, zland = take(3)
    sbuf, rbuf, ysend, yrecv, acc, nslots, tslots = take(7)
    zsend, zrecv, xsend, xrecv = take(4)
    ag_send, ag_recv, rs_send, rs_recv, ns_send, ns_recv, ts_send, ts_recv, load_sem = take(9)

    p = Place(zn, xn, yn)
    length = lengths[0]
    first = p.seq * block
    gu = dact
    w_all = kept[0]

    slopes = [slope_at(p.seq * heads + h) for h in range(heads)]
    weight_at = weight_cols(local_width)
    cols_qkv, cols_o, cols_up, cols_down = weight_at

    def load(l, which):
        if which < 4:
            cols = weight_at[which]
            return pltpu.make_async_copy(w_all.at[l, :, :, :, cols], w.at[:, :, :, cols], load_sem.at[which])
        return pltpu.make_async_copy(kept[which - 3].at[l], held[which - 3], load_sem.at[which])

    def weight(cols):
        return w[:, :, :, cols].reshape(width, cols.size)

    def unit_cols(v):
        return pl.ds(v * local_width, local_width)

    def x_copy(l, v, dx):
        cols = unit_cols(v)
        return remote(
            dw.at[:, p.xo(dx), :, cols],
            xland.at[l, dx - 1, :, :, cols],
            xsend.at[l, v, dx - 1],
            xrecv.at[l, v, dx - 1],
            p.dev(dx=dx),
        )

    def z_copy(l, v, zi):
        cols = unit_cols(v)
        return remote(
            dw.at[p.zo(zi), p.x, :, cols],
            zland.at[l, zi - 1, :, cols],
            zsend.at[l, v, zi - 1],
            zrecv.at[l, v, zi - 1],
            p.dev(dz=zi),
        )

    z_order = near_first(zn)
    zi_order = z_order[::-1] + [0]

    def weight_grad(left, right, low, count):
        def one(i, unused):
            part = mm_tn(left[:, rows_of(i, slab)], right[...]).astype(BF16)
            dw[i, :, :, pl.ds(low * local_width, count * local_width)] = part.reshape(
                xn, shard, count * local_width
            )
            return unused

        lax.fori_loop(0, zn, one, 0)

    def send_x(l, *units):
        for v in units:
            for dx in range(1, xn):
                x_copy(l, v, dx).start()

    def reduce_x(l, *units):
        for v in units:
            cols = unit_cols(v)
            for dx in range(1, xn):
                x_copy(l, v, dx).wait_recv()
            for zi in zi_order:
                zz = p.zo(zi)

                def one(i, unused, zi=zi, cols=cols, zz=zz):
                    here = rows_of(i, 32)
                    value = dw[zz, p.x, here, cols].astype(F32)
                    for dx in range(1, xn):
                        value = value + xland[l, dx - 1, zz, here, cols].astype(F32)
                    if zi:
                        dw[zz, p.x, here, cols] = value.astype(BF16)
                    else:
                        shards[l, here, cols] = value
                    return unused

                lax.fori_loop(0, shard // 32, one, 0)
                if zi:
                    z_copy(l, v, zi).start()

    def reduce_z(l, low, high):
        def unit(v, unused):
            cols = pl.ds(pl.multiple_of(v * local_width, local_width), local_width)
            here = dw.at[0, 0, :, pl.ds(0, local_width)]
            for zi in z_order:
                remote(
                    here, here, zsend.at[l, v, zi - 1], zrecv.at[l, v, zi - 1], p.dev(dz=zi)
                ).wait_recv()

            def one(at):
                value = shards[l, at, cols]
                for zi in range(1, zn):
                    value = value + zland[l, zi - 1, at, cols].astype(F32)
                shards[l, at, cols] = value

            row_loop(shard, 32, one)
            for zi in z_order:
                remote(
                    here, here, zsend.at[l, v, zi - 1], zrecv.at[l, v, zi - 1], p.dev(dz=zi)
                ).wait_send()
            every = dw.at[:, 0, :, pl.ds(0, local_width)]
            for dx in range(1, xn):
                remote(
                    every, every, xsend.at[l, v, dx - 1], xrecv.at[l, v, dx - 1], p.dev(dx=dx)
                ).wait_send()
            return unused

        lax.fori_loop(low, high, unit, 0)

    def norm_back(l, source, rs, base, row, target, low):
        gain = norms[pl.ds(4 * l + row, 1), :]
        zero = jnp.zeros((8, width), F32)

        def one(i, carry):
            at = rows_of(i, 32)
            scaled, inverse = normalise(source[at, :])
            e = rs.rows(at)
            eg = e * gain
            part = inverse * (
                eg
                - jnp.mean(eg, axis=-1, keepdims=True)
                - scaled * jnp.mean(eg * scaled, axis=-1, keepdims=True)
            )
            value = base[at, :] + part
            target[at, :] = value
            if low is not None:
                low[pl.ds(pl.multiple_of(first + i * 32, 32), 32), :] = value.astype(BF16)
            es = e * scaled
            gains, biases = carry
            for r in range(4):
                gains = gains + es[r * 8 : r * 8 + 8]
                biases = biases + e[r * 8 : r * 8 + 8]
            return gains, biases

        gains, biases = lax.fori_loop(0, block // 32, one, (zero, zero))
        npart[pl.ds(4 * l + row, 1), :] = jnp.sum(gains, axis=0, keepdims=True)
        npart[pl.ds(4 * l + row + 1, 1), :] = jnp.sum(biases, axis=0, keepdims=True)

    def attention(between):
        step = 256
        causal = lax.broadcasted_iota(jnp.int32, (step, step), 0) <= lax.broadcasted_iota(
            jnp.int32, (step, step), 1
        )
        for h in range(heads):
            cols = pl.ds(h * HD, HD)
            k_cols = pl.ds(local_width + h * HD, HD)
            v_cols = pl.ds(2 * local_width + h * HD, HD)
            key_bias(bias, slots, length, slopes[h])
            turn_rows(turned, lambda at: qkv[at, k_cols], slots)
            for b in range(slots // step):
                here = pl.ds(b * step, step)
                before = pl.ds(0, b * step)
                q = qkv[here, cols]
                gc = gctx[here, cols]
                shift = lse[pl.ds(h, 1), here]
                raw = mm_nt(qkv[here, k_cols], q) * SCORE_SCALE + twice(bias[here, :])
                p_here = jnp.exp(jnp.where(causal, raw, -jnp.inf) - shift)
                dp_here = mm_nt(qkv[here, v_cols], gc)
                delta = jnp.sum(p_here * dp_here, axis=0, keepdims=True)
                dv[here, :] = mm_nn(p_here.astype(BF16), gc)
                if b:
                    past = mm_nt(qkv[before, k_cols], q) * SCORE_SCALE + twice(bias[before, :])
                    p_past = jnp.exp(past - shift)
                    dp_past = mm_nt(qkv[before, v_cols], gc)
                    delta = delta + jnp.sum(p_past * dp_past, axis=0, keepdims=True)
                    dv[before, :] += mm_nn(p_past.astype(BF16), gc)
                ds_here = (p_here * (dp_here - delta)).astype(BF16)
                dq = mm_nn(turned[:, here], ds_here)
                dk[here, :] = mm_nn(ds_here, q)
                if b:
                    ds_past = (p_past * (dp_past - delta)).astype(BF16)
                    dq = dq + mm_nn(turned[:, before], ds_past)
                    dk[before, :] += mm_nn(ds_past, q)
                dqkv[here, cols] = (dq * SCORE_SCALE).T.astype(BF16)
                between(h * (slots // step) + b + 1, heads * (slots // step))

            def store(at):
                dqkv[at, k_cols] = (dk[at, :] * SCORE_SCALE).astype(BF16)
                dqkv[at, v_cols] = dv[at, :].astype(BF16)

            row_loop(slots, 64, store)

    p.barrier(wide=True)

    def mask_in(i, unused):
        at = rows_of(i, 32)
        slot = first + i * 32 + lax.broadcasted_iota(jnp.int32, (32, 1), 0)
        g[at, :] = jnp.where(slot < length, g_in[at, :].astype(F32), 0.0)
        return unused

    lax.fori_loop(0, block // 32, mask_in, 0)
    load_order = (3, 10, 2, 9, 5, 12, 1, 7, 6, 8, 0, 4, 11)

    def layer(step, unused):
        l = layers - 1 - step
        later = l + 1
        for which in load_order:
            load(l, which).start()
        g_one = Gather(p, gfull, block, ag_send.at[2 * l], ag_recv.at[2 * l])
        g_two = Gather(p, gbfull, block, ag_send.at[2 * l + 1], ag_recv.at[2 * l + 1])
        rs = [
            Scatter(
                p, sbuf, rbuf, ysend, yrecv, acc, rs_send.at[2 * l + i], rs_recv.at[2 * l + i]
            )
            for i in range(2)
        ]

        def low_in(i, unused):
            at = pl.ds(pl.multiple_of(first + i * 32, 32), 32)
            gfull[at, :] = g[rows_of(i, 32), :].astype(BF16)
            return unused

        lax.fori_loop(0, block // 32, low_in, 0)
        g_one.start()

        load(l, 3).wait()
        load(l, 10).wait()

        def upper_grad(index):
            at = rows_of(index, block)
            value = mm_nn(gfull[at, :], weight(cols_down))
            gu[at, :] = (value * dact[at, :].astype(F32)).astype(BF16)

        upper_grad(p.seq_at(0, 0))
        g_one.wait_chip()
        upper_grad(p.seq_at(0, 1))
        g_one.forward()

        @pl.when(step > 0)
        def _():
            reduce_x(later, 0)
            send_x(later, 2)

        g_one.wait_rest()
        for k in range(1, yn):
            upper_grad(p.seq_at(-k, 0))
            upper_grad(p.seq_at(-k, 1))
        load(l, 2).wait()
        rs[0].start(lambda b: mm_nt(gu[rows_of(b, block), :], weight(cols_up)))
        load(l, 9).wait()
        load(l, 5).wait()

        @pl.when(step > 0)
        def _():
            reduce_z(later, 3, 12)

        weight_grad(gfull, act, 8, 4)
        send_x(l, 8)
        weight_grad(xn2, gu, 4, 4)
        send_x(l, 9)

        @pl.when(step > 0)
        def _():
            reduce_x(later, 1, 2)

        load(l, 12).wait()
        reduce_x(l, 8)
        send_x(l, 10)
        rs[0].wait()
        norm_back(l, mid, rs[0], g, 2, gm, gbfull)
        g_two.start()
        reduce_x(l, 9)
        send_x(l, 11)
        load(l, 1).wait()

        def context_grad(index):
            at = rows_of(index, block)
            gctx[at, :] = mm_nn(gbfull[at, :], weight(cols_o)).astype(BF16)

        context_grad(p.seq_at(0, 0))
        g_two.wait_chip()
        context_grad(p.seq_at(0, 1))
        reduce_x(l, 10)
        send_x(l, 4)
        g_two.forward()

        @pl.when(step > 0)
        def _():
            reduce_z(later, 0, 3)

        g_two.wait_rest()
        for k in range(1, yn):
            context_grad(p.seq_at(-k, 0))
            context_grad(p.seq_at(-k, 1))
        load(l, 7).wait()
        weight_grad(gbfull, ctx, 3, 1)
        reduce_x(l, 11)
        send_x(l, 5)
        load(l, 6).wait()
        load(l, 8).wait()

        def between(done, count):
            if done == (count * 3) // 8:
                reduce_x(l, 4)
                send_x(l, 6)
            if done == (count * 6) // 8:
                reduce_x(l, 5)
                send_x(l, 7)

        attention(between)
        load(l, 0).wait()
        load(l, 4).wait()

        @pl.when(l == 0)
        def _():
            weight_grad(xn1, dqkv, 0, 3)

        reduce_x(l, 6)
        send_x(l, 3)
        rs[1].start(lambda b: mm_nt(dqkv[rows_of(b, block), :], weight(cols_qkv)))

        @pl.when(l > 0)
        def _():
            weight_grad(xn1, dqkv, 0, 3)

        reduce_x(l, 7)
        send_x(l, 0)
        reduce_x(l, 3)
        send_x(l, 1)
        load(l, 11).wait()
        rs[1].wait()
        norm_back(l, hid, rs[1], gm, 0, g, None)
        return unused

    lax.fori_loop(0, layers, layer, 0)
    reduce_x(0, 0)
    send_x(0, 2)
    reduce_x(0, 1, 2)
    g_out[...] = g[...]
    norm_grad[...] = all_sum(p, npart[...], nslots, ns_send, ns_recv)
    reduce_z(0, 3, 12)
    reduce_z(0, 0, 3)

    def squares(i, total):
        l, at = i // (shard // 8), rows_of(lax.rem(i, shard // 8), 8)
        value = shards[l, at, :]
        value = value * value
        for c in range(UNITS * local_width // 128):
            total = total + value[:, c * 128 : (c + 1) * 128]
        return total

    tile = lax.fori_loop(0, layers * shard // 8, squares, jnp.zeros((8, 128), F32))
    tile = all_sum_wide(p, tile, tslots, ts_send, ts_recv)
    value = norm_grad[...]
    value = value * value
    for c in range(width // 128):
        piece = value[:, c * 128 : (c + 1) * 128]
        for r in range(4 * layers // 8):
            tile = tile + piece[r * 8 : r * 8 + 8]
    total = jnp.sum(jnp.sum(tile, axis=0, keepdims=True), axis=1, keepdims=True)
    total_out[...] = jnp.broadcast_to(jnp.sqrt(total), (8, 128))


def run_backward(dims, lengths, g_in, norms, kept):
    (layers, slots, width, block, local_width, local_ff, groups, zn, xn, yn) = dims
    packed = UNITS * local_width
    shard = width // groups
    slot_count, sem_count = sum_slots(zn, xn, yn)
    vmem = pl.BlockSpec(memory_space=pltpu.VMEM)
    smem = pl.BlockSpec(memory_space=pltpu.SMEM)
    hbm = pl.BlockSpec(memory_space=pl.ANY)
    dma = pltpu.SemaphoreType.DMA
    return pl.pallas_call(
        functools.partial(backward_kernel, dims),
        out_shape=[
            jax.ShapeDtypeStruct((block, width), F32),
            jax.ShapeDtypeStruct((4 * layers, width), F32),
            jax.ShapeDtypeStruct((8, 128), F32),
            jax.ShapeDtypeStruct((layers, shard, packed), F32),
        ],
        in_specs=[smem, vmem, vmem] + [hbm] * len(kept),
        out_specs=[vmem] * 4,
        scratch_shapes=[pltpu.VMEM(k.shape[1:], k.dtype) for k in kept]
        + [
            pltpu.VMEM((slots, width), BF16),
            pltpu.VMEM((slots, width), BF16),
            pltpu.VMEM((slots, local_width), BF16),
            pltpu.VMEM((slots, 3 * local_width), BF16),
            pltpu.VMEM((slots, HD), F32),
            pltpu.VMEM((slots, HD), F32),
            pltpu.VMEM((slots, 128), F32),
            pltpu.VMEM((HD, slots), BF16),
            pltpu.VMEM((block, width), F32),
            pltpu.VMEM((block, width), F32),
            pltpu.VMEM((4 * layers, width), F32),
            pltpu.VMEM((zn, xn, shard, packed), BF16),
            pltpu.VMEM((layers, xn - 1, zn, shard, packed), BF16),
            pltpu.VMEM((layers, zn - 1, shard, packed), BF16),
            pltpu.VMEM((yn, block, width), BF16),
            pltpu.VMEM((yn, block, width), BF16),
            pltpu.VMEM((yn - 1, block, width), BF16),
            pltpu.VMEM((yn - 1, block, width), BF16),
            pltpu.VMEM((block, width), F32),
            pltpu.VMEM((slot_count, 4 * layers, width), F32),
            pltpu.VMEM((CORES * yn + groups, 8, 128), F32),
            dma((layers, UNITS, zn - 1)),
            dma((layers, UNITS, zn - 1)),
            dma((layers, UNITS, xn - 1)),
            dma((layers, UNITS, xn - 1)),
            dma((2 * layers, 2 * yn - 1)),
            dma((2 * layers, 2 * yn - 1)),
            dma((2 * layers, 2 * yn - 1)),
            dma((2 * layers, 2 * yn - 1)),
            dma((sem_count,)),
            dma((sem_count,)),
            dma((CORES * yn + groups - 2,)),
            dma((CORES * yn + groups - 2,)),
            dma((len(kept) + 3,)),
        ],
        compiler_params=pltpu.CompilerParams(
            collective_id=1, has_side_effects=True, vmem_limit_bytes=62 * 2**20
        ),
        name="backward_layers",
    )(lengths, g_in, norms, *kept)


def adam_kernel(dims, *refs):
    (layers, slots, width, block, local_width, local_ff, groups, zn, xn, yn) = dims
    refs = list(refs)

    def take(count):
        out = refs[:count]
        del refs[:count]
        return out

    total, norm_grad, hidden_in, input_in = take(4)
    grads, masters, firsts, seconds = take(4), take(5), take(5), take(5)
    hidden_out, input_out = take(2)
    grad_out, moment_out, variance_out, new_out, copy_out = (take(5) for unused in range(5))
    factor = CLIP_NORM / jnp.maximum(total[0:1, 0:1], CLIP_NORM)
    fix_one = 1.0 / (1.0 - BETA_ONE**STEP)
    fix_two = 1.0 / (1.0 - BETA_TWO**STEP)

    def update(k, at, grad, decay, rate):
        clipped = grad * factor
        momentum = BETA_ONE * firsts[k][at] + (1.0 - BETA_ONE) * clipped
        variance = BETA_TWO * seconds[k][at] + (1.0 - BETA_TWO) * clipped * clipped
        master = masters[k][at]
        size = momentum * fix_one / (jnp.sqrt(variance * fix_two) + ADAM_EPS)
        if decay:
            size = size + decay * master
        fresh = master - rate * size
        grad_out[k][at] = grad
        moment_out[k][at] = momentum
        variance_out[k][at] = variance
        new_out[k][at] = fresh
        copy_out[k][at] = fresh.astype(BF16)

    def matrix(k, at, grad):
        update(k, at, grad, WEIGHT_DECAY, LEARN_RATE)

    hidden_out[...] = hidden_in[...]
    input_out[...] = input_in[...]
    every = slice(None)
    for part in range(3):
        grad = grads[0][0, :, part * local_width : (part + 1) * local_width]
        matrix(0, (0, part, every, every), grad)
    matrix(1, (0, every, every), grads[1][0].T)

    def up_rows(i, unused):
        at = rows_of(i, 16)
        matrix(2, (0, at, every), grads[2][0, at, :])
        return unused

    lax.fori_loop(0, grads[2].shape[1] // 16, up_rows, 0)
    for c in range(grads[3].shape[2] // 128):
        at = pl.ds(c * 128, 128)
        matrix(3, (0, at, every), grads[3][0, :, at].T)

    @pl.when((pl.program_id(0) == 0) & (pl.program_id(1) == 0))
    def _():
        seq_count = CORES * yn
        piece = width // (groups * seq_count)
        at = (lax.axis_index("dp") * seq_count + lax.axis_index("seq")) * piece
        tile = norm_grad[:, rows_of(at // 128, 128)]
        tile = pltpu.roll(tile, lax.rem(128 - lax.rem(at, 128), 128), 1)[:, :piece]
        for l in range(layers):
            update(4, (l,), tile[4 * l : 4 * l + 4], 0.0, NORM_RATE)


def run_adam(dims, total, norm_grad, hidden, input_grad, grad, masters, firsts, seconds):
    (layers, slots, width, block, local_width, local_ff, groups, zn, xn, yn) = dims
    parts = local_width // 128
    shard = width // groups
    piece = width // (groups * CORES * yn)
    rows = block // (layers * parts)

    def same(shape):
        return pl.BlockSpec(shape, lambda l, b: (0,) * len(shape))

    flat = pl.BlockSpec((rows, width), lambda l, b: (l * parts + b, 0))
    grad_specs = [
        pl.BlockSpec((1, shard // parts, 3 * local_width), lambda l, b: (l, b, 0)),
        pl.BlockSpec((1, shard, 128), lambda l, b: (l, 0, 3 * parts + b)),
        pl.BlockSpec((1, shard // parts, local_ff), lambda l, b: (l, b, 1)),
        pl.BlockSpec((1, shard, local_ff // parts), lambda l, b: (l, 0, 2 * parts + b)),
    ]
    own_specs = [
        pl.BlockSpec((1, 3, shard // parts, local_width), lambda l, b: (l, 0, b, 0)),
        pl.BlockSpec((1, 128, shard), lambda l, b: (l, b, 0)),
        pl.BlockSpec((1, shard // parts, local_ff), lambda l, b: (l, b, 0)),
        pl.BlockSpec((1, local_ff // parts, shard), lambda l, b: (l, b, 0)),
        same((layers, 4, piece)),
    ]

    def shapes(dtype):
        return [jax.ShapeDtypeStruct(m.shape, dtype) for m in masters]

    flat_shape = jax.ShapeDtypeStruct((block, width), F32)
    return pl.pallas_call(
        functools.partial(adam_kernel, dims),
        grid=(layers, parts),
        out_shape=[flat_shape, flat_shape] + shapes(F32) * 4 + shapes(BF16),
        in_specs=[same((8, 128)), same((4 * layers, width)), flat, flat]
        + grad_specs
        + own_specs * 3,
        out_specs=[flat, flat] + own_specs * 5,
        compiler_params=pltpu.CompilerParams(vmem_limit_bytes=60 * 2**20),
        name="adam_update",
    )(total, norm_grad, hidden, input_grad, *([grad] * 4), *masters, *firsts, *seconds)


def body(
    block_input,
    output_grad,
    row_lengths,
    qkv_weight,
    proj_weight,
    up_weight,
    down_weight,
    norm_params,
    qkv_first,
    proj_first,
    up_first,
    down_first,
    norm_first,
    qkv_second,
    proj_second,
    up_second,
    down_second,
    norm_second,
):
    row_count, local_slots, width = block_input.shape
    seq_count = lax.axis_size("seq")
    groups = lax.axis_size("dp")
    layer_count = qkv_weight.shape[0]
    local_width = qkv_weight.shape[3]
    dims = (
        layer_count, local_slots * seq_count, width, local_slots, local_width,
        up_weight.shape[2], groups, ZSIZE, groups // ZSIZE, seq_count // CORES,
    )

    def turned(qkv):
        return jnp.transpose(qkv, (0, 2, 1, 3))

    masters = (turned(qkv_weight), proj_weight, up_weight, down_weight, norm_params)
    firsts = (turned(qkv_first), proj_first, up_first, down_first, norm_first)
    seconds = (turned(qkv_second), proj_second, up_second, down_second, norm_second)
    piece = norm_params.shape[2]
    norm_in = norm_params.astype(BF16).astype(F32).reshape(4 * layer_count, piece)
    norm_in = jnp.pad(norm_in, ((0, 0), (0, 128 - piece)))
    flat = (local_slots, width)
    kept = run_forward(dims, row_lengths, block_input.reshape(flat), norm_in, masters[:4])
    back = run_backward(dims, row_lengths, output_grad.reshape(flat), kept[1], kept[2:])
    outs = run_adam(dims, back[2], back[1], kept[0], back[0], back[3], masters, firsts, seconds)
    whole = (row_count,) + flat
    final = [outs[0].reshape(whole), outs[1].reshape(whole), back[2][0, 0]]
    for group in range(5):
        mine = outs[2 + 5 * group : 7 + 5 * group]
        final += [turned(mine[0])] + list(mine[1:])
    return tuple(final)


def solution(mesh):
    return jax.shard_map(
        body,
        mesh=mesh,
        in_specs=(
            P("dp", "seq", None),
            P("dp", "seq", None),
            P("dp"),
            P(None, "dp", None, "seq"),
            P(None, "seq", "dp"),
            P(None, "dp", "seq"),
            P(None, "seq", "dp"),
            P(None, None, ("dp", "seq")),
            P(None, "dp", None, "seq"),
            P(None, "seq", "dp"),
            P(None, "dp", "seq"),
            P(None, "seq", "dp"),
            P(None, None, ("dp", "seq")),
            P(None, "dp", None, "seq"),
            P(None, "seq", "dp"),
            P(None, "dp", "seq"),
            P(None, "seq", "dp"),
            P(None, None, ("dp", "seq")),
        ),
        out_specs=(
            P("dp", "seq", None),
            P("dp", "seq", None),
            P(),
            P(None, "dp", None, "seq"),
            P(None, "seq", "dp"),
            P(None, "dp", "seq"),
            P(None, "seq", "dp"),
            P(None, None, ("dp", "seq")),
            P(None, "dp", None, "seq"),
            P(None, "seq", "dp"),
            P(None, "dp", "seq"),
            P(None, "seq", "dp"),
            P(None, None, ("dp", "seq")),
            P(None, "dp", None, "seq"),
            P(None, "seq", "dp"),
            P(None, "dp", "seq"),
            P(None, "seq", "dp"),
            P(None, None, ("dp", "seq")),
            P(None, "dp", None, "seq"),
            P(None, "seq", "dp"),
            P(None, "dp", "seq"),
            P(None, "seq", "dp"),
            P(None, None, ("dp", "seq")),
            P(None, "dp", None, "seq"),
            P(None, "seq", "dp"),
            P(None, "dp", "seq"),
            P(None, "seq", "dp"),
            P(None, None, ("dp", "seq")),
        ),
        check_vma=False,
    )
```

```python
import functools

import jax
import jax.numpy as jnp
import numpy as np
from jax import lax
from jax.experimental import pallas as pl
from jax.experimental.pallas import tpu as pltpu
from jax.sharding import PartitionSpec as P

H = 8
HD = 128
STEP = 5
CORES = 2
ZSIZE = 4

EPS_NORM = 1e-05
BETA_ONE = 0.5
BETA_TWO = 0.75
LEARN_RATE = 0.03
NORM_RATE = 0.3
WEIGHT_DECAY = 0.1
CLIP_NORM = 0.1
ADAM_EPS = 1e-08

UNITS = 12
DEPTH = 2
DEEPER = (4, 6)
PUMPS = (
    ((0, 1, 2), (16, 17)),
    ((3,), (18,)),
    ((4,), (19,)),
    ((5, 6), (20, 21)),
    ((7,), (22,)),
    ((8,), (23,)),
    ((9, 10), ()),
    ((11,), ()),
    ((12, 13, 14, 15), ()),
)

F32 = jnp.float32
BF16 = jnp.bfloat16
MESH = pl.DeviceIdType.MESH
SCORE_SCALE = HD ** (-0.5)
GELU_A = (2.0 / np.pi) ** 0.5
GELU_B = 0.044715


def slope_table(head_count):
    return np.power(2.0, -8.0 * (np.arange(head_count) + 1.0) / head_count)


def ahead(u):
    return u + 1 + DEPTH + sum(u >= step for step in DEEPER)


def slope_at(head):
    value = jnp.float32(0.0)
    for index, slope in enumerate(slope_table(H)):
        value = jnp.where(head == index, jnp.float32(slope), value)
    return value


def weight_cols(c):
    return pl.ds(0, 3 * c), pl.ds(3 * c, c), pl.ds(4 * c, 4 * c), pl.ds(8 * c, 4 * c)


def mm_nn(a, b):
    return lax.dot_general(a, b, (((1,), (0,)), ((), ())), preferred_element_type=F32)


def mm_nt(a, b):
    return lax.dot_general(a, b, (((1,), (1,)), ((), ())), preferred_element_type=F32)


def mm_tn(a, b):
    return lax.dot_general(a, b, (((0,), (0,)), ((), ())), preferred_element_type=F32)


def normalise(v):
    centered = v - jnp.mean(v, axis=-1, keepdims=True)
    inverse = lax.rsqrt(jnp.mean(centered * centered, axis=-1, keepdims=True) + EPS_NORM)
    return centered * inverse, inverse


def rows_of(index, size):
    return pl.ds(pl.multiple_of(index * size, size), size)


class Place:
    def __init__(self, zn, xn, yn):
        self.zn, self.xn, self.yn = zn, xn, yn
        self.dp = lax.axis_index("dp")
        self.seq = lax.axis_index("seq")
        self.z, self.x = self.dp // xn, lax.rem(self.dp, xn)
        self.y, self.c = self.seq // CORES, lax.rem(self.seq, CORES)

    def zo(self, k):
        return lax.rem(self.z + k + self.zn, self.zn)

    def xo(self, k):
        return lax.rem(self.x + k + self.xn, self.xn)

    def yo(self, k):
        return lax.rem(self.y + k + self.yn, self.yn)

    def dev(self, dz=0, dx=0, dy=0, dc=0):
        core = (1 - self.c) if dc else self.c
        return (self.zo(dz) * self.xn + self.xo(dx), self.yo(dy) * CORES + core)

    def dp_at(self, dz, dx):
        return self.zo(dz) * self.xn + self.xo(dx)

    def seq_at(self, dy, dc):
        core = (1 - self.c) if dc else self.c
        return self.yo(dy) * CORES + core

    def seq_others(self):
        return [(y, c) for c in range(CORES) for y in range(self.yn) if y or c]

    def dp_others(self):
        return [(z, x) for x in range(self.xn) for z in range(self.zn) if z or x]

    def peers(self, wide=False):
        if wide:
            out = [self.dev(dy=y, dc=c) for y, c in self.seq_others()]
            return out + [self.dev(dz=z, dx=x) for z, x in self.dp_others()]
        out = [self.dev(dc=1)]
        out += [self.dev(dy=k) for k in range(1, self.yn)]
        out += [self.dev(dx=k) for k in range(1, self.xn)]
        out += [self.dev(dz=k) for k in range(1, self.zn)]
        return out

    def barrier(self, wide=False):
        sem = pltpu.get_barrier_semaphore()
        peers = self.peers(wide)
        for peer in peers:
            pl.semaphore_signal(sem, inc=1, device_id=peer, device_id_type=MESH)
        pl.semaphore_wait(sem, len(peers))


def near_first(count):
    order = []
    for k in range(1, count):
        order.append((min(k, count - k), k))
    return [k for unused, k in sorted(order)]


def remote(src, dst, send, recv, dev):
    return pltpu.make_async_remote_copy(
        src_ref=src, dst_ref=dst, send_sem=send, recv_sem=recv, device_id=dev, device_id_type=MESH
    )


def all_sum(place, value, slots, send, recv):
    stages = (
        (CORES, place.c, lambda k: place.dev(dc=1), lambda k: 1 - place.c),
        (place.yn, place.y, lambda k: place.dev(dy=k), lambda k: place.yo(-k)),
        (place.xn, place.x, lambda k: place.dev(dx=k), lambda k: place.xo(-k)),
        (place.zn, place.z, lambda k: place.dev(dz=k), lambda k: place.zo(-k)),
    )
    base = 0
    at = 0
    for size, mine, target, origin in stages:
        slots[base + mine] = value
        own = slots.at[base + mine]
        for k in range(1, size):
            remote(own, own, send.at[at + k - 1], recv.at[at + k - 1], target(k)).start()
        for k in range(1, size):
            came = slots.at[base + origin(k)]
            remote(came, came, send.at[at + k - 1], recv.at[at + k - 1], target(k)).wait_recv()
        for k in range(1, size):
            remote(own, own, send.at[at + k - 1], recv.at[at + k - 1], target(k)).wait_send()
        value = slots[base]
        for k in range(1, size):
            value = value + slots[base + k]
        base += size
        at += size - 1
    return value


def sum_slots(zn, xn, yn):
    return CORES + yn + xn + zn, 1 + (yn - 1) + (xn - 1) + (zn - 1)


def all_sum_wide(place, value, slots, send, recv):
    p = place
    stages = (
        (p.seq, [(p.dev(dy=y, dc=c), p.seq_at(-y, c)) for y, c in p.seq_others()]),
        (p.dp, [(p.dev(dz=z, dx=x), p.dp_at(-z, -x)) for z, x in p.dp_others()]),
    )
    base = 0
    at = 0
    for mine, others in stages:
        slots[base + mine] = value
        own = slots.at[base + mine]
        for k, (target, origin) in enumerate(others):
            remote(own, own, send.at[at + k], recv.at[at + k], target).start()
        for k, (target, origin) in enumerate(others):
            came = slots.at[base + origin]
            remote(came, came, send.at[at + k], recv.at[at + k], target).wait_recv()
        for k, (target, origin) in enumerate(others):
            remote(own, own, send.at[at + k], recv.at[at + k], target).wait_send()
        value = slots[base]
        for k in range(len(others)):
            value = value + slots[base + k + 1]
        base += len(others) + 1
        at += len(others)
    return value


class Gather:
    def __init__(self, place, buf, block, send, recv):
        self.p, self.buf, self.block, self.send, self.recv = place, buf, block, send, recv

    def at(self, dy, dc):
        return self.buf.at[rows_of(self.p.seq_at(dy, dc), self.block)]

    def start(self):
        p, own = self.p, self.at(0, 0)
        for k in range(1, p.yn):
            remote(own, own, self.send.at[k], self.recv.at[k], p.dev(dy=k)).start()
        remote(own, own, self.send.at[0], self.recv.at[0], p.dev(dc=1)).start()

    def wait_chip(self):
        came = self.at(0, 1)
        remote(came, came, self.send.at[0], self.recv.at[0], self.p.dev(dc=1)).wait_recv()

    def forward(self):
        p = self.p
        for k in range(1, p.yn):
            came = self.at(-k, 0)
            remote(came, came, self.send.at[k], self.recv.at[k], p.dev(dy=k)).wait_recv()
            f = p.yn - 1 + k
            remote(came, came, self.send.at[f], self.recv.at[f], p.dev(dc=1)).start()

    def wait_rest(self):
        p = self.p
        for k in range(1, p.yn):
            f = p.yn - 1 + k
            came = self.at(-k, 1)
            remote(came, came, self.send.at[f], self.recv.at[f], p.dev(dc=1)).wait_recv()
        own = self.at(0, 0)
        for k in range(1, p.yn):
            remote(own, own, self.send.at[k], self.recv.at[k], p.dev(dy=k)).wait_send()
            f = p.yn - 1 + k
            sent = self.at(-k, 0)
            remote(sent, sent, self.send.at[f], self.recv.at[f], p.dev(dc=1)).wait_send()
        remote(own, own, self.send.at[0], self.recv.at[0], p.dev(dc=1)).wait_send()


class Scatter:
    def __init__(self, place, sbuf, rbuf, ysend, yrecv, acc, send, recv):
        self.p = place
        self.sbuf, self.rbuf, self.ysend, self.yrecv, self.acc = sbuf, rbuf, ysend, yrecv, acc
        self.send, self.recv = send, recv

    def core(self, k):
        return remote(
            self.sbuf.at[k], self.rbuf.at[k], self.send.at[k], self.recv.at[k], self.p.dev(dc=1)
        )

    def cross(self, k):
        s = self.p.yn + k - 1
        return remote(
            self.ysend.at[k - 1],
            self.yrecv.at[k - 1],
            self.send.at[s],
            self.recv.at[s],
            self.p.dev(dy=k),
        )

    def start(self, part):
        p = self.p
        for k in list(range(1, p.yn)) + [0]:
            self.sbuf[k] = part(p.seq_at(k, 1)).astype(BF16)
            self.core(k).start()
            mine = part(p.seq_at(k, 0))
            self.core(k).wait_recv()
            mine = mine + self.rbuf[k].astype(F32)
            if k:
                self.ysend[k - 1] = mine.astype(BF16)
                self.cross(k).start()
            else:
                self.acc[...] = mine

    def wait(self):
        p = self.p
        for k in range(1, p.yn):
            self.cross(k).wait_recv()
        for k in range(1, p.yn):
            self.cross(k).wait_send()
        for k in range(p.yn):
            self.core(k).wait_send()

    def rows(self, at):
        value = self.acc[at, :]
        for k in range(1, self.p.yn):
            value = value + self.yrecv[k - 1, at, :].astype(F32)
        return value


def row_loop(total, step, fn):
    def one(i, unused):
        fn(rows_of(i, step))
        return unused

    lax.fori_loop(0, total // step, one, 0)


def twice(v):
    return jnp.concatenate([v, v], axis=1)


def key_bias(bias, slots, length, slope):
    def one(i, unused):
        key = i * 64 + lax.broadcasted_iota(jnp.int32, (64, 128), 0)
        bias[rows_of(i, 64), :] = jnp.where(key < length, slope * key.astype(F32), -jnp.inf)
        return unused

    lax.fori_loop(0, slots // 64, one, 0)


def turn_rows(target, rows, slots):
    for c in range(slots // 256):
        at = pl.ds(c * 256, 256)
        target[:, at] = rows(at).astype(F32).T.astype(BF16)


def forward_kernel(dims, *refs):
    (layers, slots, width, block, local_width, local_ff, groups, zn, xn, yn) = dims
    heads = local_width // HD
    refs = list(refs)

    def take(count):
        out = refs[:count]
        del refs[:count]
        return out

    lengths, x_in, g_in, norm_in = take(4)
    masters = take(4)
    out, norm_out = take(2)
    g_save, w_save = take(2)
    xn1_save, xn2_save, qkv_save, ctx_save, lse_save, act_save, dact_save, hid_save, mid_save = take(9)
    w = take(1)[0]
    xn1, xn2, qkv, ctx, lse, act, dact, hid, mid, upper, norm_place, bias, turned = take(13)
    sbuf, rbuf, ysend, yrecv, acc, nslots = take(6)
    zsend, zrecv, xsend, xrecv, wsave_sem = take(5)
    ag_send, ag_recv, rs_send, rs_recv, ns_send, ns_recv, save_sem = take(7)
    g_low, g_sem = take(2)

    p = Place(zn, xn, yn)
    z_order = near_first(zn)
    length = lengths[0]
    cols_qkv, cols_o, cols_up, cols_down = weight_cols(local_width)

    unit_count = UNITS * layers
    slopes = [slope_at(p.seq * heads + h) for h in range(heads)]

    def unit_cols(u):
        return pl.ds((u % UNITS) * local_width, local_width)

    def z_copy(u, dz, zi):
        here = w.at[u // UNITS, zi, p.x, :, unit_cols(u)]
        return remote(here, here, zsend.at[u, dz - 1], zrecv.at[u, dz - 1], p.dev(dz=dz))

    def x_copy(u, dx, dz):
        here = w.at[u // UNITS, p.zo(-dz), p.x, :, unit_cols(u)]
        return remote(here, here, xsend.at[u, dx - 1, dz], xrecv.at[u, dx - 1, dz], p.dev(dx=dx))

    def prepare(u):
        l, v = divmod(u, UNITS)
        cols = unit_cols(u)
        if v < 3:
            w[l, p.z, p.x, :, cols] = masters[0][l, v].astype(BF16)
        elif 4 <= v < 8:
            source = pl.ds((v - 4) * local_width, local_width)
            w[l, p.z, p.x, :, cols] = masters[2][l, :, source].astype(BF16)
        else:
            source, base = (masters[1], 0) if v == 3 else (masters[3], (v - 8) * local_width)
            for c in range(local_width // 128):
                block_t = source[l, pl.ds(base + c * 128, 128), :].T
                w[l, p.z, p.x, :, pl.ds(v * local_width + c * 128, 128)] = block_t.astype(BF16)

    def start_unit(u):
        for dz in z_order:
            z_copy(u, dz, p.z).start()
        for dx in range(1, xn):
            x_copy(u, dx, 0).start()

    def pump(u):
        for dz in z_order:
            z_copy(u, dz, p.zo(-dz)).wait_recv()
            for dx in range(1, xn):
                x_copy(u, dx, dz).start()
        for later in range(ahead(u - 1), min(ahead(u), unit_count)):
            start_unit(later)

    def pumps(l, *tables):
        for at, units in enumerate(tables):
            if units:

                @pl.when(l == at)
                def _(units=units):
                    for u in units:
                        pump(u)

    def save_weight(l):
        return pltpu.make_async_copy(w.at[l], w_save.at[l], wsave_sem.at[l])

    def need(l, low, high):
        def one(v, unused):
            u = UNITS * l + v
            at = w.at[0, 0, 0, :, pl.ds(0, local_width)]
            for dz in range(zn):
                for dx in range(1, xn):
                    remote(
                        at, at, xsend.at[u, dx - 1, dz], xrecv.at[u, dx - 1, dz], p.dev(dx=dx)
                    ).wait_recv()
            return unused

        lax.fori_loop(low, high, one, 0)

    def finish_weight(l):
        def one(v, unused):
            u = UNITS * l + v
            at = w.at[0, 0, 0, :, pl.ds(0, local_width)]
            for dz in z_order:
                remote(
                    at, at, zsend.at[u, dz - 1], zrecv.at[u, dz - 1], p.dev(dz=dz)
                ).wait_send()
            for dz in range(zn):
                for dx in range(1, xn):
                    remote(
                        at, at, xsend.at[u, dx - 1, dz], xrecv.at[u, dx - 1, dz], p.dev(dx=dx)
                    ).wait_send()
            return unused

        lax.fori_loop(0, UNITS, one, 0)
        save_weight(l).wait()

    def weight(l, cols):
        return w[l, :, :, :, cols].reshape(width, cols.size)

    def save(l, which, src, dst):
        return pltpu.make_async_copy(src, dst, save_sem.at[l, which])

    def saves(l):
        return (
            save(l, 0, xn1.at[l], xn1_save.at[l]),
            save(l, 1, xn2.at[l], xn2_save.at[l]),
            save(l, 2, qkv.at[l], qkv_save.at[l]),
            save(l, 3, ctx.at[l], ctx_save.at[l]),
            save(l, 4, lse.at[l], lse_save.at[l]),
            save(l, 5, act.at[l], act_save.at[l]),
            save(l, 6, dact.at[l], dact_save.at[l]),
            save(l, 7, hid.at[l], hid_save.at[l]),
            save(l, 8, mid.at[l], mid_save.at[l]),
        )

    p.barrier()
    for u in range(ahead(-1)):
        prepare(u)
        start_unit(u)
    first = p.seq * block
    g_zero = Gather(p, g_save, block, ag_send.at[2 * layers], ag_recv.at[2 * layers])

    def mask_in(i, unused):
        at = rows_of(i, 32)
        slot = first + i * 32 + lax.broadcasted_iota(jnp.int32, (32, 1), 0)
        g_low[at, :] = jnp.where(slot < length, g_in[at, :].astype(F32), 0.0).astype(BF16)
        return unused

    lax.fori_loop(0, block // 32, mask_in, 0)
    g_own = pltpu.make_async_copy(g_low, g_save.at[rows_of(p.seq, block)], g_sem.at[0])
    g_own.start()
    g_own.wait()
    piece = width // (groups * CORES * yn)
    at_lane = (p.dp * CORES * yn + p.seq) * piece
    norm_place[...] = jnp.zeros_like(norm_place)
    norm_place[:, rows_of(at_lane // 128, 128)] = pltpu.roll(norm_in[...], lax.rem(at_lane, 128), 1)
    norm_out[...] = all_sum(p, norm_place[...], nslots, ns_send, ns_recv)
    for u in range(ahead(-1), UNITS):
        prepare(u)

    def load_in(at):
        hid[0, at, :] = x_in[at, :].astype(F32)

    row_loop(block, 64, load_in)

    def norm_row(index):
        return norm_out[pl.ds(index, 1), :]

    def norm_into(l, source, target, row):
        gain, bias = norm_row(4 * l + row), norm_row(4 * l + row + 1)

        def one(i, unused):
            scaled, inverse = normalise(source[l, rows_of(i, 32), :])
            at = pl.ds(pl.multiple_of(first + i * 32, 32), 32)
            target[l, at, :] = (scaled * gain + bias).astype(BF16)
            return unused

        lax.fori_loop(0, block // 32, one, 0)

    def attention(l):
        step = 256
        causal = lax.broadcasted_iota(jnp.int32, (step, step), 0) <= lax.broadcasted_iota(
            jnp.int32, (step, step), 1
        )
        for h in range(heads):
            cols = pl.ds(h * HD, HD)
            k_cols = pl.ds(local_width + h * HD, HD)
            v_cols = pl.ds(2 * local_width + h * HD, HD)
            key_bias(bias, slots, length, slopes[h])
            turn_rows(turned, lambda at: qkv[l, at, v_cols], slots)
            for b in range(slots // step):
                here = pl.ds(b * step, step)
                before = pl.ds(0, b * step)
                q = qkv[l, here, cols]
                raw = mm_nt(qkv[l, here, k_cols], q) * SCORE_SCALE + twice(bias[here, :])
                raw = jnp.where(causal, raw, -jnp.inf)
                top = jnp.max(raw, axis=0, keepdims=True)
                if b:
                    past = mm_nt(qkv[l, before, k_cols], q) * SCORE_SCALE + twice(bias[before, :])
                    top = jnp.maximum(top, jnp.max(past, axis=0, keepdims=True))
                e_here = jnp.exp(raw - top)
                total = jnp.sum(e_here, axis=0, keepdims=True)
                value = mm_nn(turned[:, here], e_here.astype(BF16))
                if b:
                    e_past = jnp.exp(past - top)
                    total = total + jnp.sum(e_past, axis=0, keepdims=True)
                    value = value + mm_nn(turned[:, before], e_past.astype(BF16))
                ctx[l, here, cols] = (value / total).T.astype(BF16)
                lse[l, pl.ds(h, 1), here] = top + jnp.log(total)

    def layer(l, unused):
        last = layers - 1
        g_one = Gather(p, xn1.at[l], block, ag_send.at[2 * l], ag_recv.at[2 * l])
        g_two = Gather(p, xn2.at[l], block, ag_send.at[2 * l + 1], ag_recv.at[2 * l + 1])
        rs = [
            Scatter(
                p, sbuf, rbuf, ysend, yrecv, acc,
                rs_send.at[2 * l + i], rs_recv.at[2 * l + i],
            )
            for i in range(2)
        ]
        save_at = saves(l)
        save_at[7].start()
        norm_into(l, hid, xn1, 0)
        g_one.start()

        @pl.when(l == 0)
        def _():
            for u in range(UNITS, unit_count):
                prepare(u)

        pumps(l, *PUMPS[0])

        def project(index):
            at = rows_of(index, block)
            qkv[l, at, :] = mm_nn(xn1[l, at, :], weight(l, cols_qkv)).astype(BF16)

        g_one.wait_chip()
        g_one.forward()

        @pl.when(l == 0)
        def _():
            g_zero.start()

        need(l, 0, 3)
        project(p.seq_at(0, 0))
        project(p.seq_at(0, 1))
        pumps(l, *PUMPS[1])
        g_one.wait_rest()
        save_at[0].start()
        for k in range(1, yn):
            project(p.seq_at(-k, 0))
            project(p.seq_at(-k, 1))
        save_at[2].start()
        attention(l)
        save_at[3].start()
        save_at[4].start()
        pumps(l, *PUMPS[2])
        need(l, 3, 4)
        rs[0].start(lambda b: mm_nt(ctx[l, rows_of(b, block), :], weight(l, cols_o)))
        pumps(l, *PUMPS[3])

        @pl.when(l == 0)
        def _():
            g_zero.wait_chip()
            g_zero.forward()

        rs[0].wait()

        def add_middle(at):
            mid[l, at, :] = hid[l, at, :] + rs[0].rows(at)

        row_loop(block, 32, add_middle)
        save_at[8].start()
        norm_into(l, mid, xn2, 2)
        g_two.start()
        pumps(l, *PUMPS[4])
        need(l, 4, 8)

        def expand(index):
            base = pl.multiple_of(index * block, block)
            upper[...] = mm_nn(xn2[l, pl.ds(base, block), :], weight(l, cols_up))

            def one(i, unused):
                u = upper[rows_of(i, 16), :]
                at = pl.ds(pl.multiple_of(base + i * 16, 16), 16)
                square = u * u
                t = jnp.tanh(GELU_A * u * (1.0 + GELU_B * square))
                half = 0.5 * (1.0 + t)
                act[l, at, :] = (u * half).astype(BF16)
                slope = (0.5 * GELU_A) * u * (1.0 - t * t) * (1.0 + (3.0 * GELU_B) * square)
                dact[l, at, :] = (half + slope).astype(BF16)
                return unused

            lax.fori_loop(0, block // 16, one, 0)

        expand(p.seq_at(0, 0))
        g_two.wait_chip()
        expand(p.seq_at(0, 1))
        pumps(l, *PUMPS[5])
        g_two.forward()
        pumps(l, *PUMPS[6])
        g_two.wait_rest()
        save_at[1].start()
        for k in range(1, yn):
            expand(p.seq_at(-k, 0))
            expand(p.seq_at(-k, 1))
        save_at[5].start()
        save_at[6].start()
        pumps(l, *PUMPS[7])
        need(l, 8, 12)
        save_weight(l).start()
        rs[1].start(lambda b: mm_nt(act[l, rows_of(b, block), :], weight(l, cols_down)))
        pumps(l, *PUMPS[8])
        rs[1].wait()

        @pl.when(l < last)
        def _():
            def add_next(at):
                hid[l + 1, at, :] = mid[l, at, :] + rs[1].rows(at)

            row_loop(block, 32, add_next)

        @pl.when(l == last)
        def _():
            def add_out(at):
                out[at, :] = mid[l, at, :] + rs[1].rows(at)

            row_loop(block, 32, add_out)

        return unused

    lax.fori_loop(0, layers, layer, 0)

    def finish(l, unused):
        finish_weight(l)
        for item in saves(l):
            item.wait()
        return unused

    g_zero.wait_rest()
    lax.fori_loop(0, layers, finish, 0)


def run_forward(dims, lengths, x_in, g_in, norm_in, masters):
    (layers, slots, width, block, local_width, local_ff, groups, zn, xn, yn) = dims
    shard = width // groups
    slot_count, sem_count = sum_slots(zn, xn, yn)

    def saved(*shape, dtype=BF16):
        return jax.ShapeDtypeStruct((layers,) + shape, dtype)

    vmem = pl.BlockSpec(memory_space=pltpu.VMEM)
    smem = pl.BlockSpec(memory_space=pltpu.SMEM)
    hbm = pl.BlockSpec(memory_space=pl.ANY)
    kept = [
        saved(zn, xn, shard, UNITS * local_width),
        saved(slots, width),
        saved(slots, width),
        saved(slots, 3 * local_width),
        saved(slots, local_width),
        saved(8, slots, dtype=F32),
        saved(slots, local_ff),
        saved(slots, local_ff),
        saved(block, width, dtype=F32),
        saved(block, width, dtype=F32),
    ]
    dma = pltpu.SemaphoreType.DMA
    return pl.pallas_call(
        functools.partial(forward_kernel, dims),
        out_shape=[
            jax.ShapeDtypeStruct((block, width), F32),
            jax.ShapeDtypeStruct((4 * layers, width), F32),
        ]
        + [jax.ShapeDtypeStruct((slots, width), BF16)]
        + kept,
        in_specs=[smem] + [vmem] * 7,
        out_specs=[vmem, vmem] + [hbm] * (1 + len(kept)),
        scratch_shapes=[pltpu.VMEM(k.shape, k.dtype) for k in kept]
        + [
            pltpu.VMEM((block, local_ff), F32),
            pltpu.VMEM((4 * layers, width), F32),
            pltpu.VMEM((slots, 128), F32),
            pltpu.VMEM((HD, slots), BF16),
            pltpu.VMEM((yn, block, width), BF16),
            pltpu.VMEM((yn, block, width), BF16),
            pltpu.VMEM((yn - 1, block, width), BF16),
            pltpu.VMEM((yn - 1, block, width), BF16),
            pltpu.VMEM((block, width), F32),
            pltpu.VMEM((slot_count, 4 * layers, width), F32),
            dma((UNITS * layers, zn - 1)),
            dma((UNITS * layers, zn - 1)),
            dma((UNITS * layers, xn - 1, zn)),
            dma((UNITS * layers, xn - 1, zn)),
            dma((layers,)),
            dma((2 * layers + 1, 2 * yn - 1)),
            dma((2 * layers + 1, 2 * yn - 1)),
            dma((2 * layers, 2 * yn - 1)),
            dma((2 * layers, 2 * yn - 1)),
            dma((sem_count,)),
            dma((sem_count,)),
            dma((layers, 9)),
            pltpu.VMEM((block, width), BF16),
            dma((1,)),
        ],
        compiler_params=pltpu.CompilerParams(
            collective_id=0, has_side_effects=True, vmem_limit_bytes=62 * 2**20
        ),
        name="forward_layers",
    )(lengths, x_in, g_in, norm_in, *masters)

def backward_kernel(dims, *refs):
    (layers, slots, width, block, local_width, local_ff, groups, zn, xn, yn) = dims
    heads = local_width // HD
    shard = width // groups
    slab = shard * xn
    refs = list(refs)

    def take(count):
        out = refs[:count]
        del refs[:count]
        return out

    lengths, g_in, norms, g_all = take(4)
    kept = take(10)
    g_out, norm_grad, total_out = take(3)
    shards = take(1)[0]
    held = take(10)
    w, xn1, xn2, qkv, ctx, lse, act, dact, hid, mid = held
    gfull, gbfull, gctx, dqkv, dk, dv, bias, turned, g, gm, npart = take(11)
    dw, xland, zland = take(3)
    sbuf, rbuf, ysend, yrecv, acc, nslots, tslots = take(7)
    zsend, zrecv, xsend, xrecv = take(4)
    ag_send, ag_recv, rs_send, rs_recv, ns_send, ns_recv, ts_send, ts_recv, load_sem = take(9)

    p = Place(zn, xn, yn)
    length = lengths[0]
    first = p.seq * block
    gu = dact
    w_all = kept[0]

    slopes = [slope_at(p.seq * heads + h) for h in range(heads)]
    weight_at = weight_cols(local_width)
    cols_qkv, cols_o, cols_up, cols_down = weight_at

    def load(l, which):
        if which < 4:
            cols = weight_at[which]
            return pltpu.make_async_copy(w_all.at[l, :, :, :, cols], w.at[:, :, :, cols], load_sem.at[which])
        return pltpu.make_async_copy(kept[which - 3].at[l], held[which - 3], load_sem.at[which])

    def weight(cols):
        return w[:, :, :, cols].reshape(width, cols.size)

    def unit_cols(v):
        return pl.ds(v * local_width, local_width)

    def x_copy(l, v, dx):
        cols = unit_cols(v)
        return remote(
            dw.at[:, p.xo(dx), :, cols],
            xland.at[l, dx - 1, :, :, cols],
            xsend.at[l, v, dx - 1],
            xrecv.at[l, v, dx - 1],
            p.dev(dx=dx),
        )

    def z_copy(l, v, zi):
        cols = unit_cols(v)
        return remote(
            dw.at[p.zo(zi), p.x, :, cols],
            zland.at[l, zi - 1, :, cols],
            zsend.at[l, v, zi - 1],
            zrecv.at[l, v, zi - 1],
            p.dev(dz=zi),
        )

    z_order = near_first(zn)
    zi_order = z_order[::-1] + [0]

    def weight_grad(left, right, low, count):
        def one(i, unused):
            part = mm_tn(left[:, rows_of(i, slab)], right[...]).astype(BF16)
            dw[i, :, :, pl.ds(low * local_width, count * local_width)] = part.reshape(
                xn, shard, count * local_width
            )
            return unused

        lax.fori_loop(0, zn, one, 0)

    def send_x(l, *units):
        for v in units:
            for dx in range(1, xn):
                x_copy(l, v, dx).start()

    def reduce_x(l, *units):
        for v in units:
            cols = unit_cols(v)
            for dx in range(1, xn):
                x_copy(l, v, dx).wait_recv()
            for zi in zi_order:
                zz = p.zo(zi)

                def one(i, unused, zi=zi, cols=cols, zz=zz):
                    here = rows_of(i, 32)
                    value = dw[zz, p.x, here, cols].astype(F32)
                    for dx in range(1, xn):
                        value = value + xland[l, dx - 1, zz, here, cols].astype(F32)
                    if zi:
                        dw[zz, p.x, here, cols] = value.astype(BF16)
                    else:
                        shards[l, here, cols] = value
                    return unused

                lax.fori_loop(0, shard // 32, one, 0)
                if zi:
                    z_copy(l, v, zi).start()

    def reduce_z(l, low, high):
        def unit(v, unused):
            cols = pl.ds(pl.multiple_of(v * local_width, local_width), local_width)
            here = dw.at[0, 0, :, pl.ds(0, local_width)]
            for zi in z_order:
                remote(
                    here, here, zsend.at[l, v, zi - 1], zrecv.at[l, v, zi - 1], p.dev(dz=zi)
                ).wait_recv()

            def one(at):
                value = shards[l, at, cols]
                for zi in range(1, zn):
                    value = value + zland[l, zi - 1, at, cols].astype(F32)
                shards[l, at, cols] = value

            row_loop(shard, 32, one)
            for zi in z_order:
                remote(
                    here, here, zsend.at[l, v, zi - 1], zrecv.at[l, v, zi - 1], p.dev(dz=zi)
                ).wait_send()
            every = dw.at[:, 0, :, pl.ds(0, local_width)]
            for dx in range(1, xn):
                remote(
                    every, every, xsend.at[l, v, dx - 1], xrecv.at[l, v, dx - 1], p.dev(dx=dx)
                ).wait_send()
            return unused

        lax.fori_loop(low, high, unit, 0)

    def norm_back(l, source, rs, base, row, target, low):
        gain = norms[pl.ds(4 * l + row, 1), :]
        zero = jnp.zeros((8, width), F32)

        def one(i, carry):
            at = rows_of(i, 32)
            scaled, inverse = normalise(source[at, :])
            e = rs.rows(at)
            eg = e * gain
            part = inverse * (
                eg
                - jnp.mean(eg, axis=-1, keepdims=True)
                - scaled * jnp.mean(eg * scaled, axis=-1, keepdims=True)
            )
            value = base[at, :] + part
            target[at, :] = value
            if low is not None:
                low[pl.ds(pl.multiple_of(first + i * 32, 32), 32), :] = value.astype(BF16)
            es = e * scaled
            gains, biases = carry
            for r in range(4):
                gains = gains + es[r * 8 : r * 8 + 8]
                biases = biases + e[r * 8 : r * 8 + 8]
            return gains, biases

        gains, biases = lax.fori_loop(0, block // 32, one, (zero, zero))
        npart[pl.ds(4 * l + row, 1), :] = jnp.sum(gains, axis=0, keepdims=True)
        npart[pl.ds(4 * l + row + 1, 1), :] = jnp.sum(biases, axis=0, keepdims=True)

    def attention(between):
        step = 256
        causal = lax.broadcasted_iota(jnp.int32, (step, step), 0) <= lax.broadcasted_iota(
            jnp.int32, (step, step), 1
        )
        for h in range(heads):
            cols = pl.ds(h * HD, HD)
            k_cols = pl.ds(local_width + h * HD, HD)
            v_cols = pl.ds(2 * local_width + h * HD, HD)
            key_bias(bias, slots, length, slopes[h])
            turn_rows(turned, lambda at: qkv[at, k_cols], slots)
            for b in range(slots // step):
                here = pl.ds(b * step, step)
                before = pl.ds(0, b * step)
                q = qkv[here, cols]
                gc = gctx[here, cols]
                shift = lse[pl.ds(h, 1), here]
                raw = mm_nt(qkv[here, k_cols], q) * SCORE_SCALE + twice(bias[here, :])
                p_here = jnp.exp(jnp.where(causal, raw, -jnp.inf) - shift)
                dp_here = mm_nt(qkv[here, v_cols], gc)
                delta = jnp.sum(p_here * dp_here, axis=0, keepdims=True)
                dv[here, :] = mm_nn(p_here.astype(BF16), gc)
                if b:
                    past = mm_nt(qkv[before, k_cols], q) * SCORE_SCALE + twice(bias[before, :])
                    p_past = jnp.exp(past - shift)
                    dp_past = mm_nt(qkv[before, v_cols], gc)
                    delta = delta + jnp.sum(p_past * dp_past, axis=0, keepdims=True)
                    dv[before, :] += mm_nn(p_past.astype(BF16), gc)
                ds_here = (p_here * (dp_here - delta)).astype(BF16)
                dq = mm_nn(turned[:, here], ds_here)
                dk[here, :] = mm_nn(ds_here, q)
                if b:
                    ds_past = (p_past * (dp_past - delta)).astype(BF16)
                    dq = dq + mm_nn(turned[:, before], ds_past)
                    dk[before, :] += mm_nn(ds_past, q)
                dqkv[here, cols] = (dq * SCORE_SCALE).T.astype(BF16)
                between(h * (slots // step) + b + 1, heads * (slots // step))

            def store(at):
                dqkv[at, k_cols] = (dk[at, :] * SCORE_SCALE).astype(BF16)
                dqkv[at, v_cols] = dv[at, :].astype(BF16)

            row_loop(slots, 64, store)

    p.barrier(wide=True)

    def mask_in(i, unused):
        at = rows_of(i, 32)
        slot = first + i * 32 + lax.broadcasted_iota(jnp.int32, (32, 1), 0)
        g[at, :] = jnp.where(slot < length, g_in[at, :].astype(F32), 0.0)
        return unused

    lax.fori_loop(0, block // 32, mask_in, 0)
    load_order = (3, 10, 2, 9, 5, 12, 1, 7, 6, 8, 0, 4, 11)

    def layer(step, unused):
        l = layers - 1 - step
        later = l + 1
        g_one = Gather(p, gfull, block, ag_send.at[2 * l], ag_recv.at[2 * l])
        g_two = Gather(p, gbfull, block, ag_send.at[2 * l + 1], ag_recv.at[2 * l + 1])
        rs = [
            Scatter(
                p, sbuf, rbuf, ysend, yrecv, acc, rs_send.at[2 * l + i], rs_recv.at[2 * l + i]
            )
            for i in range(2)
        ]

        def low_in(i, unused):
            at = pl.ds(pl.multiple_of(first + i * 32, 32), 32)
            gfull[at, :] = g[rows_of(i, 32), :].astype(BF16)
            return unused

        all_in = pltpu.make_async_copy(g_all, gfull, load_sem.at[13])

        @pl.when(step == 0)
        def _():
            all_in.start()

        @pl.when(step > 0)
        def _():
            lax.fori_loop(0, block // 32, low_in, 0)
            g_one.start()

        for which in load_order:
            load(l, which).start()
        load(l, 3).wait()
        load(l, 10).wait()

        @pl.when(step == 0)
        def _():
            all_in.wait()


        def upper_grad(index):
            at = rows_of(index, block)
            value = mm_nn(gfull[at, :], weight(cols_down))
            gu[at, :] = (value * dact[at, :].astype(F32)).astype(BF16)

        upper_grad(p.seq_at(0, 0))

        @pl.when(step > 0)
        def _():
            g_one.wait_chip()

        upper_grad(p.seq_at(0, 1))

        @pl.when(step > 0)
        def _():
            g_one.forward()

        @pl.when(step > 0)
        def _():
            reduce_x(later, 0)
            send_x(later, 2)
            g_one.wait_rest()

        for k in range(1, yn):
            upper_grad(p.seq_at(-k, 0))
            upper_grad(p.seq_at(-k, 1))
        load(l, 2).wait()
        rs[0].start(lambda b: mm_nt(gu[rows_of(b, block), :], weight(cols_up)))
        load(l, 9).wait()
        load(l, 5).wait()

        @pl.when(step > 0)
        def _():
            reduce_z(later, 3, 12)

        weight_grad(gfull, act, 8, 4)
        send_x(l, 8)
        weight_grad(xn2, gu, 4, 4)
        send_x(l, 9)

        @pl.when(step > 0)
        def _():
            reduce_x(later, 1, 2)

        load(l, 12).wait()
        reduce_x(l, 8)
        send_x(l, 10)
        rs[0].wait()
        norm_back(l, mid, rs[0], g, 2, gm, gbfull)
        g_two.start()
        reduce_x(l, 9)
        send_x(l, 11)
        load(l, 1).wait()

        def context_grad(index):
            at = rows_of(index, block)
            gctx[at, :] = mm_nn(gbfull[at, :], weight(cols_o)).astype(BF16)

        context_grad(p.seq_at(0, 0))
        g_two.wait_chip()
        context_grad(p.seq_at(0, 1))
        reduce_x(l, 10)
        send_x(l, 4)
        g_two.forward()

        @pl.when(step > 0)
        def _():
            reduce_z(later, 0, 3)

        g_two.wait_rest()
        for k in range(1, yn):
            context_grad(p.seq_at(-k, 0))
            context_grad(p.seq_at(-k, 1))
        load(l, 7).wait()
        weight_grad(gbfull, ctx, 3, 1)
        reduce_x(l, 11)
        send_x(l, 5)
        load(l, 6).wait()
        load(l, 8).wait()

        def between(done, count):
            if done == (count * 3) // 8:
                reduce_x(l, 4)
                send_x(l, 6)
            if done == (count * 6) // 8:
                reduce_x(l, 5)
                send_x(l, 7)

        attention(between)
        load(l, 0).wait()
        load(l, 4).wait()

        @pl.when(l == 0)
        def _():
            weight_grad(xn1, dqkv, 0, 3)

        reduce_x(l, 6)
        send_x(l, 3)
        rs[1].start(lambda b: mm_nt(dqkv[rows_of(b, block), :], weight(cols_qkv)))

        @pl.when(l > 0)
        def _():
            weight_grad(xn1, dqkv, 0, 3)

        reduce_x(l, 7)
        send_x(l, 0)
        reduce_x(l, 3)
        send_x(l, 1)
        load(l, 11).wait()
        rs[1].wait()
        norm_back(l, hid, rs[1], gm, 0, g, None)
        return unused

    lax.fori_loop(0, layers, layer, 0)
    reduce_x(0, 0)
    send_x(0, 2)
    reduce_x(0, 1, 2)
    g_out[...] = g[...]
    norm_grad[...] = all_sum(p, npart[...], nslots, ns_send, ns_recv)
    reduce_z(0, 3, 12)
    reduce_z(0, 0, 3)

    def squares(i, total):
        l, at = i // (shard // 8), rows_of(lax.rem(i, shard // 8), 8)
        value = shards[l, at, :]
        value = value * value
        for c in range(UNITS * local_width // 128):
            total = total + value[:, c * 128 : (c + 1) * 128]
        return total

    tile = lax.fori_loop(0, layers * shard // 8, squares, jnp.zeros((8, 128), F32))
    tile = all_sum_wide(p, tile, tslots, ts_send, ts_recv)
    value = norm_grad[...]
    value = value * value
    for c in range(width // 128):
        piece = value[:, c * 128 : (c + 1) * 128]
        for r in range(4 * layers // 8):
            tile = tile + piece[r * 8 : r * 8 + 8]
    total = jnp.sum(jnp.sum(tile, axis=0, keepdims=True), axis=1, keepdims=True)
    total_out[...] = jnp.broadcast_to(jnp.sqrt(total), (8, 128))


def run_backward(dims, lengths, g_in, norms, g_all, kept):
    (layers, slots, width, block, local_width, local_ff, groups, zn, xn, yn) = dims
    packed = UNITS * local_width
    shard = width // groups
    slot_count, sem_count = sum_slots(zn, xn, yn)
    vmem = pl.BlockSpec(memory_space=pltpu.VMEM)
    smem = pl.BlockSpec(memory_space=pltpu.SMEM)
    hbm = pl.BlockSpec(memory_space=pl.ANY)
    dma = pltpu.SemaphoreType.DMA
    return pl.pallas_call(
        functools.partial(backward_kernel, dims),
        out_shape=[
            jax.ShapeDtypeStruct((block, width), F32),
            jax.ShapeDtypeStruct((4 * layers, width), F32),
            jax.ShapeDtypeStruct((8, 128), F32),
            jax.ShapeDtypeStruct((layers, shard, packed), F32),
        ],
        in_specs=[smem, vmem, vmem] + [hbm] * (1 + len(kept)),
        out_specs=[vmem] * 4,
        scratch_shapes=[pltpu.VMEM(k.shape[1:], k.dtype) for k in kept]
        + [
            pltpu.VMEM((slots, width), BF16),
            pltpu.VMEM((slots, width), BF16),
            pltpu.VMEM((slots, local_width), BF16),
            pltpu.VMEM((slots, 3 * local_width), BF16),
            pltpu.VMEM((slots, HD), F32),
            pltpu.VMEM((slots, HD), F32),
            pltpu.VMEM((slots, 128), F32),
            pltpu.VMEM((HD, slots), BF16),
            pltpu.VMEM((block, width), F32),
            pltpu.VMEM((block, width), F32),
            pltpu.VMEM((4 * layers, width), F32),
            pltpu.VMEM((zn, xn, shard, packed), BF16),
            pltpu.VMEM((layers, xn - 1, zn, shard, packed), BF16),
            pltpu.VMEM((layers, zn - 1, shard, packed), BF16),
            pltpu.VMEM((yn, block, width), BF16),
            pltpu.VMEM((yn, block, width), BF16),
            pltpu.VMEM((yn - 1, block, width), BF16),
            pltpu.VMEM((yn - 1, block, width), BF16),
            pltpu.VMEM((block, width), F32),
            pltpu.VMEM((slot_count, 4 * layers, width), F32),
            pltpu.VMEM((CORES * yn + groups, 8, 128), F32),
            dma((layers, UNITS, zn - 1)),
            dma((layers, UNITS, zn - 1)),
            dma((layers, UNITS, xn - 1)),
            dma((layers, UNITS, xn - 1)),
            dma((2 * layers, 2 * yn - 1)),
            dma((2 * layers, 2 * yn - 1)),
            dma((2 * layers, 2 * yn - 1)),
            dma((2 * layers, 2 * yn - 1)),
            dma((sem_count,)),
            dma((sem_count,)),
            dma((CORES * yn + groups - 2,)),
            dma((CORES * yn + groups - 2,)),
            dma((len(kept) + 4,)),
        ],
        compiler_params=pltpu.CompilerParams(
            collective_id=1, has_side_effects=True, vmem_limit_bytes=62 * 2**20
        ),
        name="backward_layers",
    )(lengths, g_in, norms, g_all, *kept)


def adam_kernel(dims, *refs):
    (layers, slots, width, block, local_width, local_ff, groups, zn, xn, yn) = dims
    refs = list(refs)

    def take(count):
        out = refs[:count]
        del refs[:count]
        return out

    total, norm_grad, hidden_in, input_in = take(4)
    grads, masters, firsts, seconds = take(4), take(5), take(5), take(5)
    hidden_out, input_out = take(2)
    grad_out, moment_out, variance_out, new_out, copy_out = (take(5) for unused in range(5))
    factor = CLIP_NORM / jnp.maximum(total[0:1, 0:1], CLIP_NORM)
    fix_one = 1.0 / (1.0 - BETA_ONE**STEP)
    fix_two = 1.0 / (1.0 - BETA_TWO**STEP)

    def update(k, at, grad, decay, rate):
        clipped = grad * factor
        momentum = BETA_ONE * firsts[k][at] + (1.0 - BETA_ONE) * clipped
        variance = BETA_TWO * seconds[k][at] + (1.0 - BETA_TWO) * clipped * clipped
        master = masters[k][at]
        size = momentum * fix_one / (jnp.sqrt(variance * fix_two) + ADAM_EPS)
        if decay:
            size = size + decay * master
        fresh = master - rate * size
        grad_out[k][at] = grad
        moment_out[k][at] = momentum
        variance_out[k][at] = variance
        new_out[k][at] = fresh
        copy_out[k][at] = fresh.astype(BF16)

    def matrix(k, at, grad):
        update(k, at, grad, WEIGHT_DECAY, LEARN_RATE)

    hidden_out[...] = hidden_in[...]
    input_out[...] = input_in[...]
    every = slice(None)
    for part in range(3):
        grad = grads[0][0, :, part * local_width : (part + 1) * local_width]
        matrix(0, (0, part, every, every), grad)
    matrix(1, (0, every, every), grads[1][0].T)

    def up_rows(i, unused):
        at = rows_of(i, 16)
        matrix(2, (0, at, every), grads[2][0, at, :])
        return unused

    lax.fori_loop(0, grads[2].shape[1] // 16, up_rows, 0)
    for c in range(grads[3].shape[2] // 128):
        at = pl.ds(c * 128, 128)
        matrix(3, (0, at, every), grads[3][0, :, at].T)

    @pl.when((pl.program_id(0) == 0) & (pl.program_id(1) == 0))
    def _():
        seq_count = CORES * yn
        piece = width // (groups * seq_count)
        at = (lax.axis_index("dp") * seq_count + lax.axis_index("seq")) * piece
        tile = norm_grad[:, rows_of(at // 128, 128)]
        tile = pltpu.roll(tile, lax.rem(128 - lax.rem(at, 128), 128), 1)[:, :piece]
        for l in range(layers):
            update(4, (l,), tile[4 * l : 4 * l + 4], 0.0, NORM_RATE)


def run_adam(dims, total, norm_grad, hidden, input_grad, grad, masters, firsts, seconds):
    (layers, slots, width, block, local_width, local_ff, groups, zn, xn, yn) = dims
    parts = local_width // 128
    shard = width // groups
    piece = width // (groups * CORES * yn)
    rows = block // (layers * parts)

    def same(shape):
        return pl.BlockSpec(shape, lambda l, b: (0,) * len(shape))

    flat = pl.BlockSpec((rows, width), lambda l, b: (l * parts + b, 0))
    grad_specs = [
        pl.BlockSpec((1, shard // parts, 3 * local_width), lambda l, b: (l, b, 0)),
        pl.BlockSpec((1, shard, 128), lambda l, b: (l, 0, 3 * parts + b)),
        pl.BlockSpec((1, shard // parts, local_ff), lambda l, b: (l, b, 1)),
        pl.BlockSpec((1, shard, local_ff // parts), lambda l, b: (l, 0, 2 * parts + b)),
    ]
    own_specs = [
        pl.BlockSpec((1, 3, shard // parts, local_width), lambda l, b: (l, 0, b, 0)),
        pl.BlockSpec((1, 128, shard), lambda l, b: (l, b, 0)),
        pl.BlockSpec((1, shard // parts, local_ff), lambda l, b: (l, b, 0)),
        pl.BlockSpec((1, local_ff // parts, shard), lambda l, b: (l, b, 0)),
        same((layers, 4, piece)),
    ]

    def shapes(dtype):
        return [jax.ShapeDtypeStruct(m.shape, dtype) for m in masters]

    flat_shape = jax.ShapeDtypeStruct((block, width), F32)
    return pl.pallas_call(
        functools.partial(adam_kernel, dims),
        grid=(layers, parts),
        out_shape=[flat_shape, flat_shape] + shapes(F32) * 4 + shapes(BF16),
        in_specs=[same((8, 128)), same((4 * layers, width)), flat, flat]
        + grad_specs
        + own_specs * 3,
        out_specs=[flat, flat] + own_specs * 5,
        compiler_params=pltpu.CompilerParams(vmem_limit_bytes=60 * 2**20),
        name="adam_update",
    )(total, norm_grad, hidden, input_grad, *([grad] * 4), *masters, *firsts, *seconds)


def body(
    block_input,
    output_grad,
    row_lengths,
    qkv_weight,
    proj_weight,
    up_weight,
    down_weight,
    norm_params,
    qkv_first,
    proj_first,
    up_first,
    down_first,
    norm_first,
    qkv_second,
    proj_second,
    up_second,
    down_second,
    norm_second,
):
    row_count, local_slots, width = block_input.shape
    seq_count = lax.axis_size("seq")
    groups = lax.axis_size("dp")
    layer_count = qkv_weight.shape[0]
    local_width = qkv_weight.shape[3]
    dims = (
        layer_count, local_slots * seq_count, width, local_slots, local_width,
        up_weight.shape[2], groups, ZSIZE, groups // ZSIZE, seq_count // CORES,
    )

    def turned(qkv):
        return jnp.transpose(qkv, (0, 2, 1, 3))

    masters = (turned(qkv_weight), proj_weight, up_weight, down_weight, norm_params)
    firsts = (turned(qkv_first), proj_first, up_first, down_first, norm_first)
    seconds = (turned(qkv_second), proj_second, up_second, down_second, norm_second)
    piece = norm_params.shape[2]
    norm_in = norm_params.astype(BF16).astype(F32).reshape(4 * layer_count, piece)
    norm_in = jnp.pad(norm_in, ((0, 0), (0, 128 - piece)))
    flat = (local_slots, width)
    g_in = output_grad.reshape(flat)
    kept = run_forward(dims, row_lengths, block_input.reshape(flat), g_in, norm_in, masters[:4])
    back = run_backward(dims, row_lengths, g_in, kept[1], kept[2], kept[3:])
    outs = run_adam(dims, back[2], back[1], kept[0], back[0], back[3], masters, firsts, seconds)
    whole = (row_count,) + flat
    final = [outs[0].reshape(whole), outs[1].reshape(whole), back[2][0, 0]]
    for group in range(5):
        mine = outs[2 + 5 * group : 7 + 5 * group]
        final += [turned(mine[0])] + list(mine[1:])
    return tuple(final)


def solution(mesh):
    return jax.shard_map(
        body,
        mesh=mesh,
        in_specs=(
            P("dp", "seq", None),
            P("dp", "seq", None),
            P("dp"),
            P(None, "dp", None, "seq"),
            P(None, "seq", "dp"),
            P(None, "dp", "seq"),
            P(None, "seq", "dp"),
            P(None, None, ("dp", "seq")),
            P(None, "dp", None, "seq"),
            P(None, "seq", "dp"),
            P(None, "dp", "seq"),
            P(None, "seq", "dp"),
            P(None, None, ("dp", "seq")),
            P(None, "dp", None, "seq"),
            P(None, "seq", "dp"),
            P(None, "dp", "seq"),
            P(None, "seq", "dp"),
            P(None, None, ("dp", "seq")),
        ),
        out_specs=(
            P("dp", "seq", None),
            P("dp", "seq", None),
            P(),
            P(None, "dp", None, "seq"),
            P(None, "seq", "dp"),
            P(None, "dp", "seq"),
            P(None, "seq", "dp"),
            P(None, None, ("dp", "seq")),
            P(None, "dp", None, "seq"),
            P(None, "seq", "dp"),
            P(None, "dp", "seq"),
            P(None, "seq", "dp"),
            P(None, None, ("dp", "seq")),
            P(None, "dp", None, "seq"),
            P(None, "seq", "dp"),
            P(None, "dp", "seq"),
            P(None, "seq", "dp"),
            P(None, None, ("dp", "seq")),
            P(None, "dp", None, "seq"),
            P(None, "seq", "dp"),
            P(None, "dp", "seq"),
            P(None, "seq", "dp"),
            P(None, None, ("dp", "seq")),
            P(None, "dp", None, "seq"),
            P(None, "seq", "dp"),
            P(None, "dp", "seq"),
            P(None, "seq", "dp"),
            P(None, None, ("dp", "seq")),
        ),
        check_vma=False,
    )
```

```python
import functools

import jax
import jax.numpy as jnp
import numpy as np
from jax import lax
from jax.experimental import pallas as pl
from jax.experimental.pallas import tpu as pltpu
from jax.sharding import PartitionSpec as P

H = 8
HD = 128
STEP = 5
CORES = 2
ZSIZE = 4

EPS_NORM = 1e-05
BETA_ONE = 0.5
BETA_TWO = 0.75
LEARN_RATE = 0.03
NORM_RATE = 0.3
WEIGHT_DECAY = 0.1
CLIP_NORM = 0.1
ADAM_EPS = 1e-08

UNITS = 12
DEPTH = 2
DEEPER = (4, 6)
PUMPS = (
    ((0, 1, 2), (16, 17)),
    ((3,), (18,)),
    ((4,), (19,)),
    ((5, 6), (20, 21)),
    ((7,), (22,)),
    ((8,), (23,)),
    ((9, 10), ()),
    ((11,), ()),
    ((12, 13, 14, 15), ()),
)

F32 = jnp.float32
BF16 = jnp.bfloat16
MESH = pl.DeviceIdType.MESH
SCORE_SCALE = HD ** (-0.5)
GELU_A = (2.0 / np.pi) ** 0.5
GELU_B = 0.044715


def slope_table(head_count):
    return np.power(2.0, -8.0 * (np.arange(head_count) + 1.0) / head_count)


def ahead(u):
    return u + 1 + DEPTH + sum(u >= step for step in DEEPER)


def slope_at(head):
    value = jnp.float32(0.0)
    for index, slope in enumerate(slope_table(H)):
        value = jnp.where(head == index, jnp.float32(slope), value)
    return value


def weight_cols(c):
    return pl.ds(0, 3 * c), pl.ds(3 * c, c), pl.ds(4 * c, 4 * c), pl.ds(8 * c, 4 * c)


def mm_nn(a, b):
    return lax.dot_general(a, b, (((1,), (0,)), ((), ())), preferred_element_type=F32)


def mm_nt(a, b):
    return lax.dot_general(a, b, (((1,), (1,)), ((), ())), preferred_element_type=F32)


def mm_tn(a, b):
    return lax.dot_general(a, b, (((0,), (0,)), ((), ())), preferred_element_type=F32)


def normalise(v):
    centered = v - jnp.mean(v, axis=-1, keepdims=True)
    inverse = lax.rsqrt(jnp.mean(centered * centered, axis=-1, keepdims=True) + EPS_NORM)
    return centered * inverse, inverse


def rows_of(index, size):
    return pl.ds(pl.multiple_of(index * size, size), size)


class Place:
    def __init__(self, zn, xn, yn):
        self.zn, self.xn, self.yn = zn, xn, yn
        self.dp = lax.axis_index("dp")
        self.seq = lax.axis_index("seq")
        self.z, self.x = self.dp // xn, lax.rem(self.dp, xn)
        self.y, self.c = self.seq // CORES, lax.rem(self.seq, CORES)

    def zo(self, k):
        return lax.rem(self.z + k + self.zn, self.zn)

    def xo(self, k):
        return lax.rem(self.x + k + self.xn, self.xn)

    def yo(self, k):
        return lax.rem(self.y + k + self.yn, self.yn)

    def dev(self, dz=0, dx=0, dy=0, dc=0):
        core = (1 - self.c) if dc else self.c
        return (self.zo(dz) * self.xn + self.xo(dx), self.yo(dy) * CORES + core)

    def dp_at(self, dz, dx):
        return self.zo(dz) * self.xn + self.xo(dx)

    def seq_at(self, dy, dc):
        core = (1 - self.c) if dc else self.c
        return self.yo(dy) * CORES + core

    def seq_others(self):
        return [(y, c) for c in range(CORES) for y in range(self.yn) if y or c]

    def dp_others(self):
        return [(z, x) for x in range(self.xn) for z in range(self.zn) if z or x]

    def peers(self, wide=False):
        if wide:
            out = [self.dev(dy=y, dc=c) for y, c in self.seq_others()]
            return out + [self.dev(dz=z, dx=x) for z, x in self.dp_others()]
        out = [self.dev(dc=1)]
        out += [self.dev(dy=k) for k in range(1, self.yn)]
        out += [self.dev(dx=k) for k in range(1, self.xn)]
        out += [self.dev(dz=k) for k in range(1, self.zn)]
        return out

    def barrier(self, wide=False):
        sem = pltpu.get_barrier_semaphore()
        peers = self.peers(wide)
        for peer in peers:
            pl.semaphore_signal(sem, inc=1, device_id=peer, device_id_type=MESH)
        pl.semaphore_wait(sem, len(peers))


def near_first(count):
    order = []
    for k in range(1, count):
        order.append((min(k, count - k), k))
    return [k for unused, k in sorted(order)]


def remote(src, dst, send, recv, dev):
    return pltpu.make_async_remote_copy(
        src_ref=src, dst_ref=dst, send_sem=send, recv_sem=recv, device_id=dev, device_id_type=MESH
    )


def all_sum(place, value, slots, send, recv):
    stages = (
        (CORES, place.c, lambda k: place.dev(dc=1), lambda k: 1 - place.c),
        (place.yn, place.y, lambda k: place.dev(dy=k), lambda k: place.yo(-k)),
        (place.xn, place.x, lambda k: place.dev(dx=k), lambda k: place.xo(-k)),
        (place.zn, place.z, lambda k: place.dev(dz=k), lambda k: place.zo(-k)),
    )
    base = 0
    at = 0
    for size, mine, target, origin in stages:
        slots[base + mine] = value
        own = slots.at[base + mine]
        for k in range(1, size):
            remote(own, own, send.at[at + k - 1], recv.at[at + k - 1], target(k)).start()
        for k in range(1, size):
            came = slots.at[base + origin(k)]
            remote(came, came, send.at[at + k - 1], recv.at[at + k - 1], target(k)).wait_recv()
        for k in range(1, size):
            remote(own, own, send.at[at + k - 1], recv.at[at + k - 1], target(k)).wait_send()
        value = slots[base]
        for k in range(1, size):
            value = value + slots[base + k]
        base += size
        at += size - 1
    return value


def sum_slots(zn, xn, yn):
    return CORES + yn + xn + zn, 1 + (yn - 1) + (xn - 1) + (zn - 1)


def all_sum_wide(place, value, slots, send, recv):
    p = place
    stages = (
        (p.seq, [(p.dev(dy=y, dc=c), p.seq_at(-y, c)) for y, c in p.seq_others()]),
        (p.dp, [(p.dev(dz=z, dx=x), p.dp_at(-z, -x)) for z, x in p.dp_others()]),
    )
    base = 0
    at = 0
    for mine, others in stages:
        slots[base + mine] = value
        own = slots.at[base + mine]
        for k, (target, origin) in enumerate(others):
            remote(own, own, send.at[at + k], recv.at[at + k], target).start()
        for k, (target, origin) in enumerate(others):
            came = slots.at[base + origin]
            remote(came, came, send.at[at + k], recv.at[at + k], target).wait_recv()
        for k, (target, origin) in enumerate(others):
            remote(own, own, send.at[at + k], recv.at[at + k], target).wait_send()
        value = slots[base]
        for k in range(len(others)):
            value = value + slots[base + k + 1]
        base += len(others) + 1
        at += len(others)
    return value


class Gather:
    def __init__(self, place, buf, block, send, recv):
        self.p, self.buf, self.block, self.send, self.recv = place, buf, block, send, recv

    def at(self, dy, dc):
        return self.buf.at[rows_of(self.p.seq_at(dy, dc), self.block)]

    def start(self):
        p, own = self.p, self.at(0, 0)
        for k in range(1, p.yn):
            remote(own, own, self.send.at[k], self.recv.at[k], p.dev(dy=k)).start()
        remote(own, own, self.send.at[0], self.recv.at[0], p.dev(dc=1)).start()

    def wait_chip(self):
        came = self.at(0, 1)
        remote(came, came, self.send.at[0], self.recv.at[0], self.p.dev(dc=1)).wait_recv()

    def forward(self):
        p = self.p
        for k in range(1, p.yn):
            came = self.at(-k, 0)
            remote(came, came, self.send.at[k], self.recv.at[k], p.dev(dy=k)).wait_recv()
            f = p.yn - 1 + k
            remote(came, came, self.send.at[f], self.recv.at[f], p.dev(dc=1)).start()

    def wait_rest(self):
        p = self.p
        for k in range(1, p.yn):
            f = p.yn - 1 + k
            came = self.at(-k, 1)
            remote(came, came, self.send.at[f], self.recv.at[f], p.dev(dc=1)).wait_recv()
        own = self.at(0, 0)
        for k in range(1, p.yn):
            remote(own, own, self.send.at[k], self.recv.at[k], p.dev(dy=k)).wait_send()
            f = p.yn - 1 + k
            sent = self.at(-k, 0)
            remote(sent, sent, self.send.at[f], self.recv.at[f], p.dev(dc=1)).wait_send()
        remote(own, own, self.send.at[0], self.recv.at[0], p.dev(dc=1)).wait_send()


class Scatter:
    def __init__(self, place, sbuf, rbuf, ysend, yrecv, acc, send, recv):
        self.p = place
        self.sbuf, self.rbuf, self.ysend, self.yrecv, self.acc = sbuf, rbuf, ysend, yrecv, acc
        self.send, self.recv = send, recv

    def core(self, k):
        return remote(
            self.sbuf.at[k], self.rbuf.at[k], self.send.at[k], self.recv.at[k], self.p.dev(dc=1)
        )

    def cross(self, k):
        s = self.p.yn + k - 1
        return remote(
            self.ysend.at[k - 1],
            self.yrecv.at[k - 1],
            self.send.at[s],
            self.recv.at[s],
            self.p.dev(dy=k),
        )

    def start(self, part):
        p = self.p
        for k in list(range(1, p.yn)) + [0]:
            self.sbuf[k] = part(p.seq_at(k, 1)).astype(BF16)
            self.core(k).start()
            mine = part(p.seq_at(k, 0))
            self.core(k).wait_recv()
            mine = mine + self.rbuf[k].astype(F32)
            if k:
                self.ysend[k - 1] = mine.astype(BF16)
                self.cross(k).start()
            else:
                self.acc[...] = mine

    def wait(self):
        p = self.p
        for k in range(1, p.yn):
            self.cross(k).wait_recv()
        for k in range(1, p.yn):
            self.cross(k).wait_send()
        for k in range(p.yn):
            self.core(k).wait_send()

    def rows(self, at):
        value = self.acc[at, :]
        for k in range(1, self.p.yn):
            value = value + self.yrecv[k - 1, at, :].astype(F32)
        return value


def row_loop(total, step, fn):
    def one(i, unused):
        fn(rows_of(i, step))
        return unused

    lax.fori_loop(0, total // step, one, 0)


def twice(v):
    return jnp.concatenate([v, v], axis=1)


def key_bias(bias, slots, length, slope):
    def one(i, unused):
        key = i * 64 + lax.broadcasted_iota(jnp.int32, (64, 128), 0)
        bias[rows_of(i, 64), :] = jnp.where(key < length, slope * key.astype(F32), -jnp.inf)
        return unused

    lax.fori_loop(0, slots // 64, one, 0)


def turn_rows(target, rows, slots):
    for c in range(slots // 256):
        at = pl.ds(c * 256, 256)
        target[:, at] = rows(at).astype(F32).T.astype(BF16)


def forward_kernel(dims, *refs):
    (layers, slots, width, block, local_width, local_ff, groups, zn, xn, yn) = dims
    heads = local_width // HD
    refs = list(refs)

    def take(count):
        out = refs[:count]
        del refs[:count]
        return out

    lengths, x_in, g_in, norm_in = take(4)
    masters = take(4)
    out, norm_out = take(2)
    g_save, w_save = take(2)
    xn1_save, xn2_save, qkv_save, ctx_save, lse_save, act_save, dact_save, hid_save, mid_save = take(9)
    w = take(1)[0]
    xn1, xn2, qkv, ctx, lse, act, dact, hid, mid, upper, norm_place, bias, turned = take(13)
    sbuf, rbuf, ysend, yrecv, acc, nslots = take(6)
    zsend, zrecv, xsend, xrecv, wsave_sem = take(5)
    ag_send, ag_recv, rs_send, rs_recv, ns_send, ns_recv, save_sem = take(7)
    g_low, g_sem = take(2)

    p = Place(zn, xn, yn)
    z_order = near_first(zn)
    length = lengths[0]
    cols_qkv, cols_o, cols_up, cols_down = weight_cols(local_width)

    unit_count = UNITS * layers
    slopes = [slope_at(p.seq * heads + h) for h in range(heads)]

    def unit_cols(u):
        return pl.ds((u % UNITS) * local_width, local_width)

    def z_copy(u, dz, zi):
        here = w.at[u // UNITS, zi, p.x, :, unit_cols(u)]
        return remote(here, here, zsend.at[u, dz - 1], zrecv.at[u, dz - 1], p.dev(dz=dz))

    def x_copy(u, dx, dz):
        here = w.at[u // UNITS, p.zo(-dz), p.x, :, unit_cols(u)]
        return remote(here, here, xsend.at[u, dx - 1, dz], xrecv.at[u, dx - 1, dz], p.dev(dx=dx))

    def prepare(u):
        l, v = divmod(u, UNITS)
        cols = unit_cols(u)
        if v < 3:
            w[l, p.z, p.x, :, cols] = masters[0][l, v].astype(BF16)
        elif 4 <= v < 8:
            source = pl.ds((v - 4) * local_width, local_width)
            w[l, p.z, p.x, :, cols] = masters[2][l, :, source].astype(BF16)
        else:
            source, base = (masters[1], 0) if v == 3 else (masters[3], (v - 8) * local_width)
            for c in range(local_width // 128):
                block_t = source[l, pl.ds(base + c * 128, 128), :].T
                w[l, p.z, p.x, :, pl.ds(v * local_width + c * 128, 128)] = block_t.astype(BF16)

    def start_unit(u):
        for dz in z_order:
            z_copy(u, dz, p.z).start()
        for dx in range(1, xn):
            x_copy(u, dx, 0).start()

    def pump(u):
        for dz in z_order:
            z_copy(u, dz, p.zo(-dz)).wait_recv()
            for dx in range(1, xn):
                x_copy(u, dx, dz).start()
        for later in range(ahead(u - 1), min(ahead(u), unit_count)):
            start_unit(later)

    def pumps(l, *tables):
        for at, units in enumerate(tables):
            if units:

                @pl.when(l == at)
                def _(units=units):
                    for u in units:
                        pump(u)

    def save_weight(l):
        return pltpu.make_async_copy(w.at[l], w_save.at[l], wsave_sem.at[l])

    def need(l, low, high):
        def one(v, unused):
            u = UNITS * l + v
            at = w.at[0, 0, 0, :, pl.ds(0, local_width)]
            for dz in range(zn):
                for dx in range(1, xn):
                    remote(
                        at, at, xsend.at[u, dx - 1, dz], xrecv.at[u, dx - 1, dz], p.dev(dx=dx)
                    ).wait_recv()
            return unused

        lax.fori_loop(low, high, one, 0)

    def finish_weight(l):
        def one(v, unused):
            u = UNITS * l + v
            at = w.at[0, 0, 0, :, pl.ds(0, local_width)]
            for dz in z_order:
                remote(
                    at, at, zsend.at[u, dz - 1], zrecv.at[u, dz - 1], p.dev(dz=dz)
                ).wait_send()
            for dz in range(zn):
                for dx in range(1, xn):
                    remote(
                        at, at, xsend.at[u, dx - 1, dz], xrecv.at[u, dx - 1, dz], p.dev(dx=dx)
                    ).wait_send()
            return unused

        lax.fori_loop(0, UNITS, one, 0)
        save_weight(l).wait()

    def weight(l, cols):
        return w[l, :, :, :, cols].reshape(width, cols.size)

    def save(l, which, src, dst):
        return pltpu.make_async_copy(src, dst, save_sem.at[l, which])

    def saves(l):
        return (
            save(l, 0, xn1.at[l], xn1_save.at[l]),
            save(l, 1, xn2.at[l], xn2_save.at[l]),
            save(l, 2, qkv.at[l], qkv_save.at[l]),
            save(l, 3, ctx.at[l], ctx_save.at[l]),
            save(l, 4, lse.at[l], lse_save.at[l]),
            save(l, 5, act.at[l], act_save.at[l]),
            save(l, 6, dact.at[l], dact_save.at[l]),
            save(l, 7, hid.at[l], hid_save.at[l]),
            save(l, 8, mid.at[l], mid_save.at[l]),
        )

    p.barrier()
    for u in range(ahead(-1)):
        prepare(u)
        start_unit(u)
    first = p.seq * block
    g_zero = Gather(p, g_save, block, ag_send.at[2 * layers], ag_recv.at[2 * layers])

    def mask_in(i, unused):
        at = rows_of(i, 32)
        slot = first + i * 32 + lax.broadcasted_iota(jnp.int32, (32, 1), 0)
        g_low[at, :] = jnp.where(slot < length, g_in[at, :].astype(F32), 0.0).astype(BF16)
        return unused

    lax.fori_loop(0, block // 32, mask_in, 0)
    g_own = pltpu.make_async_copy(g_low, g_save.at[rows_of(p.seq, block)], g_sem.at[0])
    g_own.start()
    g_own.wait()
    piece = width // (groups * CORES * yn)
    at_lane = (p.dp * CORES * yn + p.seq) * piece
    norm_place[...] = jnp.zeros_like(norm_place)
    norm_place[:, rows_of(at_lane // 128, 128)] = pltpu.roll(norm_in[...], lax.rem(at_lane, 128), 1)
    norm_out[...] = all_sum(p, norm_place[...], nslots, ns_send, ns_recv)
    for u in range(ahead(-1), UNITS):
        prepare(u)

    def load_in(at):
        hid[0, at, :] = x_in[at, :].astype(F32)

    row_loop(block, 64, load_in)

    def norm_row(index):
        return norm_out[pl.ds(index, 1), :]

    def norm_into(l, source, target, row):
        gain, bias = norm_row(4 * l + row), norm_row(4 * l + row + 1)

        def one(i, unused):
            scaled, inverse = normalise(source[l, rows_of(i, 32), :])
            at = pl.ds(pl.multiple_of(first + i * 32, 32), 32)
            target[l, at, :] = (scaled * gain + bias).astype(BF16)
            return unused

        lax.fori_loop(0, block // 32, one, 0)

    def attention(l):
        step = 256
        causal = lax.broadcasted_iota(jnp.int32, (step, step), 0) <= lax.broadcasted_iota(
            jnp.int32, (step, step), 1
        )
        for h in range(heads):
            cols = pl.ds(h * HD, HD)
            k_cols = pl.ds(local_width + h * HD, HD)
            v_cols = pl.ds(2 * local_width + h * HD, HD)
            key_bias(bias, slots, length, slopes[h])
            turn_rows(turned, lambda at: qkv[l, at, v_cols], slots)
            for b in range(slots // step):
                here = pl.ds(b * step, step)
                before = pl.ds(0, b * step)
                q = qkv[l, here, cols]
                raw = mm_nt(qkv[l, here, k_cols], q) * SCORE_SCALE + twice(bias[here, :])
                raw = jnp.where(causal, raw, -jnp.inf)
                top = jnp.max(raw, axis=0, keepdims=True)
                if b:
                    past = mm_nt(qkv[l, before, k_cols], q) * SCORE_SCALE + twice(bias[before, :])
                    top = jnp.maximum(top, jnp.max(past, axis=0, keepdims=True))
                e_here = jnp.exp(raw - top)
                total = jnp.sum(e_here, axis=0, keepdims=True)
                value = mm_nn(turned[:, here], e_here.astype(BF16))
                if b:
                    e_past = jnp.exp(past - top)
                    total = total + jnp.sum(e_past, axis=0, keepdims=True)
                    value = value + mm_nn(turned[:, before], e_past.astype(BF16))
                ctx[l, here, cols] = (value / total).T.astype(BF16)
                lse[l, pl.ds(h, 1), here] = top + jnp.log(total)

    def layer(l, unused):
        last = layers - 1
        g_one = Gather(p, xn1.at[l], block, ag_send.at[2 * l], ag_recv.at[2 * l])
        g_two = Gather(p, xn2.at[l], block, ag_send.at[2 * l + 1], ag_recv.at[2 * l + 1])
        rs = [
            Scatter(
                p, sbuf, rbuf, ysend, yrecv, acc,
                rs_send.at[2 * l + i], rs_recv.at[2 * l + i],
            )
            for i in range(2)
        ]
        save_at = saves(l)
        save_at[7].start()
        norm_into(l, hid, xn1, 0)
        g_one.start()

        @pl.when(l == 0)
        def _():
            for u in range(UNITS, unit_count):
                prepare(u)

        pumps(l, *PUMPS[0])

        def project(index):
            at = rows_of(index, block)
            qkv[l, at, :] = mm_nn(xn1[l, at, :], weight(l, cols_qkv)).astype(BF16)

        g_one.wait_chip()
        g_one.forward()

        @pl.when(l == 0)
        def _():
            g_zero.start()

        need(l, 0, 3)
        project(p.seq_at(0, 0))
        project(p.seq_at(0, 1))
        pumps(l, *PUMPS[1])
        g_one.wait_rest()
        save_at[0].start()
        for k in range(1, yn):
            project(p.seq_at(-k, 0))
            project(p.seq_at(-k, 1))
        save_at[2].start()
        attention(l)
        save_at[3].start()
        save_at[4].start()
        pumps(l, *PUMPS[2])
        need(l, 3, 4)
        rs[0].start(lambda b: mm_nt(ctx[l, rows_of(b, block), :], weight(l, cols_o)))
        pumps(l, *PUMPS[3])

        @pl.when(l == 0)
        def _():
            g_zero.wait_chip()
            g_zero.forward()

        rs[0].wait()

        def add_middle(at):
            mid[l, at, :] = hid[l, at, :] + rs[0].rows(at)

        row_loop(block, 32, add_middle)
        save_at[8].start()
        norm_into(l, mid, xn2, 2)
        g_two.start()
        pumps(l, *PUMPS[4])
        need(l, 4, 8)

        def expand(index):
            base = pl.multiple_of(index * block, block)
            upper[...] = mm_nn(xn2[l, pl.ds(base, block), :], weight(l, cols_up))

            def one(i, unused):
                u = upper[rows_of(i, 16), :]
                at = pl.ds(pl.multiple_of(base + i * 16, 16), 16)
                square = u * u
                t = jnp.tanh(GELU_A * u * (1.0 + GELU_B * square))
                half = 0.5 * (1.0 + t)
                act[l, at, :] = (u * half).astype(BF16)
                slope = (0.5 * GELU_A) * u * (1.0 - t * t) * (1.0 + (3.0 * GELU_B) * square)
                dact[l, at, :] = (half + slope).astype(BF16)
                return unused

            lax.fori_loop(0, block // 16, one, 0)

        expand(p.seq_at(0, 0))
        g_two.wait_chip()
        expand(p.seq_at(0, 1))
        pumps(l, *PUMPS[5])
        g_two.forward()
        pumps(l, *PUMPS[6])
        g_two.wait_rest()
        save_at[1].start()
        for k in range(1, yn):
            expand(p.seq_at(-k, 0))
            expand(p.seq_at(-k, 1))
        save_at[5].start()
        save_at[6].start()
        pumps(l, *PUMPS[7])
        need(l, 8, 12)
        save_weight(l).start()
        rs[1].start(lambda b: mm_nt(act[l, rows_of(b, block), :], weight(l, cols_down)))
        pumps(l, *PUMPS[8])
        rs[1].wait()

        @pl.when(l < last)
        def _():
            def add_next(at):
                hid[l + 1, at, :] = mid[l, at, :] + rs[1].rows(at)

            row_loop(block, 32, add_next)

        @pl.when(l == last)
        def _():
            def add_out(at):
                out[at, :] = mid[l, at, :] + rs[1].rows(at)

            row_loop(block, 32, add_out)

        return unused

    lax.fori_loop(0, layers, layer, 0)

    def finish(l, unused):
        finish_weight(l)
        for item in saves(l):
            item.wait()
        return unused

    g_zero.wait_rest()
    lax.fori_loop(0, layers, finish, 0)


def run_forward(dims, lengths, x_in, g_in, norm_in, masters):
    (layers, slots, width, block, local_width, local_ff, groups, zn, xn, yn) = dims
    shard = width // groups
    slot_count, sem_count = sum_slots(zn, xn, yn)

    def saved(*shape, dtype=BF16):
        return jax.ShapeDtypeStruct((layers,) + shape, dtype)

    vmem = pl.BlockSpec(memory_space=pltpu.VMEM)
    smem = pl.BlockSpec(memory_space=pltpu.SMEM)
    hbm = pl.BlockSpec(memory_space=pl.ANY)
    kept = [
        saved(zn, xn, shard, UNITS * local_width),
        saved(slots, width),
        saved(slots, width),
        saved(slots, 3 * local_width),
        saved(slots, local_width),
        saved(8, slots, dtype=F32),
        saved(slots, local_ff),
        saved(slots, local_ff),
        saved(block, width, dtype=F32),
        saved(block, width, dtype=F32),
    ]
    dma = pltpu.SemaphoreType.DMA
    return pl.pallas_call(
        functools.partial(forward_kernel, dims),
        out_shape=[
            jax.ShapeDtypeStruct((block, width), F32),
            jax.ShapeDtypeStruct((4 * layers, width), F32),
        ]
        + [jax.ShapeDtypeStruct((slots, width), BF16)]
        + kept,
        in_specs=[smem] + [vmem] * 7,
        out_specs=[vmem, vmem] + [hbm] * (1 + len(kept)),
        scratch_shapes=[pltpu.VMEM(k.shape, k.dtype) for k in kept]
        + [
            pltpu.VMEM((block, local_ff), F32),
            pltpu.VMEM((4 * layers, width), F32),
            pltpu.VMEM((slots, 128), F32),
            pltpu.VMEM((HD, slots), BF16),
            pltpu.VMEM((yn, block, width), BF16),
            pltpu.VMEM((yn, block, width), BF16),
            pltpu.VMEM((yn - 1, block, width), BF16),
            pltpu.VMEM((yn - 1, block, width), BF16),
            pltpu.VMEM((block, width), F32),
            pltpu.VMEM((slot_count, 4 * layers, width), F32),
            dma((UNITS * layers, zn - 1)),
            dma((UNITS * layers, zn - 1)),
            dma((UNITS * layers, xn - 1, zn)),
            dma((UNITS * layers, xn - 1, zn)),
            dma((layers,)),
            dma((2 * layers + 1, 2 * yn - 1)),
            dma((2 * layers + 1, 2 * yn - 1)),
            dma((2 * layers, 2 * yn - 1)),
            dma((2 * layers, 2 * yn - 1)),
            dma((sem_count,)),
            dma((sem_count,)),
            dma((layers, 9)),
            pltpu.VMEM((block, width), BF16),
            dma((1,)),
        ],
        compiler_params=pltpu.CompilerParams(
            collective_id=0, has_side_effects=True, vmem_limit_bytes=62 * 2**20
        ),
        name="forward_layers",
    )(lengths, x_in, g_in, norm_in, *masters)

def backward_kernel(dims, *refs):
    (layers, slots, width, block, local_width, local_ff, groups, zn, xn, yn) = dims
    heads = local_width // HD
    shard = width // groups
    slab = shard * xn
    refs = list(refs)

    def take(count):
        out = refs[:count]
        del refs[:count]
        return out

    lengths, g_in, norms, g_all = take(4)
    kept = take(10)
    g_out, norm_grad, total_out = take(3)
    shards = take(1)[0]
    held = take(10)
    w, xn1, xn2, qkv, ctx, lse, act, dact, hid, mid = held
    gfull, gbfull, gctx, dqkv, dk, dv, bias, turned, g, gm, npart = take(11)
    dw, xland, zland = take(3)
    sbuf, rbuf, ysend, yrecv, acc, nslots, tslots = take(7)
    zsend, zrecv, xsend, xrecv = take(4)
    ag_send, ag_recv, rs_send, rs_recv, ns_send, ns_recv, ts_send, ts_recv, load_sem = take(9)

    p = Place(zn, xn, yn)
    length = lengths[0]
    first = p.seq * block
    gu = dact
    w_all = kept[0]

    slopes = [slope_at(p.seq * heads + h) for h in range(heads)]
    weight_at = weight_cols(local_width)
    cols_qkv, cols_o, cols_up, cols_down = weight_at

    def load(l, which):
        if which < 4:
            cols = weight_at[which]
            return pltpu.make_async_copy(w_all.at[l, :, :, :, cols], w.at[:, :, :, cols], load_sem.at[which])
        return pltpu.make_async_copy(kept[which - 3].at[l], held[which - 3], load_sem.at[which])

    def weight(cols):
        return w[:, :, :, cols].reshape(width, cols.size)

    def unit_cols(v):
        return pl.ds(v * local_width, local_width)

    def x_copy(l, v, dx):
        cols = unit_cols(v)
        return remote(
            dw.at[:, p.xo(dx), :, cols],
            xland.at[l, dx - 1, :, :, cols],
            xsend.at[l, v, dx - 1],
            xrecv.at[l, v, dx - 1],
            p.dev(dx=dx),
        )

    def z_copy(l, v, zi):
        cols = unit_cols(v)
        return remote(
            dw.at[p.zo(zi), p.x, :, cols],
            zland.at[l, zi - 1, :, cols],
            zsend.at[l, v, zi - 1],
            zrecv.at[l, v, zi - 1],
            p.dev(dz=zi),
        )

    z_order = near_first(zn)
    zi_order = z_order[::-1] + [0]

    def weight_grad(left, right, low, count):
        def one(i, unused):
            part = mm_tn(left[:, rows_of(i, slab)], right[...]).astype(BF16)
            dw[i, :, :, pl.ds(low * local_width, count * local_width)] = part.reshape(
                xn, shard, count * local_width
            )
            return unused

        lax.fori_loop(0, zn, one, 0)

    def send_x(l, *units):
        for v in units:
            for dx in range(1, xn):
                x_copy(l, v, dx).start()

    def reduce_x(l, *units):
        for v in units:
            cols = unit_cols(v)
            for dx in range(1, xn):
                x_copy(l, v, dx).wait_recv()
            for zi in zi_order:
                zz = p.zo(zi)

                def one(i, unused, zi=zi, cols=cols, zz=zz):
                    here = rows_of(i, 32)
                    value = dw[zz, p.x, here, cols].astype(F32)
                    for dx in range(1, xn):
                        value = value + xland[l, dx - 1, zz, here, cols].astype(F32)
                    if zi:
                        dw[zz, p.x, here, cols] = value.astype(BF16)
                    else:
                        shards[l, here, cols] = value
                    return unused

                lax.fori_loop(0, shard // 32, one, 0)
                if zi:
                    z_copy(l, v, zi).start()

    def reduce_z(l, low, high):
        def unit(v, unused):
            cols = pl.ds(pl.multiple_of(v * local_width, local_width), local_width)
            here = dw.at[0, 0, :, pl.ds(0, local_width)]
            for zi in z_order:
                remote(
                    here, here, zsend.at[l, v, zi - 1], zrecv.at[l, v, zi - 1], p.dev(dz=zi)
                ).wait_recv()

            def one(at):
                value = shards[l, at, cols]
                for zi in range(1, zn):
                    value = value + zland[l, zi - 1, at, cols].astype(F32)
                shards[l, at, cols] = value

            row_loop(shard, 32, one)
            for zi in z_order:
                remote(
                    here, here, zsend.at[l, v, zi - 1], zrecv.at[l, v, zi - 1], p.dev(dz=zi)
                ).wait_send()
            every = dw.at[:, 0, :, pl.ds(0, local_width)]
            for dx in range(1, xn):
                remote(
                    every, every, xsend.at[l, v, dx - 1], xrecv.at[l, v, dx - 1], p.dev(dx=dx)
                ).wait_send()
            return unused

        lax.fori_loop(low, high, unit, 0)

    def norm_back(l, source, rs, base, row, target, low):
        gain = norms[pl.ds(4 * l + row, 1), :]
        zero = jnp.zeros((8, width), F32)

        def one(i, carry):
            at = rows_of(i, 32)
            scaled, inverse = normalise(source[at, :])
            e = rs.rows(at)
            eg = e * gain
            part = inverse * (
                eg
                - jnp.mean(eg, axis=-1, keepdims=True)
                - scaled * jnp.mean(eg * scaled, axis=-1, keepdims=True)
            )
            value = base[at, :] + part
            target[at, :] = value
            if low is not None:
                low[pl.ds(pl.multiple_of(first + i * 32, 32), 32), :] = value.astype(BF16)
            es = e * scaled
            gains, biases = carry
            for r in range(4):
                gains = gains + es[r * 8 : r * 8 + 8]
                biases = biases + e[r * 8 : r * 8 + 8]
            return gains, biases

        gains, biases = lax.fori_loop(0, block // 32, one, (zero, zero))
        npart[pl.ds(4 * l + row, 1), :] = jnp.sum(gains, axis=0, keepdims=True)
        npart[pl.ds(4 * l + row + 1, 1), :] = jnp.sum(biases, axis=0, keepdims=True)

    def attention(between):
        step = 256
        causal = lax.broadcasted_iota(jnp.int32, (step, step), 0) <= lax.broadcasted_iota(
            jnp.int32, (step, step), 1
        )
        for h in range(heads):
            cols = pl.ds(h * HD, HD)
            k_cols = pl.ds(local_width + h * HD, HD)
            v_cols = pl.ds(2 * local_width + h * HD, HD)
            key_bias(bias, slots, length, slopes[h])
            turn_rows(turned, lambda at: qkv[at, k_cols], slots)
            for b in range(slots // step):
                here = pl.ds(b * step, step)
                before = pl.ds(0, b * step)
                q = qkv[here, cols]
                gc = gctx[here, cols]
                shift = lse[pl.ds(h, 1), here]
                raw = mm_nt(qkv[here, k_cols], q) * SCORE_SCALE + twice(bias[here, :])
                p_here = jnp.exp(jnp.where(causal, raw, -jnp.inf) - shift)
                dp_here = mm_nt(qkv[here, v_cols], gc)
                delta = jnp.sum(p_here * dp_here, axis=0, keepdims=True)
                dv[here, :] = mm_nn(p_here.astype(BF16), gc)
                if b:
                    past = mm_nt(qkv[before, k_cols], q) * SCORE_SCALE + twice(bias[before, :])
                    p_past = jnp.exp(past - shift)
                    dp_past = mm_nt(qkv[before, v_cols], gc)
                    delta = delta + jnp.sum(p_past * dp_past, axis=0, keepdims=True)
                    dv[before, :] += mm_nn(p_past.astype(BF16), gc)
                ds_here = (p_here * (dp_here - delta)).astype(BF16)
                dq = mm_nn(turned[:, here], ds_here)
                dk[here, :] = mm_nn(ds_here, q)
                if b:
                    ds_past = (p_past * (dp_past - delta)).astype(BF16)
                    dq = dq + mm_nn(turned[:, before], ds_past)
                    dk[before, :] += mm_nn(ds_past, q)
                dqkv[here, cols] = (dq * SCORE_SCALE).T.astype(BF16)
                between(h * (slots // step) + b + 1, heads * (slots // step))

            def store(at):
                dqkv[at, k_cols] = (dk[at, :] * SCORE_SCALE).astype(BF16)
                dqkv[at, v_cols] = dv[at, :].astype(BF16)

            row_loop(slots, 64, store)

    p.barrier(wide=True)

    def mask_in(i, unused):
        at = rows_of(i, 32)
        slot = first + i * 32 + lax.broadcasted_iota(jnp.int32, (32, 1), 0)
        g[at, :] = jnp.where(slot < length, g_in[at, :].astype(F32), 0.0)
        return unused

    lax.fori_loop(0, block // 32, mask_in, 0)
    load_order = (3, 10, 2, 9, 5, 12, 1, 7, 6, 8, 0, 4, 11)

    def layer(step, unused):
        l = layers - 1 - step
        later = l + 1
        g_one = Gather(p, gfull, block, ag_send.at[2 * l], ag_recv.at[2 * l])
        g_two = Gather(p, gbfull, block, ag_send.at[2 * l + 1], ag_recv.at[2 * l + 1])
        rs = [
            Scatter(
                p, sbuf, rbuf, ysend, yrecv, acc, rs_send.at[2 * l + i], rs_recv.at[2 * l + i]
            )
            for i in range(2)
        ]

        def low_in(i, unused):
            at = pl.ds(pl.multiple_of(first + i * 32, 32), 32)
            gfull[at, :] = g[rows_of(i, 32), :].astype(BF16)
            return unused

        all_in = pltpu.make_async_copy(g_all, gfull, load_sem.at[13])

        @pl.when(step == 0)
        def _():
            all_in.start()

        @pl.when(step > 0)
        def _():
            lax.fori_loop(0, block // 32, low_in, 0)
            g_one.start()

        for which in load_order:
            load(l, which).start()
        load(l, 3).wait()
        load(l, 10).wait()

        @pl.when(step == 0)
        def _():
            all_in.wait()


        def upper_grad(index):
            at = rows_of(index, block)
            value = mm_nn(gfull[at, :], weight(cols_down))
            gu[at, :] = (value * dact[at, :].astype(F32)).astype(BF16)

        upper_grad(p.seq_at(0, 0))

        @pl.when(step > 0)
        def _():
            g_one.wait_chip()

        upper_grad(p.seq_at(0, 1))

        @pl.when(step > 0)
        def _():
            g_one.forward()

        @pl.when(step > 0)
        def _():
            reduce_x(later, 0)
            send_x(later, 2)
            g_one.wait_rest()

        for k in range(1, yn):
            upper_grad(p.seq_at(-k, 0))
            upper_grad(p.seq_at(-k, 1))
        load(l, 2).wait()
        rs[0].start(lambda b: mm_nt(gu[rows_of(b, block), :], weight(cols_up)))
        load(l, 9).wait()
        load(l, 5).wait()

        @pl.when(step > 0)
        def _():
            reduce_z(later, 3, 12)

        weight_grad(gfull, act, 8, 4)
        send_x(l, 8)
        weight_grad(xn2, gu, 4, 4)
        send_x(l, 9)

        @pl.when(step > 0)
        def _():
            reduce_x(later, 1, 2)

        load(l, 12).wait()
        reduce_x(l, 8)
        send_x(l, 10)
        rs[0].wait()
        norm_back(l, mid, rs[0], g, 2, gm, gbfull)
        g_two.start()
        reduce_x(l, 9)
        send_x(l, 11)
        load(l, 1).wait()

        def context_grad(index):
            at = rows_of(index, block)
            gctx[at, :] = mm_nn(gbfull[at, :], weight(cols_o)).astype(BF16)

        context_grad(p.seq_at(0, 0))
        g_two.wait_chip()
        context_grad(p.seq_at(0, 1))
        reduce_x(l, 10)
        send_x(l, 4)
        g_two.forward()

        @pl.when(step > 0)
        def _():
            reduce_z(later, 0, 3)

        g_two.wait_rest()
        for k in range(1, yn):
            context_grad(p.seq_at(-k, 0))
            context_grad(p.seq_at(-k, 1))
        load(l, 7).wait()
        weight_grad(gbfull, ctx, 3, 1)
        reduce_x(l, 11)
        send_x(l, 5)
        load(l, 6).wait()
        load(l, 8).wait()

        def between(done, count):
            if done == (count * 3) // 8:
                reduce_x(l, 4)
                send_x(l, 6)
            if done == (count * 6) // 8:
                reduce_x(l, 5)
                send_x(l, 7)

        attention(between)
        load(l, 0).wait()
        load(l, 4).wait()

        @pl.when(l == 0)
        def _():
            weight_grad(xn1, dqkv, 0, 3)

        reduce_x(l, 6)
        send_x(l, 3)
        rs[1].start(lambda b: mm_nt(dqkv[rows_of(b, block), :], weight(cols_qkv)))

        @pl.when(l > 0)
        def _():
            weight_grad(xn1, dqkv, 0, 3)

        reduce_x(l, 7)
        send_x(l, 0)
        reduce_x(l, 3)
        send_x(l, 1)
        load(l, 11).wait()
        rs[1].wait()
        norm_back(l, hid, rs[1], gm, 0, g, None)
        return unused

    lax.fori_loop(0, layers, layer, 0)
    reduce_x(0, 0)
    send_x(0, 2)
    reduce_x(0, 1, 2)
    g_out[...] = g[...]
    norm_grad[...] = all_sum(p, npart[...], nslots, ns_send, ns_recv)
    def squares(i, total):
        l, at = i // (shard // 8), rows_of(lax.rem(i, shard // 8), 8)
        value = shards[l, at, :]
        value = value * value
        for c in range(UNITS * local_width // 128):
            total = total + value[:, c * 128 : (c + 1) * 128]
        return total

    tile = jnp.zeros((8, 128), F32)
    tile = lax.fori_loop(shard // 8, layers * shard // 8, squares, tile)
    reduce_z(0, 3, 12)
    reduce_z(0, 0, 3)
    tile = lax.fori_loop(0, shard // 8, squares, tile)
    tile = all_sum_wide(p, tile, tslots, ts_send, ts_recv)
    value = norm_grad[...]
    value = value * value
    for c in range(width // 128):
        piece = value[:, c * 128 : (c + 1) * 128]
        for r in range(4 * layers // 8):
            tile = tile + piece[r * 8 : r * 8 + 8]
    total = jnp.sum(jnp.sum(tile, axis=0, keepdims=True), axis=1, keepdims=True)
    total_out[...] = jnp.broadcast_to(jnp.sqrt(total), (8, 128))


def run_backward(dims, lengths, g_in, norms, g_all, kept):
    (layers, slots, width, block, local_width, local_ff, groups, zn, xn, yn) = dims
    packed = UNITS * local_width
    shard = width // groups
    slot_count, sem_count = sum_slots(zn, xn, yn)
    vmem = pl.BlockSpec(memory_space=pltpu.VMEM)
    smem = pl.BlockSpec(memory_space=pltpu.SMEM)
    hbm = pl.BlockSpec(memory_space=pl.ANY)
    dma = pltpu.SemaphoreType.DMA
    return pl.pallas_call(
        functools.partial(backward_kernel, dims),
        out_shape=[
            jax.ShapeDtypeStruct((block, width), F32),
            jax.ShapeDtypeStruct((4 * layers, width), F32),
            jax.ShapeDtypeStruct((8, 128), F32),
            jax.ShapeDtypeStruct((layers, shard, packed), F32),
        ],
        in_specs=[smem, vmem, vmem] + [hbm] * (1 + len(kept)),
        out_specs=[vmem] * 4,
        scratch_shapes=[pltpu.VMEM(k.shape[1:], k.dtype) for k in kept]
        + [
            pltpu.VMEM((slots, width), BF16),
            pltpu.VMEM((slots, width), BF16),
            pltpu.VMEM((slots, local_width), BF16),
            pltpu.VMEM((slots, 3 * local_width), BF16),
            pltpu.VMEM((slots, HD), F32),
            pltpu.VMEM((slots, HD), F32),
            pltpu.VMEM((slots, 128), F32),
            pltpu.VMEM((HD, slots), BF16),
            pltpu.VMEM((block, width), F32),
            pltpu.VMEM((block, width), F32),
            pltpu.VMEM((4 * layers, width), F32),
            pltpu.VMEM((zn, xn, shard, packed), BF16),
            pltpu.VMEM((layers, xn - 1, zn, shard, packed), BF16),
            pltpu.VMEM((layers, zn - 1, shard, packed), BF16),
            pltpu.VMEM((yn, block, width), BF16),
            pltpu.VMEM((yn, block, width), BF16),
            pltpu.VMEM((yn - 1, block, width), BF16),
            pltpu.VMEM((yn - 1, block, width), BF16),
            pltpu.VMEM((block, width), F32),
            pltpu.VMEM((slot_count, 4 * layers, width), F32),
            pltpu.VMEM((CORES * yn + groups, 8, 128), F32),
            dma((layers, UNITS, zn - 1)),
            dma((layers, UNITS, zn - 1)),
            dma((layers, UNITS, xn - 1)),
            dma((layers, UNITS, xn - 1)),
            dma((2 * layers, 2 * yn - 1)),
            dma((2 * layers, 2 * yn - 1)),
            dma((2 * layers, 2 * yn - 1)),
            dma((2 * layers, 2 * yn - 1)),
            dma((sem_count,)),
            dma((sem_count,)),
            dma((CORES * yn + groups - 2,)),
            dma((CORES * yn + groups - 2,)),
            dma((len(kept) + 4,)),
        ],
        compiler_params=pltpu.CompilerParams(
            collective_id=1, has_side_effects=True, vmem_limit_bytes=62 * 2**20
        ),
        name="backward_layers",
    )(lengths, g_in, norms, g_all, *kept)


def adam_kernel(dims, *refs):
    (layers, slots, width, block, local_width, local_ff, groups, zn, xn, yn) = dims
    refs = list(refs)

    def take(count):
        out = refs[:count]
        del refs[:count]
        return out

    total, norm_grad, hidden_in, input_in = take(4)
    grads, masters, firsts, seconds = take(4), take(5), take(5), take(5)
    hidden_out, input_out = take(2)
    grad_out, moment_out, variance_out, new_out, copy_out = (take(5) for unused in range(5))
    factor = CLIP_NORM / jnp.maximum(total[0:1, 0:1], CLIP_NORM)
    fix_one = 1.0 / (1.0 - BETA_ONE**STEP)
    fix_two = 1.0 / (1.0 - BETA_TWO**STEP)

    def update(k, at, grad, decay, rate):
        clipped = grad * factor
        momentum = BETA_ONE * firsts[k][at] + (1.0 - BETA_ONE) * clipped
        variance = BETA_TWO * seconds[k][at] + (1.0 - BETA_TWO) * clipped * clipped
        master = masters[k][at]
        size = momentum * fix_one / (jnp.sqrt(variance * fix_two) + ADAM_EPS)
        if decay:
            size = size + decay * master
        fresh = master - rate * size
        grad_out[k][at] = grad
        moment_out[k][at] = momentum
        variance_out[k][at] = variance
        new_out[k][at] = fresh
        copy_out[k][at] = fresh.astype(BF16)

    def matrix(k, at, grad):
        update(k, at, grad, WEIGHT_DECAY, LEARN_RATE)

    hidden_out[...] = hidden_in[...]
    input_out[...] = input_in[...]
    every = slice(None)
    for part in range(3):
        grad = grads[0][0, :, part * local_width : (part + 1) * local_width]
        matrix(0, (0, part, every, every), grad)
    matrix(1, (0, every, every), grads[1][0].T)

    def up_rows(i, unused):
        at = rows_of(i, 16)
        matrix(2, (0, at, every), grads[2][0, at, :])
        return unused

    lax.fori_loop(0, grads[2].shape[1] // 16, up_rows, 0)
    for c in range(grads[3].shape[2] // 128):
        at = pl.ds(c * 128, 128)
        matrix(3, (0, at, every), grads[3][0, :, at].T)

    @pl.when((pl.program_id(0) == 0) & (pl.program_id(1) == 0))
    def _():
        seq_count = CORES * yn
        piece = width // (groups * seq_count)
        at = (lax.axis_index("dp") * seq_count + lax.axis_index("seq")) * piece
        tile = norm_grad[:, rows_of(at // 128, 128)]
        tile = pltpu.roll(tile, lax.rem(128 - lax.rem(at, 128), 128), 1)[:, :piece]
        for l in range(layers):
            update(4, (l,), tile[4 * l : 4 * l + 4], 0.0, NORM_RATE)


def run_adam(dims, total, norm_grad, hidden, input_grad, grad, masters, firsts, seconds):
    (layers, slots, width, block, local_width, local_ff, groups, zn, xn, yn) = dims
    parts = local_width // 128
    shard = width // groups
    piece = width // (groups * CORES * yn)
    rows = block // (layers * parts)

    def same(shape):
        return pl.BlockSpec(shape, lambda l, b: (0,) * len(shape))

    flat = pl.BlockSpec((rows, width), lambda l, b: (l * parts + b, 0))
    grad_specs = [
        pl.BlockSpec((1, shard // parts, 3 * local_width), lambda l, b: (l, b, 0)),
        pl.BlockSpec((1, shard, 128), lambda l, b: (l, 0, 3 * parts + b)),
        pl.BlockSpec((1, shard // parts, local_ff), lambda l, b: (l, b, 1)),
        pl.BlockSpec((1, shard, local_ff // parts), lambda l, b: (l, 0, 2 * parts + b)),
    ]
    own_specs = [
        pl.BlockSpec((1, 3, shard // parts, local_width), lambda l, b: (l, 0, b, 0)),
        pl.BlockSpec((1, 128, shard), lambda l, b: (l, b, 0)),
        pl.BlockSpec((1, shard // parts, local_ff), lambda l, b: (l, b, 0)),
        pl.BlockSpec((1, local_ff // parts, shard), lambda l, b: (l, b, 0)),
        same((layers, 4, piece)),
    ]

    def shapes(dtype):
        return [jax.ShapeDtypeStruct(m.shape, dtype) for m in masters]

    flat_shape = jax.ShapeDtypeStruct((block, width), F32)
    return pl.pallas_call(
        functools.partial(adam_kernel, dims),
        grid=(layers, parts),
        out_shape=[flat_shape, flat_shape] + shapes(F32) * 4 + shapes(BF16),
        in_specs=[same((8, 128)), same((4 * layers, width)), flat, flat]
        + grad_specs
        + own_specs * 3,
        out_specs=[flat, flat] + own_specs * 5,
        compiler_params=pltpu.CompilerParams(vmem_limit_bytes=60 * 2**20),
        name="adam_update",
    )(total, norm_grad, hidden, input_grad, *([grad] * 4), *masters, *firsts, *seconds)


def body(
    block_input,
    output_grad,
    row_lengths,
    qkv_weight,
    proj_weight,
    up_weight,
    down_weight,
    norm_params,
    qkv_first,
    proj_first,
    up_first,
    down_first,
    norm_first,
    qkv_second,
    proj_second,
    up_second,
    down_second,
    norm_second,
):
    row_count, local_slots, width = block_input.shape
    seq_count = lax.axis_size("seq")
    groups = lax.axis_size("dp")
    layer_count = qkv_weight.shape[0]
    local_width = qkv_weight.shape[3]
    dims = (
        layer_count, local_slots * seq_count, width, local_slots, local_width,
        up_weight.shape[2], groups, ZSIZE, groups // ZSIZE, seq_count // CORES,
    )

    def turned(qkv):
        return jnp.transpose(qkv, (0, 2, 1, 3))

    masters = (turned(qkv_weight), proj_weight, up_weight, down_weight, norm_params)
    firsts = (turned(qkv_first), proj_first, up_first, down_first, norm_first)
    seconds = (turned(qkv_second), proj_second, up_second, down_second, norm_second)
    piece = norm_params.shape[2]
    norm_in = norm_params.astype(BF16).astype(F32).reshape(4 * layer_count, piece)
    norm_in = jnp.pad(norm_in, ((0, 0), (0, 128 - piece)))
    flat = (local_slots, width)
    g_in = output_grad.reshape(flat)
    kept = run_forward(dims, row_lengths, block_input.reshape(flat), g_in, norm_in, masters[:4])
    back = run_backward(dims, row_lengths, g_in, kept[1], kept[2], kept[3:])
    outs = run_adam(dims, back[2], back[1], kept[0], back[0], back[3], masters, firsts, seconds)
    whole = (row_count,) + flat
    final = [outs[0].reshape(whole), outs[1].reshape(whole), back[2][0, 0]]
    for group in range(5):
        mine = outs[2 + 5 * group : 7 + 5 * group]
        final += [turned(mine[0])] + list(mine[1:])
    return tuple(final)


def solution(mesh):
    return jax.shard_map(
        body,
        mesh=mesh,
        in_specs=(
            P("dp", "seq", None),
            P("dp", "seq", None),
            P("dp"),
            P(None, "dp", None, "seq"),
            P(None, "seq", "dp"),
            P(None, "dp", "seq"),
            P(None, "seq", "dp"),
            P(None, None, ("dp", "seq")),
            P(None, "dp", None, "seq"),
            P(None, "seq", "dp"),
            P(None, "dp", "seq"),
            P(None, "seq", "dp"),
            P(None, None, ("dp", "seq")),
            P(None, "dp", None, "seq"),
            P(None, "seq", "dp"),
            P(None, "dp", "seq"),
            P(None, "seq", "dp"),
            P(None, None, ("dp", "seq")),
        ),
        out_specs=(
            P("dp", "seq", None),
            P("dp", "seq", None),
            P(),
            P(None, "dp", None, "seq"),
            P(None, "seq", "dp"),
            P(None, "dp", "seq"),
            P(None, "seq", "dp"),
            P(None, None, ("dp", "seq")),
            P(None, "dp", None, "seq"),
            P(None, "seq", "dp"),
            P(None, "dp", "seq"),
            P(None, "seq", "dp"),
            P(None, None, ("dp", "seq")),
            P(None, "dp", None, "seq"),
            P(None, "seq", "dp"),
            P(None, "dp", "seq"),
            P(None, "seq", "dp"),
            P(None, None, ("dp", "seq")),
            P(None, "dp", None, "seq"),
            P(None, "seq", "dp"),
            P(None, "dp", "seq"),
            P(None, "seq", "dp"),
            P(None, None, ("dp", "seq")),
            P(None, "dp", None, "seq"),
            P(None, "seq", "dp"),
            P(None, "dp", "seq"),
            P(None, "seq", "dp"),
            P(None, None, ("dp", "seq")),
        ),
        check_vma=False,
    )
```
